128 devices in a mesh: grp: 4 (over y_lo, core), dev: 32 (over z, x, y_hi).
Axes of the slice: x: 4, y: 4 (y_hi: 2, y_lo: 2; y = y_hi * 2 + y_lo), z: 4, core: 2. Of those that a mesh axis runs over, the one named last changes fastest.
Arguments:
- voltage_real: bfloat16 [2048, 110592], P(('grp', 'dev')), may hold values from -6 to 6
- voltage_imaginary: bfloat16 [2048, 110592], P(('grp', 'dev')), may hold values from -6 to 6
- filter_taps: float32 [16, 4096], replicated, may hold values from -1.5 to 1.5
- weights_re: float32 [32, 2048, 512], P('dev'), may hold values from -0.0625 to 0.0625
- weights_im: float32 [32, 2048, 512], P('dev'), may hold values from -0.0625 to 0.0625
- owners: int32 [2], replicated, may hold values from 0 to 31
- antenna_map: int32 [2048], replicated, may hold values from 0 to 2047, each once
Outputs:
- beam_power: float32 [2, 4096, 512], P(None, ('grp', 'dev'))
The draws below stay inside these ranges and needn't reach their ends.
Inputs may be any that keep to these rules, and one draw needn't show every extreme that they name: `owners`: the index along dev of the device whose calibration serves each step. A permutation: voltage slot j carries antenna antenna_map[j].
All inputs are finite; a program needn't handle non-finite values.
Results may differ from the reference program's by a relative error of at most 0.0022.
Values may be sent and summed in bfloat16 or wider, within the bound.
No kernel may reach another device: no remote copies, remote signals or barrier semaphores. Data moves between devices by JAX's collectives and lax.ppermute only.
A program may use at most 192 MiB of HBM per device.

```python
import jax
import jax.numpy as jnp
from jax import lax

A = 2048
FREQ_CHANNELS = 4096
B = 512
TAPS = 16
SPECTRA_PER_STEP = 6
STEPS = 2
SAMPLES = 110592
N_DEV = 32


def steps_of(key, shape, split, least, top_value):
    loudness = 1.0
    for axis_at, shards_of in split:
        steps = jax.random.uniform(jax.random.fold_in(jax.random.fold_in(key, 6), axis_at), (shards_of,), jnp.float32, least / len(split), top_value / len(split))
        loudness = loudness * jnp.repeat(jnp.exp(steps), shape[axis_at] // shards_of).reshape((-1,) + (1,) * (len(shape) - 1 - axis_at))
    return loudness


def bell_draw(own_key, extent, scale, limit, cuts=(), kind=jnp.bfloat16):
    factor_of = steps_of(own_key, extent, cuts, -0.22, 0.18) if cuts else 1.0
    result = jax.random.normal(own_key, extent, jnp.float32) * scale * factor_of
    return jnp.minimum(jnp.maximum(result, -limit), limit).astype(kind)


def setup_inputs(seed: int = 0) -> dict:
    seeds = jax.random.split(jax.random.key(seed), 8)
    return {
        "voltage_real": bell_draw(seeds[0], (A, SAMPLES), 1.0, 6.0, ((0, 128),)),
        "voltage_imaginary": bell_draw(seeds[1], (A, SAMPLES), 1.0, 6.0, ((0, 128),)),
        "filter_taps": bell_draw(seeds[2], (TAPS, FREQ_CHANNELS), 0.25, 1.5, (), jnp.float32),
        "weights_re": bell_draw(seeds[3], (N_DEV, A, B), (4 * A) ** -0.5, 0.0625, ((0, 32),), jnp.float32),
        "weights_im": bell_draw(seeds[4], (N_DEV, A, B), (4 * A) ** -0.5, 0.0625, ((0, 32),), jnp.float32),
        "owners": jax.random.randint(seeds[5], (STEPS,), 0, N_DEV).astype(jnp.int32),
        "antenna_map": jax.random.permutation(seeds[6], A).astype(jnp.int32),
    }


def spectra_block(pieces, filter_taps, offset):
    blocks_re, blocks_im = pieces
    frames_re = jnp.zeros((blocks_re.shape[0], SPECTRA_PER_STEP, FREQ_CHANNELS), jnp.float32)
    frames_im = jnp.zeros((blocks_re.shape[0], SPECTRA_PER_STEP, FREQ_CHANNELS), jnp.float32)
    for tap_index in range(TAPS):
        lower = offset + tap_index
        frames_re = frames_re + blocks_re[:, lower:lower + SPECTRA_PER_STEP].astype(jnp.float32) * filter_taps[tap_index]
        frames_im = frames_im + blocks_im[:, lower:lower + SPECTRA_PER_STEP].astype(jnp.float32) * filter_taps[tap_index]
    spectrum_rows = jnp.fft.fft(frames_re + 1j * frames_im, axis=-1) * (FREQ_CHANNELS ** -0.5)
    return jnp.real(spectrum_rows).astype(jnp.bfloat16), jnp.imag(spectrum_rows).astype(jnp.bfloat16)


def reference(voltage_real, voltage_imaginary, filter_taps, weights_re, weights_im, owners, antenna_map):
    width = min(A, 256)
    count = A // width
    blocks_re = voltage_real.reshape(count, width, -1, FREQ_CHANNELS)
    blocks_im = voltage_imaginary.reshape(count, width, -1, FREQ_CHANNELS)
    col_width = min(FREQ_CHANNELS, 256)
    results = []
    for window_step in range(STEPS):
        offset = window_step * SPECTRA_PER_STEP

        def make_block(pieces):
            return spectra_block(pieces, filter_taps, offset)

        spectrum_real, spectrum_imaginary = lax.map(make_block, (blocks_re, blocks_im))
        stacked = jnp.concatenate([spectrum_real.reshape(A, SPECTRA_PER_STEP, FREQ_CHANNELS), spectrum_imaginary.reshape(A, SPECTRA_PER_STEP, FREQ_CHANNELS)], 0)
        leader = owners[window_step]
        cal_re = jnp.take(weights_re[leader].astype(jnp.bfloat16), antenna_map, axis=0)
        cal_im = jnp.take(weights_im[leader].astype(jnp.bfloat16), antenna_map, axis=0)
        mixing = jnp.concatenate([jnp.concatenate([cal_re, cal_im], 1), jnp.concatenate([-cal_im, cal_re], 1)], 0).astype(jnp.float32)

        def detect_block(block_index):
            start_channel = (block_index * col_width).astype(jnp.int32)
            column_part = lax.dynamic_slice_in_dim(stacked, start_channel, col_width, 2).astype(jnp.float32)
            beam_terms = jnp.einsum('atf,ab->tfb', column_part, mixing, precision=lax.Precision.HIGHEST)
            return jnp.mean(beam_terms[..., :B] ** 2 + beam_terms[..., B:] ** 2, axis=0)

        beam_power = lax.map(detect_block, jnp.arange(FREQ_CHANNELS // col_width, dtype=jnp.int32))
        results.append(beam_power.reshape(FREQ_CHANNELS, B))
    return jnp.stack(results)
```

```python
import math

import jax
import jax.numpy as jnp
import numpy as np
from jax import lax
from jax.experimental import pallas as pl
from jax.experimental.pallas import tpu as pltpu
from jax.sharding import PartitionSpec as P

CHANNELS = 4096
TAPS = 16
SPECTRA = 6
STEPS = 2
FRAMES = STEPS * SPECTRA
BLOCKS = FRAMES + TAPS - 1
OUTER = 32
INNER = 128
SLOTS = 16
DEVICES = 128
ALL = ("grp", "dev")
MIB = 1 << 20


def twist_tables():
    products = np.outer(np.arange(OUTER), np.arange(INNER)) % CHANNELS
    angles = products * (2.0 * math.pi / CHANNELS)
    return np.cos(angles).astype(np.float32), np.sin(angles).astype(np.float32)


def inner_matrix():
    products = np.outer(np.arange(INNER), np.arange(INNER)) % INNER
    angles = products * (2.0 * math.pi / INNER)
    norm = CHANNELS ** (-0.5)
    c, s = np.cos(angles) * norm, np.sin(angles) * norm
    return np.block([[c, s], [-s, c]]).astype(np.float32)


def small_fft(points):
    count = len(points)
    if count == 1:
        return points
    even = small_fft(points[0::2])
    odd = small_fft(points[1::2])
    half = count // 2
    result = [None] * count
    for k in range(half):
        er, ei = even[k]
        xr, xi = odd[k]
        if k == 0:
            tr, ti = xr, xi
        elif 4 * k == count:
            tr, ti = xi, -xr
        elif 8 * k == count:
            r = math.sqrt(0.5)
            tr, ti = (xr + xi) * r, (xi - xr) * r
        elif 8 * k == 3 * count:
            r = math.sqrt(0.5)
            tr, ti = (xi - xr) * r, (xr + xi) * (-r)
        else:
            c = math.cos(2.0 * math.pi * k / count)
            s = math.sin(2.0 * math.pi * k / count)
            tr, ti = xr * c + xi * s, xi * c - xr * s
        result[k] = (er + tr, ei + ti)
        result[k + half] = (er - tr, ei - ti)
    return result


def spectra_kernel(vre, vim, taps, cos_t, sin_t, mat, out, frames, turned, packed):
    def fir(n1, _):
        rows = [taps[k : k + 1, pl.ds(pl.multiple_of(n1 * INNER, INNER), INNER)] for k in range(TAPS)]
        for c, volts in ((0, vre), (1, vim)):
            window = [
                volts[:, pl.ds(pl.multiple_of(b * CHANNELS + n1 * INNER, INNER), INNER)].astype(jnp.float32)
                for b in range(BLOCKS)
            ]
            for u in range(FRAMES):
                total = window[u] * rows[0]
                for k in range(1, TAPS):
                    total = total + window[u + k] * rows[k]
                frames[c, u, n1] = total
        return 0

    lax.fori_loop(0, OUTER, fir, 0)

    def outer(i, _):
        u = i // 2
        low = pl.multiple_of((i % 2) * 8, 8)
        s = u // SPECTRA
        t = u % SPECTRA
        place = jnp.where(t < 4, s * 128 + t * 32, 256 + s * 64 + (t - 4) * 32)
        points = [
            (frames[0, u, n1, pl.ds(low, 8), :], frames[1, u, n1, pl.ds(low, 8), :]) for n1 in range(OUTER)
        ]
        points = small_fft(points)
        for f1 in range(OUTER):
            re, im = points[f1]
            if f1:
                c, d = cos_t[f1 : f1 + 1, :], sin_t[f1 : f1 + 1, :]
                re, im = re * c + im * d, im * c - re * d
            at = low * 384 + place + f1
            turned[0, pl.ds(at, 8, stride=384), :] = re
            turned[1, pl.ds(at, 8, stride=384), :] = im
        return 0

    lax.fori_loop(0, 2 * FRAMES, outer, 0)

    matrix = mat[...]
    lane = lax.broadcasted_iota(jnp.int32, (32, INNER), 1)

    def inner(a, _):
        base = pl.multiple_of(a * 384, 128)
        rows = jnp.concatenate(
            [turned[0, pl.ds(base, 384), :], turned[1, pl.ds(base, 384), :]], axis=1
        ).astype(jnp.bfloat16)
        spec = lax.dot_general(
            matrix, rows, (((1,), (1,)), ((), ())), preferred_element_type=jnp.float32
        )
        for y in range(2):
            for c in range(2):
                mixed = []
                for pair in range(2):
                    f2 = c * 128 + (y * 2 + pair) * 32
                    for s in range(2):
                        to = (y * 2 + s) * 32 * SLOTS + a
                        packed[c * 3 + pair, pl.ds(to, 32, stride=SLOTS), :] = spec[
                            f2 : f2 + 32, s * 128 : s * 128 + 128
                        ]
                    mixed.append(spec[f2 : f2 + 32, 256:384])
                first = jnp.where(lane < 64, mixed[0], pltpu.roll(mixed[1], 64, 1))
                second = jnp.where(lane < 64, pltpu.roll(mixed[0], 64, 1), mixed[1])
                packed[c * 3 + 2, pl.ds(y * 64 * SLOTS + a, 32, stride=SLOTS), :] = first
                packed[c * 3 + 2, pl.ds((y * 2 + 1) * 32 * SLOTS + a, 32, stride=SLOTS), :] = second
        return 0

    lax.fori_loop(0, SLOTS, inner, 0)

    def emit(p, _):
        for tile in range(6):
            out[p, :, tile * INNER : (tile + 1) * INNER] = packed[
                tile, pl.ds(pl.multiple_of(p * SLOTS, SLOTS), SLOTS), :
            ].astype(jnp.bfloat16)
        return 0

    lax.fori_loop(0, DEVICES, emit, 0, unroll=4)


def spectra_of(vre, vim, taps, interpret=False):
    cos_t, sin_t = twist_tables()
    mat = inner_matrix().astype(jnp.bfloat16)
    return pl.pallas_call(
        spectra_kernel,
        out_shape=jax.ShapeDtypeStruct((DEVICES, SLOTS, 6 * INNER), jnp.bfloat16),
        in_specs=[pl.BlockSpec(memory_space=pltpu.VMEM)] * 6,
        out_specs=pl.BlockSpec(memory_space=pltpu.VMEM),
        scratch_shapes=[
            pltpu.VMEM((2, FRAMES, OUTER, SLOTS, INNER), jnp.float32),
            pltpu.VMEM((2, SLOTS * 384, INNER), jnp.float32),
            pltpu.VMEM((6, DEVICES * SLOTS, INNER), jnp.float32),
        ],
        compiler_params=pltpu.CompilerParams(vmem_limit_bytes=52 * MIB),
        cost_estimate=pl.CostEstimate(flops=2 * 10**9, bytes_accessed=60 * 10**6, transcendentals=0),
        interpret=interpret,
        name="spectra",
    )(vre, vim, taps, jnp.asarray(cos_t), jnp.asarray(sin_t), jnp.asarray(mat))


def quarter_kernel(where, wre, wim, slots, out, total):
    step = pl.program_id(0)
    rows = jnp.where(where[0] == 0, wre[...], wim[...]).astype(jnp.bfloat16)
    antenna = lax.broadcasted_iota(jnp.int32, (rows.shape[0], slots.shape[2]), 0) + step * rows.shape[0]
    chosen = jnp.where(antenna == slots[0], 1.0, 0.0).astype(jnp.bfloat16)
    part = lax.dot_general(rows, chosen, (((0,), (0,)), ((), ())), preferred_element_type=jnp.float32)

    @pl.when(step == 0)
    def _():
        total[...] = part

    @pl.when(step > 0)
    def _():
        total[...] = total[...] + part

    @pl.when(step == pl.num_programs(0) - 1)
    def _():
        out[...] = total[...].astype(jnp.bfloat16)


def quarter_of(y_lo, core, wre, wim, antenna_map, interpret=False):
    antennas, beams = wre.shape
    depth = 256
    half = antennas // 2
    grid_spec = pltpu.PrefetchScalarGridSpec(
        num_scalar_prefetch=1,
        grid=(antennas // depth,),
        in_specs=[
            pl.BlockSpec((depth, beams), lambda i, w: (jnp.where(w[0] == 0, i, 0), 0)),
            pl.BlockSpec((depth, beams), lambda i, w: (jnp.where(w[0] == 0, 0, i), 0)),
            pl.BlockSpec((1, 1, half), lambda i, w: (w[1], 0, 0)),
        ],
        out_specs=pl.BlockSpec((beams, half), lambda i, w: (0, 0)),
        scratch_shapes=[pltpu.VMEM((beams, half), jnp.float32)],
    )
    return pl.pallas_call(
        quarter_kernel,
        grid_spec=grid_spec,
        out_shape=jax.ShapeDtypeStruct((beams, half), jnp.bfloat16),
        compiler_params=pltpu.CompilerParams(vmem_limit_bytes=32 * MIB),
        cost_estimate=pl.CostEstimate(flops=2 * 10**9, bytes_accessed=6 * 10**6, transcendentals=0),
        interpret=interpret,
        name="quarter",
    )(jnp.stack([y_lo, core]).astype(jnp.int32), wre, wim, antenna_map.reshape(2, 1, half))


def choose_matrix():
    chosen = np.zeros((2, 32, 3, 4, 32), np.float32)
    for pair in range(2):
        for f1 in range(32):
            chosen[pair, f1, pair, :, f1] = 1.0
            chosen[pair, f1, 2, 2 * pair : 2 * pair + 2, f1] = 1.0
    return chosen.reshape(64, 384)


def beams_kernel(places, w0, w1, w2, w3, spectra, choose, out, sums):
    spec = spectra[...]
    for k3, part in enumerate((w0, w1, w2, w3)):
        result = jnp.dot(part[...], spec, preferred_element_type=jnp.float32)
        for k in range(16):
            at = pl.multiple_of(places[k3 * 16 + k], 16)
            sums[pl.ds(at, 16), :] = result[k * 16 : (k + 1) * 16, :]
    beams = sums.shape[0] // 2
    re = sums[:beams, :384] - sums[beams:, 384:]
    im = sums[beams:, :384] + sums[:beams, 384:]
    power = re * re + im * im
    total = lax.dot_general(
        choose[...],
        power,
        (((1,), (1,)), ((), ())),
        preferred_element_type=jnp.float32,
        precision=lax.Precision.HIGHEST,
    )
    out[...] = total * (1.0 / SPECTRA)


def beams_of(places, parts, spectra, interpret=False):
    rows = sum(p.shape[0] for p in parts)
    return pl.pallas_call(
        beams_kernel,
        out_shape=jax.ShapeDtypeStruct((64, rows // 2), jnp.float32),
        in_specs=[pl.BlockSpec(memory_space=pltpu.SMEM)] + [pl.BlockSpec(memory_space=pltpu.VMEM)] * 6,
        out_specs=pl.BlockSpec(memory_space=pltpu.VMEM),
        scratch_shapes=[pltpu.VMEM((rows, 768), jnp.float32)],
        compiler_params=pltpu.CompilerParams(vmem_limit_bytes=40 * MIB),
        cost_estimate=pl.CostEstimate(flops=33 * 10**8, bytes_accessed=8 * 10**6, transcendentals=0),
        interpret=interpret,
        name="beams",
    )(places, *parts, spectra, jnp.asarray(choose_matrix()))


def index_of(z, x, y, core):
    return ((y % 2) * 2 + core) * 32 + (z % 4) * 8 + (x % 4) * 2 + (y % 4) // 2


EVERY = [(z, x, y, c) for z in range(4) for x in range(4) for y in range(4) for c in range(2)]
ORDER = (("y", "x", "z"), ("z", "y", "x"))
SHIFTS = (0, -1, 1, 2)


def permutation(stage, shift):
    pairs = []
    for z, x, y, core in EVERY:
        axis = ORDER[core][stage]
        source = {"z": z, "x": x, "y": y}
        source[axis] += shift
        pairs.append((index_of(source["z"], source["x"], source["y"], core), index_of(z, x, y, core)))
    return pairs


def gather_stage(block, stage):
    return [block] + [lax.ppermute(block, ALL, permutation(stage, shift)) for shift in SHIFTS[1:]]


def block_places(grp, dev):
    core = grp % 2
    z, x, y = dev // 8, dev // 2 % 4, dev % 2 * 2 + grp // 2
    k = np.arange(64)
    shift = np.array(SHIFTS)
    first, second, third = shift[k % 4], shift[k // 4 % 4], shift[k // 16]
    by_core = []
    for order in ORDER:
        moved = dict(zip(order, (first, second, third)))
        by_core.append([moved[axis] for axis in "zxy"])
    is_first = core == 0
    mz, mx, my = [jnp.where(is_first, jnp.asarray(a), jnp.asarray(b)) for a, b in zip(*by_core)]
    fz, fx, fy = (z + mz + 4) % 4, (x + mx + 4) % 4, (y + my + 4) % 4
    return (((fy % 2) * 32 + fz * 8 + fx * 2 + fy // 2) * 16).astype(jnp.int32)


SWAP = [(0, 1), (1, 0), (2, 3), (3, 2)]


def on_device(voltage_real, voltage_imaginary, filter_taps, weights_re, weights_im, owners, antenna_map):
    grp, dev = lax.axis_index("grp"), lax.axis_index("dev")
    y_lo, core = grp // 2, grp % 2

    quarter = quarter_of(y_lo, core, weights_re[0], weights_im[0], antenna_map)
    offers = lax.all_to_all(quarter.reshape(32, 16, -1), "dev", split_axis=0, concat_axis=0, tiled=True)

    spectra = spectra_of(voltage_real, voltage_imaginary, filter_taps)
    spectra = lax.all_to_all(spectra, ALL, split_axis=0, concat_axis=0, tiled=True)

    mine = lax.dynamic_index_in_dim(offers, owners[core], 0, keepdims=False)
    other = lax.dynamic_index_in_dim(offers, owners[1 - core], 0, keepdims=False)
    other = lax.ppermute(other, "grp", SWAP)
    block = jnp.where(
        core == 0,
        jnp.concatenate([mine, other], axis=1),
        jnp.concatenate([other, mine], axis=1),
    )
    block = jnp.concatenate(gather_stage(block, 0), axis=0)
    block = jnp.concatenate(gather_stage(block, 1), axis=0)
    parts = gather_stage(block, 2)

    power = beams_of(block_places(grp, dev), parts, spectra.reshape(DEVICES * SLOTS, -1))
    power = power.reshape(2, 32, -1)
    own = lax.dynamic_index_in_dim(power, core, 0, keepdims=False)
    given = lax.dynamic_index_in_dim(power, 1 - core, 0, keepdims=False)
    taken = lax.ppermute(given, "grp", SWAP)
    return jnp.where(core == 0, jnp.stack([own, taken]), jnp.stack([taken, own]))


def solution(mesh):
    return jax.shard_map(
        on_device,
        mesh=mesh,
        in_specs=(
            P(("grp", "dev"), None),
            P(("grp", "dev"), None),
            P(),
            P("dev", None, None),
            P("dev", None, None),
            P(),
            P(),
        ),
        out_specs=P(None, ("grp", "dev"), None),
        check_vma=False,
    )
```

```python
import functools
import math

import jax
import jax.numpy as jnp
import numpy as np
from jax import lax
from jax.experimental import pallas as pl
from jax.experimental.pallas import tpu as pltpu
from jax.sharding import PartitionSpec as P

CHANNELS = 4096
TAPS = 16
SPECTRA = 6
STEPS = 2
FRAMES = STEPS * SPECTRA
BLOCKS = FRAMES + TAPS - 1
OUTER = 32
INNER = 128
SLOTS = 16
DEVICES = 128
ROW_STRIDE = 24
PARTS = ((0, 1, 2, 3, 6, 7, 8, 9), (4, 5, 10, 11))
ALL = ("grp", "dev")
MIB = 1 << 20


def twist_tables():
    products = np.outer(np.arange(OUTER), np.arange(INNER)) % CHANNELS
    angles = products * (2.0 * math.pi / CHANNELS)
    return np.cos(angles).astype(np.float32), np.sin(angles).astype(np.float32)


def inner_matrix():
    products = np.outer(np.arange(INNER), np.arange(INNER)) % INNER
    angles = products * (2.0 * math.pi / INNER)
    norm = CHANNELS ** (-0.5)
    c, s = np.cos(angles) * norm, np.sin(angles) * norm
    return np.block([[c, s], [-s, c]]).astype(np.float32)


def small_fft(points):
    count = len(points)
    if count == 1:
        return points
    even = small_fft(points[0::2])
    odd = small_fft(points[1::2])
    half = count // 2
    result = [None] * count
    for k in range(half):
        er, ei = even[k]
        xr, xi = odd[k]
        if k == 0:
            tr, ti = xr, xi
        elif 4 * k == count:
            tr, ti = xi, -xr
        elif 8 * k == count:
            r = math.sqrt(0.5)
            tr, ti = (xr + xi) * r, (xi - xr) * r
        elif 8 * k == 3 * count:
            r = math.sqrt(0.5)
            tr, ti = (xi - xr) * r, (xr + xi) * (-r)
        else:
            c = math.cos(2.0 * math.pi * k / count)
            s = math.sin(2.0 * math.pi * k / count)
            tr, ti = xr * c + xi * s, xi * c - xr * s
        result[k] = (er + tr, ei + ti)
        result[k + half] = (er - tr, ei - ti)
    return result


def spectra_kernel(part, vre, vim, taps, cos_t, sin_t, mat, out, frames, turned, packed):
    chosen = PARTS[part]
    first, last = min(chosen), max(chosen) + TAPS
    rows_per_slot = 32 * len(chosen)
    slot_stride = rows_per_slot + 8

    def fir(n1, _):
        rows = [taps[k : k + 1, pl.ds(pl.multiple_of(n1 * INNER, INNER), INNER)] for k in range(TAPS)]
        for c, volts in ((0, vre), (1, vim)):
            window = {
                b: volts[:, pl.ds(pl.multiple_of(b * CHANNELS + n1 * INNER, INNER), INNER)].astype(jnp.float32)
                for b in range(first, last)
            }
            for i, u in enumerate(chosen):
                total = window[u] * rows[0]
                for k in range(1, TAPS):
                    total = total + window[u + k] * rows[k]
                frames[c, i, n1] = total
        return 0

    lax.fori_loop(0, OUTER, fir, 0)

    def outer(i, _):
        u = i // 2
        low = pl.multiple_of((i % 2) * 8, 8)
        points = [
            (frames[0, u, n1, pl.ds(low, 8), :], frames[1, u, n1, pl.ds(low, 8), :]) for n1 in range(OUTER)
        ]
        points = small_fft(points)
        for f1 in range(OUTER):
            re, im = points[f1]
            if f1:
                c, d = cos_t[f1 : f1 + 1, :], sin_t[f1 : f1 + 1, :]
                re, im = re * c + im * d, im * c - re * d
            at = low * slot_stride + u * 32 + f1
            turned[0, pl.ds(at, 8, stride=slot_stride), :] = re
            turned[1, pl.ds(at, 8, stride=slot_stride), :] = im
        return 0

    lax.fori_loop(0, 2 * len(chosen), outer, 0)

    matrix = mat[...]
    lane = lax.broadcasted_iota(jnp.int32, (32, INNER), 1)

    def inner(a, _):
        base = pl.multiple_of(a * slot_stride, 8)
        rows = jnp.concatenate(
            [turned[0, pl.ds(base, rows_per_slot), :], turned[1, pl.ds(base, rows_per_slot), :]], axis=1
        ).astype(jnp.bfloat16)
        spec = lax.dot_general(
            matrix, rows, (((1,), (1,)), ((), ())), preferred_element_type=jnp.float32
        )
        for y in range(2):
            for c in range(2):
                to = [pl.ds((y * 2 + s) * 32 * ROW_STRIDE + a, 32, stride=ROW_STRIDE) for s in range(2)]
                at = [c * 128 + (y * 2 + pair) * 32 for pair in range(2)]
                if part == 0:
                    for pair in range(2):
                        for s in range(2):
                            packed[c * 2 + pair, to[s], :] = spec[at[pair] : at[pair] + 32, s * 128 : s * 128 + 128]
                else:
                    mixed = [spec[f2 : f2 + 32, :] for f2 in at]
                    packed[c, to[0], :] = jnp.where(lane < 64, mixed[0], pltpu.roll(mixed[1], 64, 1))
                    packed[c, to[1], :] = jnp.where(lane < 64, pltpu.roll(mixed[0], 64, 1), mixed[1])
        return 0

    lax.fori_loop(0, SLOTS, inner, 0)

    def emit(p, _):
        for tile in range(packed.shape[0]):
            out[p, :, tile * INNER : (tile + 1) * INNER] = packed[
                tile, pl.ds(pl.multiple_of(p * ROW_STRIDE, 8), SLOTS), :
            ].astype(jnp.bfloat16)
        return 0

    lax.fori_loop(0, DEVICES, emit, 0, unroll=4)


def spectra_of(part, vre, vim, taps, interpret=False):
    cos_t, sin_t = twist_tables()
    mat = inner_matrix().astype(jnp.bfloat16)
    count = len(PARTS[part])
    tiles = count // 2
    return pl.pallas_call(
        functools.partial(spectra_kernel, part),
        out_shape=jax.ShapeDtypeStruct((DEVICES, SLOTS, tiles * INNER), jnp.bfloat16),
        in_specs=[pl.BlockSpec(memory_space=pltpu.VMEM)] * 6,
        out_specs=pl.BlockSpec(memory_space=pltpu.VMEM),
        scratch_shapes=[
            pltpu.VMEM((2, count, OUTER, SLOTS, INNER), jnp.float32),
            pltpu.VMEM((2, SLOTS * (32 * count + 8), INNER), jnp.float32),
            pltpu.VMEM((tiles, DEVICES * ROW_STRIDE, INNER), jnp.float32),
        ],
        compiler_params=pltpu.CompilerParams(vmem_limit_bytes=32 * MIB),
        cost_estimate=pl.CostEstimate(flops=2 * 10**8 * count, bytes_accessed=4 * 10**6 * count, transcendentals=0),
        interpret=interpret,
        name="spectra" + "ab"[part],
    )(vre, vim, taps, jnp.asarray(cos_t), jnp.asarray(sin_t), jnp.asarray(mat))


def quarter_kernel(where, wre, wim, slots, out, total):
    step = pl.program_id(0)
    rows = jnp.where(where[0] == 0, wre[...], wim[...]).astype(jnp.bfloat16)
    antenna = lax.broadcasted_iota(jnp.int32, (rows.shape[0], slots.shape[2]), 0) + step * rows.shape[0]
    chosen = jnp.where(antenna == slots[0], 1.0, 0.0).astype(jnp.bfloat16)
    part = lax.dot_general(rows, chosen, (((0,), (0,)), ((), ())), preferred_element_type=jnp.float32)

    @pl.when(step == 0)
    def _():
        total[...] = part

    @pl.when(step > 0)
    def _():
        total[...] = total[...] + part

    @pl.when(step == pl.num_programs(0) - 1)
    def _():
        out[...] = total[...].astype(jnp.bfloat16)


def quarter_of(y_lo, core, wre, wim, antenna_map, interpret=False):
    antennas, beams = wre.shape
    depth = 512
    half = antennas // 2
    grid_spec = pltpu.PrefetchScalarGridSpec(
        num_scalar_prefetch=1,
        grid=(antennas // depth,),
        in_specs=[
            pl.BlockSpec((depth, beams), lambda i, w: (jnp.where(w[0] == 0, i, 0), 0)),
            pl.BlockSpec((depth, beams), lambda i, w: (jnp.where(w[0] == 0, 0, i), 0)),
            pl.BlockSpec((1, 1, half), lambda i, w: (w[1], 0, 0)),
        ],
        out_specs=pl.BlockSpec((beams, half), lambda i, w: (0, 0)),
        scratch_shapes=[pltpu.VMEM((beams, half), jnp.float32)],
    )
    return pl.pallas_call(
        quarter_kernel,
        grid_spec=grid_spec,
        out_shape=jax.ShapeDtypeStruct((beams, half), jnp.bfloat16),
        compiler_params=pltpu.CompilerParams(vmem_limit_bytes=57 * MIB),
        cost_estimate=pl.CostEstimate(flops=2 * 10**9, bytes_accessed=6 * 10**6, transcendentals=0),
        interpret=interpret,
        name="quarter",
    )(jnp.stack([y_lo, core]).astype(jnp.int32), wre, wim, antenna_map.reshape(2, 1, half))


def choose_matrix():
    chosen = np.zeros((2, 32, 3, 4, 32), np.float32)
    for pair in range(2):
        for f1 in range(32):
            chosen[pair, f1, pair, :, f1] = 1.0
            chosen[pair, f1, 2, 2 * pair : 2 * pair + 2, f1] = 1.0
    return chosen.reshape(64, 384)


def early_kernel(w0, w1, za, zb, out):
    for i, part in enumerate((w0, w1)):
        w = part[...]
        n = w.shape[0]
        out[i * n : (i + 1) * n, :512] = jnp.dot(w, za[...], preferred_element_type=jnp.float32)
        out[i * n : (i + 1) * n, 512:] = jnp.dot(w, zb[...], preferred_element_type=jnp.float32)


def early_of(w0, w1, za, zb, interpret=False):
    return pl.pallas_call(
        early_kernel,
        out_shape=jax.ShapeDtypeStruct((2 * w0.shape[0], 768), jnp.float32),
        in_specs=[pl.BlockSpec(memory_space=pltpu.VMEM)] * 4,
        out_specs=pl.BlockSpec(memory_space=pltpu.VMEM),
        compiler_params=pltpu.CompilerParams(vmem_limit_bytes=24 * MIB),
        cost_estimate=pl.CostEstimate(flops=17 * 10**8, bytes_accessed=8 * 10**6, transcendentals=0),
        interpret=interpret,
        name="early",
    )(w0, w1, za, zb)


def beams_kernel(places, early, w2, w3, za, zb, choose, out, sums):
    for k in range(32):
        at = pl.multiple_of(places[k], 16)
        sums[pl.ds(at, 16), :] = early[k * 16 : (k + 1) * 16, :]
    for i, part in enumerate((w2, w3)):
        w = part[...]
        first = jnp.dot(w, za[...], preferred_element_type=jnp.float32)
        second = jnp.dot(w, zb[...], preferred_element_type=jnp.float32)
        for k in range(16):
            at = pl.multiple_of(places[(i + 2) * 16 + k], 16)
            sums[pl.ds(at, 16), :512] = first[k * 16 : (k + 1) * 16, :]
            sums[pl.ds(at, 16), 512:] = second[k * 16 : (k + 1) * 16, :]
    beams = sums.shape[0] // 2

    def power(re_lanes, im_lanes):
        re = sums[:beams, re_lanes] - sums[beams:, im_lanes]
        im = sums[beams:, re_lanes] + sums[:beams, im_lanes]
        return re * re + im * im

    powers = jnp.concatenate(
        [power(slice(0, 256), slice(256, 512)), power(slice(512, 640), slice(640, 768))], axis=1
    )
    total = lax.dot_general(
        choose[...],
        powers,
        (((1,), (1,)), ((), ())),
        preferred_element_type=jnp.float32,
        precision=lax.Precision.HIGHEST,
    )
    out[...] = total * (1.0 / SPECTRA)


def beams_of(places, early, w2, w3, za, zb, interpret=False):
    rows = early.shape[0] + 2 * w2.shape[0]
    return pl.pallas_call(
        beams_kernel,
        out_shape=jax.ShapeDtypeStruct((64, rows // 2), jnp.float32),
        in_specs=[pl.BlockSpec(memory_space=pltpu.SMEM)] + [pl.BlockSpec(memory_space=pltpu.VMEM)] * 6,
        out_specs=pl.BlockSpec(memory_space=pltpu.VMEM),
        scratch_shapes=[pltpu.VMEM((rows, 768), jnp.float32)],
        compiler_params=pltpu.CompilerParams(vmem_limit_bytes=32 * MIB),
        cost_estimate=pl.CostEstimate(flops=17 * 10**8, bytes_accessed=8 * 10**6, transcendentals=0),
        interpret=interpret,
        name="beams",
    )(places, early, w2, w3, za, zb, jnp.asarray(choose_matrix()))


def index_of(z, x, y, core):
    return ((y % 2) * 2 + core) * 32 + (z % 4) * 8 + (x % 4) * 2 + (y % 4) // 2


EVERY = [(z, x, y, c) for z in range(4) for x in range(4) for y in range(4) for c in range(2)]
ORDER = (("y", "x", "z"), ("z", "y", "x"))
SHIFTS = (0, -1, 1, 2)


def permutation(stage, shift):
    pairs = []
    for z, x, y, core in EVERY:
        axis = ORDER[core][stage]
        source = {"z": z, "x": x, "y": y}
        source[axis] += shift
        pairs.append((index_of(source["z"], source["x"], source["y"], core), index_of(z, x, y, core)))
    return pairs


def gather_stage(block, stage):
    return [block] + [lax.ppermute(block, ALL, permutation(stage, shift)) for shift in SHIFTS[1:]]


def block_places(grp, dev):
    core = grp % 2
    z, x, y = dev // 8, dev // 2 % 4, dev % 2 * 2 + grp // 2
    k = np.arange(64)
    shift = np.array(SHIFTS)
    first, second, third = shift[k % 4], shift[k // 4 % 4], shift[k // 16]
    by_core = []
    for order in ORDER:
        moved = dict(zip(order, (first, second, third)))
        by_core.append([moved[axis] for axis in "zxy"])
    is_first = core == 0
    mz, mx, my = [jnp.where(is_first, jnp.asarray(a), jnp.asarray(b)) for a, b in zip(*by_core)]
    fz, fx, fy = (z + mz + 4) % 4, (x + mx + 4) % 4, (y + my + 4) % 4
    return (((fy % 2) * 32 + fz * 8 + fx * 2 + fy // 2) * 16).astype(jnp.int32)


SWAP = [(0, 1), (1, 0), (2, 3), (3, 2)]


def on_device(voltage_real, voltage_imaginary, filter_taps, weights_re, weights_im, owners, antenna_map):
    grp, dev = lax.axis_index("grp"), lax.axis_index("dev")
    y_lo, core = grp // 2, grp % 2

    quarter = quarter_of(y_lo, core, weights_re[0], weights_im[0], antenna_map)
    offers = lax.all_to_all(quarter.reshape(32, 16, -1), "dev", split_axis=0, concat_axis=0, tiled=True)

    moved = []
    for part in range(2):
        rows = spectra_of(part, voltage_real, voltage_imaginary, filter_taps)
        rows = lax.all_to_all(rows, ALL, split_axis=0, concat_axis=0, tiled=True)
        moved.append(rows.reshape(DEVICES * SLOTS, -1))

    mine = lax.dynamic_index_in_dim(offers, owners[core], 0, keepdims=False)
    other = lax.dynamic_index_in_dim(offers, owners[1 - core], 0, keepdims=False)
    other = lax.ppermute(other, "grp", SWAP)
    block = jnp.where(
        core == 0,
        jnp.concatenate([mine, other], axis=1),
        jnp.concatenate([other, mine], axis=1),
    )
    block = jnp.concatenate(gather_stage(block, 0), axis=0)
    block = jnp.concatenate(gather_stage(block, 1), axis=0)
    parts = gather_stage(block, 2)

    early = early_of(parts[0], parts[3], *moved)
    places = block_places(grp, dev)
    places = jnp.concatenate([places[:16], places[48:], places[16:48]])
    power = beams_of(places, early, parts[1], parts[2], *moved)
    power = power.reshape(2, 32, -1)
    own = lax.dynamic_index_in_dim(power, core, 0, keepdims=False)
    given = lax.dynamic_index_in_dim(power, 1 - core, 0, keepdims=False)
    taken = lax.ppermute(given, "grp", SWAP)
    return jnp.where(core == 0, jnp.stack([own, taken]), jnp.stack([taken, own]))


def solution(mesh):
    return jax.shard_map(
        on_device,
        mesh=mesh,
        in_specs=(
            P(("grp", "dev"), None),
            P(("grp", "dev"), None),
            P(),
            P("dev", None, None),
            P("dev", None, None),
            P(),
            P(),
        ),
        out_specs=P(None, ("grp", "dev"), None),
        check_vma=False,
    )
```

```python
import functools
import math

import jax
import jax.numpy as jnp
import numpy as np
from jax import lax
from jax.experimental import pallas as pl
from jax.experimental.pallas import tpu as pltpu
from jax.sharding import PartitionSpec as P

CHANNELS = 4096
TAPS = 16
SPECTRA = 6
STEPS = 2
FRAMES = STEPS * SPECTRA
BLOCKS = FRAMES + TAPS - 1
OUTER = 32
INNER = 128
SLOTS = 16
DEVICES = 128
ROW_STRIDE = 24
GROUPS = ((0, 1, 6, 7), (2, 3, 8, 9), (4, 5, 10, 11))
MESSAGES = ((0, 1), (2,))
ALL = ("grp", "dev")
MIB = 1 << 20


def twist_tables():
    products = np.outer(np.arange(OUTER), np.arange(INNER)) % CHANNELS
    angles = products * (2.0 * math.pi / CHANNELS)
    return np.cos(angles).astype(np.float32), np.sin(angles).astype(np.float32)


def inner_matrix():
    products = np.outer(np.arange(INNER), np.arange(INNER)) % INNER
    angles = products * (2.0 * math.pi / INNER)
    norm = CHANNELS ** (-0.5)
    c, s = np.cos(angles) * norm, np.sin(angles) * norm
    return np.block([[c, s], [-s, c]]).astype(np.float32)


def small_fft(points):
    count = len(points)
    if count == 1:
        return points
    even = small_fft(points[0::2])
    odd = small_fft(points[1::2])
    half = count // 2
    result = [None] * count
    for k in range(half):
        er, ei = even[k]
        xr, xi = odd[k]
        if k == 0:
            tr, ti = xr, xi
        elif 4 * k == count:
            tr, ti = xi, -xr
        elif 8 * k == count:
            r = math.sqrt(0.5)
            tr, ti = (xr + xi) * r, (xi - xr) * r
        elif 8 * k == 3 * count:
            r = math.sqrt(0.5)
            tr, ti = (xi - xr) * r, (xr + xi) * (-r)
        else:
            c = math.cos(2.0 * math.pi * k / count)
            s = math.sin(2.0 * math.pi * k / count)
            tr, ti = xr * c + xi * s, xi * c - xr * s
        result[k] = (er + tr, ei + ti)
        result[k + half] = (er - tr, ei - ti)
    return result


def spectra_kernel(messages, *refs):
    groups = [group for message in messages for group in message]
    count = len(groups)
    sources, outs = refs[:6], refs[6 : 6 + len(messages)]
    vre, vim, taps, cos_t, sin_t, mat, frames, turned, packed, ready, sems = refs[6 + len(messages) :]
    chosen = [u for group in groups for u in GROUPS[group]]
    first, last = min(chosen), max(chosen) + TAPS
    rows_per_slot = 32 * len(chosen)
    slot_stride = rows_per_slot + 8

    loads = []
    for i in (2, 0, 1, 3, 4, 5):
        source = sources[i]
        if i < 2:
            source = source.at[:, first * CHANNELS : last * CHANNELS]
        loads.append(pltpu.make_async_copy(source, (vre, vim, taps, cos_t, sin_t, mat)[i], sems.at[i]))
        loads[-1].start()
    loads[0].wait()

    for c, volts in ((0, vre), (1, vim)):
        loads[1 + c].wait()

        def fir(n1, _, c=c, volts=volts):
            rows = [taps[k : k + 1, pl.ds(pl.multiple_of(n1 * INNER, INNER), INNER)] for k in range(TAPS)]
            needed = sorted({u + k for u in chosen for k in range(TAPS)})
            window = {
                b: volts[
                    :, pl.ds(pl.multiple_of((b - first) * CHANNELS + n1 * INNER, INNER), INNER)
                ].astype(jnp.float32)
                for b in needed
            }
            for i, u in enumerate(chosen):
                total = window[u] * rows[0]
                for k in range(1, TAPS):
                    total = total + window[u + k] * rows[k]
                frames[c, i, n1] = total
            return 0

        lax.fori_loop(0, OUTER, fir, 0)

    for load in loads[3:]:
        load.wait()

    def outer(i, _):
        u = i // 2
        low = pl.multiple_of((i % 2) * 8, 8)
        points = [
            (frames[0, u, n1, pl.ds(low, 8), :], frames[1, u, n1, pl.ds(low, 8), :]) for n1 in range(OUTER)
        ]
        points = small_fft(points)
        for f1 in range(OUTER):
            re, im = points[f1]
            if f1:
                c, d = cos_t[f1 : f1 + 1, :], sin_t[f1 : f1 + 1, :]
                re, im = re * c + im * d, im * c - re * d
            at = low * slot_stride + u * 32 + f1
            turned[0, pl.ds(at, 8, stride=slot_stride), :] = re
            turned[1, pl.ds(at, 8, stride=slot_stride), :] = im
        return 0

    lax.fori_loop(0, 2 * len(chosen), outer, 0)

    matrix = mat[...]
    lane = lax.broadcasted_iota(jnp.int32, (32, INNER), 1)

    def inner(a, _):
        base = pl.multiple_of(a * slot_stride, 8)
        rows = jnp.concatenate(
            [turned[0, pl.ds(base, rows_per_slot), :], turned[1, pl.ds(base, rows_per_slot), :]], axis=1
        ).astype(jnp.bfloat16)
        spec = lax.dot_general(
            matrix, rows, (((1,), (1,)), ((), ())), preferred_element_type=jnp.float32
        )
        for g in range(count):
            for y in range(2):
                for c in range(2):
                    to = [pl.ds((y * 2 + s) * 32 * ROW_STRIDE + a, 32, stride=ROW_STRIDE) for s in range(2)]
                    at = [c * 128 + (y * 2 + pair) * 32 for pair in range(2)]
                    mixed = [spec[f2 : f2 + 32, g * INNER : (g + 1) * INNER] for f2 in at]
                    packed[g * 2 + c, to[0], :] = jnp.where(lane < 64, mixed[0], pltpu.roll(mixed[1], 64, 1))
                    packed[g * 2 + c, to[1], :] = jnp.where(lane < 64, pltpu.roll(mixed[0], 64, 1), mixed[1])
        return 0

    lax.fori_loop(0, SLOTS, inner, 0)

    stores = []
    tile = 0
    for message, to in zip(messages, outs):
        for quarter in range(4):

            def emit(p, _, tile=tile, wide=2 * len(message)):
                for i in range(tile, tile + wide):
                    ready[p, :, i * INNER : (i + 1) * INNER] = packed[
                        i, pl.ds(pl.multiple_of(p * ROW_STRIDE, 8), SLOTS), :
                    ].astype(jnp.bfloat16)
                return 0

            lax.fori_loop(quarter * 32, quarter * 32 + 32, emit, 0, unroll=4)
            part = pl.ds(quarter * 32, 32)
            lanes = slice(tile * INNER, (tile + 2 * len(message)) * INNER)
            stores.append(
                pltpu.make_async_copy(ready.at[part, :, lanes], to.at[part], sems.at[6 + len(stores)])
            )
            stores[-1].start()
        tile += 2 * len(message)
    for store in stores:
        store.wait()


def spectra_of(messages, vre, vim, taps, interpret=False):
    cos_t, sin_t = twist_tables()
    mat = inner_matrix().astype(jnp.bfloat16)
    groups = [group for message in messages for group in message]
    count = len(groups)
    many = 4 * count
    chosen = [u for group in groups for u in GROUPS[group]]
    samples = (max(chosen) + TAPS - min(chosen)) * CHANNELS
    return pl.pallas_call(
        functools.partial(spectra_kernel, messages),
        out_shape=[jax.ShapeDtypeStruct((DEVICES, SLOTS, 2 * INNER * len(m)), jnp.bfloat16) for m in messages],
        in_specs=[pl.BlockSpec(memory_space=pltpu.HBM)] * 6,
        out_specs=[pl.BlockSpec(memory_space=pltpu.HBM)] * len(messages),
        scratch_shapes=[
            pltpu.VMEM((SLOTS, samples), jnp.bfloat16),
            pltpu.VMEM((SLOTS, samples), jnp.bfloat16),
            pltpu.VMEM((TAPS, CHANNELS), jnp.float32),
            pltpu.VMEM((OUTER, INNER), jnp.float32),
            pltpu.VMEM((OUTER, INNER), jnp.float32),
            pltpu.VMEM((256, 256), jnp.bfloat16),
            pltpu.VMEM((2, many, OUTER, SLOTS, INNER), jnp.float32),
            pltpu.VMEM((2, SLOTS * (32 * many + 8), INNER), jnp.float32),
            pltpu.VMEM((2 * count, DEVICES * ROW_STRIDE, INNER), jnp.float32),
            pltpu.VMEM((DEVICES, SLOTS, 2 * count * INNER), jnp.bfloat16),
            pltpu.SemaphoreType.DMA((6 + 4 * len(messages),)),
        ],
        compiler_params=pltpu.CompilerParams(vmem_limit_bytes=58 * MIB),
        cost_estimate=pl.CostEstimate(
            flops=8 * 10**8 * count, bytes_accessed=16 * 10**6 * count, transcendentals=0
        ),
        interpret=interpret,
        name="spectra",
    )(vre, vim, taps, jnp.asarray(cos_t), jnp.asarray(sin_t), jnp.asarray(mat))


def quarter_kernel(where, wre, wim, slots, out, total):
    step = pl.program_id(0)
    rows = jnp.where(where[0] == 0, wre[...], wim[...]).astype(jnp.bfloat16)
    antenna = lax.broadcasted_iota(jnp.int32, (rows.shape[0], slots.shape[2]), 0) + step * rows.shape[0]
    chosen = jnp.where(antenna == slots[0], 1.0, 0.0).astype(jnp.bfloat16)
    part = lax.dot_general(rows, chosen, (((0,), (0,)), ((), ())), preferred_element_type=jnp.float32)

    @pl.when(step == 0)
    def _():
        total[...] = part

    @pl.when(step > 0)
    def _():
        total[...] = total[...] + part

    @pl.when(step == pl.num_programs(0) - 1)
    def _():
        out[...] = total[...].astype(jnp.bfloat16)


def quarter_of(info, wre, wim, antenna_map, interpret=False):
    antennas, beams = wre.shape
    depth = 512
    half = antennas // 2
    grid_spec = pltpu.PrefetchScalarGridSpec(
        num_scalar_prefetch=1,
        grid=(antennas // depth,),
        in_specs=[
            pl.BlockSpec((depth, beams), lambda i, w: (jnp.where(w[0] == 0, i, 0), 0)),
            pl.BlockSpec((depth, beams), lambda i, w: (jnp.where(w[0] == 0, 0, i), 0)),
            pl.BlockSpec((1, 1, half), lambda i, w: (w[1], 0, 0)),
        ],
        out_specs=pl.BlockSpec((beams, half), lambda i, w: (0, 0)),
        scratch_shapes=[pltpu.VMEM((beams, half), jnp.float32)],
    )
    return pl.pallas_call(
        quarter_kernel,
        grid_spec=grid_spec,
        out_shape=jax.ShapeDtypeStruct((beams, half), jnp.bfloat16),
        compiler_params=pltpu.CompilerParams(vmem_limit_bytes=58 * MIB),
        cost_estimate=pl.CostEstimate(flops=2 * 10**9, bytes_accessed=6 * 10**6, transcendentals=0),
        interpret=interpret,
        name="quarter",
    )(info, wre, wim, antenna_map.reshape(2, 1, half))


def pick_kernel(info, first, second, mine, other):
    mine[...] = first[0]
    other[...] = second[0]


def pick_of(info, offers, interpret=False):
    _, rows, columns = offers.shape
    return pl.pallas_call(
        pick_kernel,
        grid_spec=pltpu.PrefetchScalarGridSpec(
            num_scalar_prefetch=1,
            grid=(1,),
            in_specs=[
                pl.BlockSpec((1, rows, columns), lambda i, w: (w[2], 0, 0)),
                pl.BlockSpec((1, rows, columns), lambda i, w: (w[3], 0, 0)),
            ],
            out_specs=[pl.BlockSpec((rows, columns), lambda i, w: (0, 0))] * 2,
        ),
        out_shape=[jax.ShapeDtypeStruct((rows, columns), offers.dtype)] * 2,
        interpret=interpret,
        name="pick",
    )(info, offers, offers)


def join_kernel(*refs):
    parts, out = refs[:-1], refs[-1]
    at = 0
    for part in parts:
        rows = part.shape[0]
        out[at : at + rows, :] = part[...]
        at += rows


def join_of(parts, interpret=False):
    rows = sum(p.shape[0] for p in parts)
    return pl.pallas_call(
        join_kernel,
        out_shape=jax.ShapeDtypeStruct((rows, parts[0].shape[1]), parts[0].dtype),
        in_specs=[pl.BlockSpec(memory_space=pltpu.VMEM)] * len(parts),
        out_specs=pl.BlockSpec(memory_space=pltpu.VMEM),
        compiler_params=pltpu.CompilerParams(vmem_limit_bytes=8 * MIB),
        interpret=interpret,
        name="join",
    )(*parts)


def choose_matrix():
    chosen = np.zeros((2, 32, 3, 2, 2, 32), np.float32)
    for pair in range(2):
        for f1 in range(32):
            chosen[pair, f1, :, pair, :, f1] = 1.0
    return chosen.reshape(64, 384)


def products(core, part, spectra):
    half = part.shape[1] // 2
    near = pl.ds(pl.multiple_of(core * half, half), half)
    far = pl.ds(pl.multiple_of((1 - core) * half, half), half)
    left, right = part[:, :half], part[:, half:]
    return [
        jnp.dot(left, z[near, :], preferred_element_type=jnp.float32)
        + jnp.dot(right, z[far, :], preferred_element_type=jnp.float32)
        for z in spectra
    ]


def early_kernel(info, w0, w1, za, zb, out):
    for i, part in enumerate((w0, w1)):
        n = part.shape[0]
        first, second = products(info[1], part, (za, zb))
        out[i * n : (i + 1) * n, :512] = first
        out[i * n : (i + 1) * n, 512:] = second


def early_of(info, w0, w1, spectra, interpret=False):
    return pl.pallas_call(
        early_kernel,
        out_shape=jax.ShapeDtypeStruct((2 * w0.shape[0], 768), jnp.float32),
        in_specs=[pl.BlockSpec(memory_space=pltpu.SMEM)] + [pl.BlockSpec(memory_space=pltpu.VMEM)] * 4,
        out_specs=pl.BlockSpec(memory_space=pltpu.VMEM),
        compiler_params=pltpu.CompilerParams(vmem_limit_bytes=24 * MIB),
        cost_estimate=pl.CostEstimate(flops=17 * 10**8, bytes_accessed=8 * 10**6, transcendentals=0),
        interpret=interpret,
        name="early",
    )(info, w0, w1, *spectra)


def beams_kernel(info, places, early, w2, w3, za, zb, choose, out, sums):
    for k in range(32):
        at = pl.multiple_of(places[k], 16)
        sums[pl.ds(at, 16), :] = early[k * 16 : (k + 1) * 16, :]
    for i, part in enumerate((w2, w3)):
        first, second = products(info[1], part, (za, zb))
        for k in range(16):
            at = pl.multiple_of(places[(i + 2) * 16 + k], 16)
            sums[pl.ds(at, 16), :512] = first[k * 16 : (k + 1) * 16, :]
            sums[pl.ds(at, 16), 512:] = second[k * 16 : (k + 1) * 16, :]
    beams = sums.shape[0] // 2
    powers = []
    for g in range(3):
        re_lanes, im_lanes = slice(g * 256, g * 256 + 128), slice(g * 256 + 128, g * 256 + 256)
        re = sums[:beams, re_lanes] - sums[beams:, im_lanes]
        im = sums[beams:, re_lanes] + sums[:beams, im_lanes]
        powers.append(re * re + im * im)
    total = lax.dot_general(
        choose[...],
        jnp.concatenate(powers, axis=1),
        (((1,), (1,)), ((), ())),
        preferred_element_type=jnp.float32,
        precision=lax.Precision.HIGHEST,
    )
    out[...] = total * (1.0 / SPECTRA)


def beams_of(info, places, early, w2, w3, spectra, interpret=False):
    rows = early.shape[0] + 2 * w2.shape[0]
    return pl.pallas_call(
        beams_kernel,
        out_shape=jax.ShapeDtypeStruct((64, rows // 2), jnp.float32),
        in_specs=[pl.BlockSpec(memory_space=pltpu.SMEM)] * 2 + [pl.BlockSpec(memory_space=pltpu.VMEM)] * 6,
        out_specs=pl.BlockSpec(memory_space=pltpu.VMEM),
        scratch_shapes=[pltpu.VMEM((rows, 768), jnp.float32)],
        compiler_params=pltpu.CompilerParams(vmem_limit_bytes=32 * MIB),
        cost_estimate=pl.CostEstimate(flops=17 * 10**8, bytes_accessed=8 * 10**6, transcendentals=0),
        interpret=interpret,
        name="beams",
    )(info, places, early, w2, w3, *spectra, jnp.asarray(choose_matrix()))


def index_of(z, x, y, core):
    return ((y % 2) * 2 + core) * 32 + (z % 4) * 8 + (x % 4) * 2 + (y % 4) // 2


EVERY = [(z, x, y, c) for z in range(4) for x in range(4) for y in range(4) for c in range(2)]
ORDER = (("y", "x", "z"), ("z", "y", "x"))
SHIFTS = (0, -1, 1, 2)


def permutation(stage, shift):
    pairs = []
    for z, x, y, core in EVERY:
        axis = ORDER[core][stage]
        source = {"z": z, "x": x, "y": y}
        source[axis] += shift
        pairs.append((index_of(source["z"], source["x"], source["y"], core), index_of(z, x, y, core)))
    return pairs


def gather_stage(block, stage):
    return [block] + [lax.ppermute(block, ALL, permutation(stage, shift)) for shift in SHIFTS[1:]]


def block_places(grp, dev):
    core = grp % 2
    z, x, y = dev // 8, dev // 2 % 4, dev % 2 * 2 + grp // 2
    k = np.arange(64)
    shift = np.array(SHIFTS)
    first, second, third = shift[k % 4], shift[k // 4 % 4], shift[k // 16]
    by_core = []
    for order in ORDER:
        moved = dict(zip(order, (first, second, third)))
        by_core.append([moved[axis] for axis in "zxy"])
    is_first = core == 0
    mz, mx, my = [jnp.where(is_first, jnp.asarray(a), jnp.asarray(b)) for a, b in zip(*by_core)]
    fz, fx, fy = (z + mz + 4) % 4, (x + mx + 4) % 4, (y + my + 4) % 4
    return (((fy % 2) * 32 + fz * 8 + fx * 2 + fy // 2) * 16).astype(jnp.int32)


SWAP = [(0, 1), (1, 0), (2, 3), (3, 2)]


def on_device(voltage_real, voltage_imaginary, filter_taps, weights_re, weights_im, owners, antenna_map):
    grp, dev = lax.axis_index("grp"), lax.axis_index("dev")
    core = grp % 2
    ordered = jnp.where(core == 0, owners, owners[::-1])
    info = jnp.concatenate([jnp.stack([grp // 2, core]).astype(jnp.int32), ordered])

    quarter = quarter_of(info, weights_re[0], weights_im[0], antenna_map)
    offers = lax.all_to_all(quarter.reshape(32, 16, -1), "dev", split_axis=0, concat_axis=0, tiled=True)

    volts = (voltage_real, voltage_imaginary, filter_taps)
    quarter, *volts = lax.optimization_barrier((quarter, *volts))
    messages = spectra_of(MESSAGES, *volts)
    def turn(message):
        moved = lax.all_to_all(message, ALL, split_axis=0, concat_axis=0, tiled=True)
        return moved.reshape(DEVICES * SLOTS, -1)

    message, offers = lax.optimization_barrier((messages[0], offers))
    spectra = [turn(message)]
    mine, other = pick_of(info, offers)
    other = lax.ppermute(other, "grp", SWAP)
    block = jnp.concatenate([mine, other], axis=1)
    block = join_of(gather_stage(block, 0))
    block, message, spectra[0] = lax.optimization_barrier((block, messages[1], spectra[0]))
    spectra.append(turn(message))
    block = join_of(gather_stage(block, 1))
    parts = gather_stage(block, 2)

    early = early_of(info, parts[0], parts[3], spectra)
    places = block_places(grp, dev)
    places = jnp.concatenate([places[:16], places[48:], places[16:48]])
    power = beams_of(info, places, early, parts[1], parts[2], spectra)
    power = power.reshape(2, 32, -1)
    own = jnp.where(core == 0, power[0], power[1])
    given = jnp.where(core == 0, power[1], power[0])
    taken = lax.ppermute(given, "grp", SWAP)
    return jnp.where(core == 0, jnp.stack([own, taken]), jnp.stack([taken, own]))


def solution(mesh):
    return jax.shard_map(
        on_device,
        mesh=mesh,
        in_specs=(
            P(("grp", "dev"), None),
            P(("grp", "dev"), None),
            P(),
            P("dev", None, None),
            P("dev", None, None),
            P(),
            P(),
        ),
        out_specs=P(None, ("grp", "dev"), None),
        check_vma=False,
    )
```

```python
import functools
import math

import jax
import jax.numpy as jnp
import numpy as np
from jax import lax
from jax.experimental import pallas as pl
from jax.experimental.pallas import tpu as pltpu
from jax.sharding import PartitionSpec as P

CHANNELS = 4096
TAPS = 16
SPECTRA = 6
STEPS = 2
FRAMES = STEPS * SPECTRA
BLOCKS = FRAMES + TAPS - 1
OUTER = 32
INNER = 128
SLOTS = 16
DEVICES = 128
ROW_STRIDE = 24
GROUPS = ((0, 1, 6, 7), (2, 3, 8, 9), (4, 5, 10, 11))
MESSAGES = ((2,), (0, 1))
ALL = ("grp", "dev")
MIB = 1 << 20


def twist_tables():
    products = np.outer(np.arange(OUTER), np.arange(INNER)) % CHANNELS
    angles = products * (2.0 * math.pi / CHANNELS)
    return np.cos(angles).astype(np.float32), np.sin(angles).astype(np.float32)


def inner_matrix():
    products = np.outer(np.arange(INNER), np.arange(INNER)) % INNER
    angles = products * (2.0 * math.pi / INNER)
    norm = CHANNELS ** (-0.5)
    c, s = np.cos(angles) * norm, np.sin(angles) * norm
    return np.block([[c, s], [-s, c]]).astype(np.float32)


def small_fft(points):
    count = len(points)
    if count == 1:
        return points
    even = small_fft(points[0::2])
    odd = small_fft(points[1::2])
    half = count // 2
    result = [None] * count
    for k in range(half):
        er, ei = even[k]
        xr, xi = odd[k]
        if k == 0:
            tr, ti = xr, xi
        elif 4 * k == count:
            tr, ti = xi, -xr
        elif 8 * k == count:
            r = math.sqrt(0.5)
            tr, ti = (xr + xi) * r, (xi - xr) * r
        elif 8 * k == 3 * count:
            r = math.sqrt(0.5)
            tr, ti = (xi - xr) * r, (xr + xi) * (-r)
        else:
            c = math.cos(2.0 * math.pi * k / count)
            s = math.sin(2.0 * math.pi * k / count)
            tr, ti = xr * c + xi * s, xi * c - xr * s
        result[k] = (er + tr, ei + ti)
        result[k + half] = (er - tr, ei - ti)
    return result


def spectra_kernel(messages, *refs):
    groups = [group for message in messages for group in message]
    count = len(groups)
    sources, outs = refs[:6], refs[6 : 6 + len(messages)]
    vre, vim, taps, cos_t, sin_t, mat, frames, turned, packed, ready, sems = refs[6 + len(messages) :]
    chosen = [u for group in groups for u in GROUPS[group]]
    first, last = min(chosen), max(chosen) + TAPS
    rows_per_slot = 32 * len(chosen)
    slot_stride = rows_per_slot + 8

    loads = []
    for i in (2, 0, 1, 3, 4, 5):
        source = sources[i]
        if i < 2:
            source = source.at[:, first * CHANNELS : last * CHANNELS]
        loads.append(pltpu.make_async_copy(source, (vre, vim, taps, cos_t, sin_t, mat)[i], sems.at[i]))
        loads[-1].start()
    loads[0].wait()

    for c, volts in ((0, vre), (1, vim)):
        loads[1 + c].wait()

        def fir(n1, _, c=c, volts=volts):
            rows = [taps[k : k + 1, pl.ds(pl.multiple_of(n1 * INNER, INNER), INNER)] for k in range(TAPS)]
            needed = sorted({u + k for u in chosen for k in range(TAPS)})
            window = {
                b: volts[
                    :, pl.ds(pl.multiple_of((b - first) * CHANNELS + n1 * INNER, INNER), INNER)
                ].astype(jnp.float32)
                for b in needed
            }
            for i, u in enumerate(chosen):
                total = window[u] * rows[0]
                for k in range(1, TAPS):
                    total = total + window[u + k] * rows[k]
                frames[c, i, n1] = total
            return 0

        lax.fori_loop(0, OUTER, fir, 0)

    for load in loads[3:]:
        load.wait()

    def outer(i, _):
        u = i // 2
        low = pl.multiple_of((i % 2) * 8, 8)
        points = [
            (frames[0, u, n1, pl.ds(low, 8), :], frames[1, u, n1, pl.ds(low, 8), :]) for n1 in range(OUTER)
        ]
        points = small_fft(points)
        for f1 in range(OUTER):
            re, im = points[f1]
            if f1:
                c, d = cos_t[f1 : f1 + 1, :], sin_t[f1 : f1 + 1, :]
                re, im = re * c + im * d, im * c - re * d
            at = low * slot_stride + u * 32 + f1
            turned[0, pl.ds(at, 8, stride=slot_stride), :] = re
            turned[1, pl.ds(at, 8, stride=slot_stride), :] = im
        return 0

    lax.fori_loop(0, 2 * len(chosen), outer, 0)

    matrix = mat[...]
    lane = lax.broadcasted_iota(jnp.int32, (32, INNER), 1)

    def inner(a, _):
        base = pl.multiple_of(a * slot_stride, 8)
        rows = jnp.concatenate(
            [turned[0, pl.ds(base, rows_per_slot), :], turned[1, pl.ds(base, rows_per_slot), :]], axis=1
        ).astype(jnp.bfloat16)
        spec = lax.dot_general(
            matrix, rows, (((1,), (1,)), ((), ())), preferred_element_type=jnp.float32
        )
        for g in range(count):
            for y in range(2):
                for c in range(2):
                    to = [pl.ds((y * 2 + s) * 32 * ROW_STRIDE + a, 32, stride=ROW_STRIDE) for s in range(2)]
                    at = [c * 128 + (y * 2 + pair) * 32 for pair in range(2)]
                    mixed = [spec[f2 : f2 + 32, g * INNER : (g + 1) * INNER] for f2 in at]
                    packed[g * 2 + c, to[0], :] = jnp.where(lane < 64, mixed[0], pltpu.roll(mixed[1], 64, 1))
                    packed[g * 2 + c, to[1], :] = jnp.where(lane < 64, pltpu.roll(mixed[0], 64, 1), mixed[1])
        return 0

    lax.fori_loop(0, SLOTS, inner, 0, unroll=4)

    stores = []
    tile = 0
    for message, to in zip(messages, outs):
        for quarter in range(4):

            def emit(p, _, tile=tile, wide=2 * len(message)):
                for i in range(tile, tile + wide):
                    ready[p, :, i * INNER : (i + 1) * INNER] = packed[
                        i, pl.ds(pl.multiple_of(p * ROW_STRIDE, 8), SLOTS), :
                    ].astype(jnp.bfloat16)
                return 0

            lax.fori_loop(quarter * 32, quarter * 32 + 32, emit, 0, unroll=4)
            part = pl.ds(quarter * 32, 32)
            lanes = slice(tile * INNER, (tile + 2 * len(message)) * INNER)
            stores.append(
                pltpu.make_async_copy(ready.at[part, :, lanes], to.at[part], sems.at[6 + len(stores)])
            )
            stores[-1].start()
        tile += 2 * len(message)
    for store in stores:
        store.wait()


def spectra_of(messages, vre, vim, taps, interpret=False):
    cos_t, sin_t = twist_tables()
    mat = inner_matrix().astype(jnp.bfloat16)
    groups = [group for message in messages for group in message]
    count = len(groups)
    many = 4 * count
    chosen = [u for group in groups for u in GROUPS[group]]
    samples = (max(chosen) + TAPS - min(chosen)) * CHANNELS
    return pl.pallas_call(
        functools.partial(spectra_kernel, messages),
        out_shape=[jax.ShapeDtypeStruct((DEVICES, SLOTS, 2 * INNER * len(m)), jnp.bfloat16) for m in messages],
        in_specs=[pl.BlockSpec(memory_space=pltpu.HBM)] * 6,
        out_specs=[pl.BlockSpec(memory_space=pltpu.HBM)] * len(messages),
        scratch_shapes=[
            pltpu.VMEM((SLOTS, samples), jnp.bfloat16),
            pltpu.VMEM((SLOTS, samples), jnp.bfloat16),
            pltpu.VMEM((TAPS, CHANNELS), jnp.float32),
            pltpu.VMEM((OUTER, INNER), jnp.float32),
            pltpu.VMEM((OUTER, INNER), jnp.float32),
            pltpu.VMEM((256, 256), jnp.bfloat16),
            pltpu.VMEM((2, many, OUTER, SLOTS, INNER), jnp.float32),
            pltpu.VMEM((2, SLOTS * (32 * many + 8), INNER), jnp.float32),
            pltpu.VMEM((2 * count, DEVICES * ROW_STRIDE, INNER), jnp.float32),
            pltpu.VMEM((DEVICES, SLOTS, 2 * count * INNER), jnp.bfloat16),
            pltpu.SemaphoreType.DMA((6 + 4 * len(messages),)),
        ],
        compiler_params=pltpu.CompilerParams(vmem_limit_bytes=58 * MIB),
        cost_estimate=pl.CostEstimate(
            flops=8 * 10**8 * count, bytes_accessed=16 * 10**6 * count, transcendentals=0
        ),
        interpret=interpret,
        name="spectra",
    )(vre, vim, taps, jnp.asarray(cos_t), jnp.asarray(sin_t), jnp.asarray(mat))


def quarter_kernel(wre, wim, slots, out, buf, names, chosen, sems):
    grp = lax.axis_index("grp")
    y_lo, core = grp // 2, grp % 2
    antennas, beams = wre.shape
    half = antennas // 2
    name_copy = pltpu.make_async_copy(slots.at[core], names, sems.at[4])
    name_copy.start()
    for y, source in ((0, wre), (1, wim)):

        @pl.when(y_lo == y)
        def _():
            for i in range(4):
                part = pl.ds(i * half // 2, half // 2)
                pltpu.make_async_copy(source.at[part], buf.at[part], sems.at[i]).start()
    name_copy.wait()
    row = names[...]

    def build(i, _):
        antenna = lax.broadcasted_iota(jnp.int32, (16, half), 0) + i * 16
        chosen[pl.ds(pl.multiple_of(i * 16, 16), 16), :] = jnp.where(antenna == row, 1.0, 0.0).astype(jnp.bfloat16)
        return 0
    lax.fori_loop(0, antennas // 16, build, 0, unroll=4)
    for y, source in ((0, wre), (1, wim)):

        @pl.when(y_lo == y)
        def _():
            for i in range(4):
                part = pl.ds(i * half // 2, half // 2)
                pltpu.make_async_copy(source.at[part], buf.at[part], sems.at[i]).wait()
    for j in range(0, beams, 256):
        w = buf[:, j : j + 256].astype(jnp.bfloat16)
        for k in range(0, half, 512):
            out[j : j + 256, k : k + 512] = lax.dot_general(
                w, chosen[:, k : k + 512], (((0,), (0,)), ((), ())), preferred_element_type=jnp.float32
            ).astype(jnp.bfloat16)


def quarter_of(wre, wim, antenna_map, interpret=False):
    antennas, beams = wre.shape
    half = antennas // 2
    return pl.pallas_call(
        quarter_kernel,
        in_specs=[pl.BlockSpec(memory_space=pltpu.HBM)] * 3,
        out_specs=pl.BlockSpec(memory_space=pltpu.VMEM),
        out_shape=jax.ShapeDtypeStruct((beams, half), jnp.bfloat16),
        scratch_shapes=[
            pltpu.VMEM((antennas, beams), jnp.float32),
            pltpu.VMEM((1, half), jnp.int32),
            pltpu.VMEM((antennas, half), jnp.bfloat16),
            pltpu.SemaphoreType.DMA((5,)),
        ],
        compiler_params=pltpu.CompilerParams(vmem_limit_bytes=58 * MIB),
        cost_estimate=pl.CostEstimate(flops=2 * 10**9, bytes_accessed=6 * 10**6, transcendentals=0),
        interpret=interpret,
        name="quarter",
    )(wre, wim, antenna_map.reshape(2, 1, half))


def pick_kernel(owners, offers, mine, other, sems):
    core = lax.axis_index("grp") % 2
    copies = [
        pltpu.make_async_copy(offers.at[owners[core]], mine, sems.at[0]),
        pltpu.make_async_copy(offers.at[owners[1 - core]], other, sems.at[1]),
    ]
    for copy in copies:
        copy.start()
    for copy in copies:
        copy.wait()


def pick_of(owners, offers, interpret=False):
    _, rows, columns = offers.shape
    return pl.pallas_call(
        pick_kernel,
        in_specs=[pl.BlockSpec(memory_space=pltpu.SMEM), pl.BlockSpec(memory_space=pltpu.HBM)],
        out_specs=[pl.BlockSpec(memory_space=pltpu.VMEM)] * 2,
        out_shape=[jax.ShapeDtypeStruct((rows, columns), offers.dtype)] * 2,
        scratch_shapes=[pltpu.SemaphoreType.DMA((2,))],
        compiler_params=pltpu.CompilerParams(vmem_limit_bytes=58 * MIB),
        interpret=interpret,
        name="pick",
    )(owners, offers)


def join_kernel(axis, *refs):
    parts, out = refs[:-1], refs[-1]
    at = 0
    for part in parts:
        size = part.shape[axis]
        if axis == 0:
            out[at : at + size, :] = part[...]
        else:
            out[:, at : at + size] = part[...]
        at += size


def join_of(parts, axis, interpret=False):
    shape = list(parts[0].shape)
    shape[axis] = sum(p.shape[axis] for p in parts)
    return pl.pallas_call(
        functools.partial(join_kernel, axis),
        out_shape=jax.ShapeDtypeStruct(tuple(shape), parts[0].dtype),
        in_specs=[pl.BlockSpec(memory_space=pltpu.VMEM)] * len(parts),
        out_specs=pl.BlockSpec(memory_space=pltpu.VMEM),
        compiler_params=pltpu.CompilerParams(vmem_limit_bytes=8 * MIB),
        interpret=interpret,
        name="join",
    )(*parts)


def choose_matrix():
    chosen = np.zeros((2, 32, 3, 2, 2, 32), np.float32)
    for pair in range(2):
        for f1 in range(32):
            chosen[pair, f1, :, pair, :, f1] = 1.0
    return chosen.reshape(64, 384)


def products(core, part, spectra):
    half = part.shape[1] // 2
    near = pl.ds(pl.multiple_of(core * half, half), half)
    far = pl.ds(pl.multiple_of((1 - core) * half, half), half)
    left, right = part[:, :half], part[:, half:]
    return [
        jnp.dot(left, z[near, :], preferred_element_type=jnp.float32)
        + jnp.dot(right, z[far, :], preferred_element_type=jnp.float32)
        for z in spectra
    ]


def early_kernel(w0, w1, za, zb, out):
    core = lax.axis_index("grp") % 2
    wide = za.shape[1]
    for i, part in enumerate((w0, w1)):
        n = part.shape[0]
        first, second = products(core, part, (za, zb))
        out[i * n : (i + 1) * n, :wide] = first
        out[i * n : (i + 1) * n, wide:] = second


def early_of(w0, w1, spectra, interpret=False):
    return pl.pallas_call(
        early_kernel,
        out_shape=jax.ShapeDtypeStruct((2 * w0.shape[0], 768), jnp.float32),
        in_specs=[pl.BlockSpec(memory_space=pltpu.VMEM)] * 4,
        out_specs=pl.BlockSpec(memory_space=pltpu.VMEM),
        compiler_params=pltpu.CompilerParams(vmem_limit_bytes=24 * MIB),
        cost_estimate=pl.CostEstimate(flops=17 * 10**8, bytes_accessed=8 * 10**6, transcendentals=0),
        interpret=interpret,
        name="early",
    )(w0, w1, *spectra)


def beams_kernel(places, early, w2, w3, za, zb, choose, out, sums):
    for k in range(32):
        at = pl.multiple_of(places[k], 16)
        sums[pl.ds(at, 16), :] = early[k * 16 : (k + 1) * 16, :]
    core = lax.axis_index("grp") % 2
    wide = za.shape[1]
    for i, part in enumerate((w2, w3)):
        first, second = products(core, part, (za, zb))
        for k in range(16):
            at = pl.multiple_of(places[(i + 2) * 16 + k], 16)
            sums[pl.ds(at, 16), :wide] = first[k * 16 : (k + 1) * 16, :]
            sums[pl.ds(at, 16), wide:] = second[k * 16 : (k + 1) * 16, :]
    beams = sums.shape[0] // 2
    powers = []
    for g in range(3):
        re_lanes, im_lanes = slice(g * 256, g * 256 + 128), slice(g * 256 + 128, g * 256 + 256)
        re = sums[:beams, re_lanes] - sums[beams:, im_lanes]
        im = sums[beams:, re_lanes] + sums[:beams, im_lanes]
        powers.append(re * re + im * im)
    total = lax.dot_general(
        choose[...],
        jnp.concatenate(powers, axis=1),
        (((1,), (1,)), ((), ())),
        preferred_element_type=jnp.float32,
        precision=lax.Precision.HIGHEST,
    )
    out[...] = total * (1.0 / SPECTRA)


def beams_of(places, early, w2, w3, spectra, interpret=False):
    rows = early.shape[0] + 2 * w2.shape[0]
    return pl.pallas_call(
        beams_kernel,
        out_shape=jax.ShapeDtypeStruct((64, rows // 2), jnp.float32),
        in_specs=[pl.BlockSpec(memory_space=pltpu.SMEM)] + [pl.BlockSpec(memory_space=pltpu.VMEM)] * 6,
        out_specs=pl.BlockSpec(memory_space=pltpu.VMEM),
        scratch_shapes=[pltpu.VMEM((rows, 768), jnp.float32)],
        compiler_params=pltpu.CompilerParams(vmem_limit_bytes=32 * MIB),
        cost_estimate=pl.CostEstimate(flops=17 * 10**8, bytes_accessed=8 * 10**6, transcendentals=0),
        interpret=interpret,
        name="beams",
    )(places, early, w2, w3, *spectra, jnp.asarray(choose_matrix()))


def index_of(z, x, y, core):
    return ((y % 2) * 2 + core) * 32 + (z % 4) * 8 + (x % 4) * 2 + (y % 4) // 2


EVERY = [(z, x, y, c) for z in range(4) for x in range(4) for y in range(4) for c in range(2)]
ORDER = (("y", "x", "z"), ("z", "y", "x"))
SHIFTS = (0, -1, 1, 2)


def permutation(stage, shift):
    pairs = []
    for z, x, y, core in EVERY:
        axis = ORDER[core][stage]
        source = {"z": z, "x": x, "y": y}
        source[axis] += shift
        pairs.append((index_of(source["z"], source["x"], source["y"], core), index_of(z, x, y, core)))
    return pairs


def gather_stage(block, stage):
    return [block] + [lax.ppermute(block, ALL, permutation(stage, shift)) for shift in SHIFTS[1:]]


def block_places(grp, dev):
    core = grp % 2
    z, x, y = dev // 8, dev // 2 % 4, dev % 2 * 2 + grp // 2
    k = np.arange(64)
    shift = np.array(SHIFTS)
    first, second, third = shift[k % 4], shift[k // 4 % 4], shift[k // 16]
    by_core = []
    for order in ORDER:
        moved = dict(zip(order, (first, second, third)))
        by_core.append([moved[axis] for axis in "zxy"])
    is_first = core == 0
    mz, mx, my = [jnp.where(is_first, jnp.asarray(a), jnp.asarray(b)) for a, b in zip(*by_core)]
    fz, fx, fy = (z + mz + 4) % 4, (x + mx + 4) % 4, (y + my + 4) % 4
    return (((fy % 2) * 32 + fz * 8 + fx * 2 + fy // 2) * 16).astype(jnp.int32)


SWAP = [(0, 1), (1, 0), (2, 3), (3, 2)]


def on_device(voltage_real, voltage_imaginary, filter_taps, weights_re, weights_im, owners, antenna_map):
    grp, dev = lax.axis_index("grp"), lax.axis_index("dev")
    core = grp % 2

    quarter = quarter_of(weights_re[0], weights_im[0], antenna_map)
    offers = lax.all_to_all(quarter.reshape(32, 16, -1), "dev", split_axis=0, concat_axis=0, tiled=True)

    volts = (voltage_real, voltage_imaginary, filter_taps)
    quarter, *volts = lax.optimization_barrier((quarter, *volts))
    messages = spectra_of(MESSAGES, *volts)

    def turn(message):
        moved = lax.all_to_all(message, ALL, split_axis=0, concat_axis=0, tiled=True)
        return moved.reshape(DEVICES * SLOTS, -1)

    message, offers = lax.optimization_barrier((messages[0], offers))
    spectra = [turn(message)]
    mine, other = pick_of(owners, offers)
    other = lax.ppermute(other, "grp", SWAP)
    block = join_of([mine, other], 1)
    block = join_of(gather_stage(block, 0), 0)
    block, message, spectra[0] = lax.optimization_barrier((block, messages[1], spectra[0]))
    spectra.append(turn(message))
    block = join_of(gather_stage(block, 1), 0)
    parts = gather_stage(block, 2)

    early = early_of(parts[0], parts[3], spectra)
    places = block_places(grp, dev)
    places = jnp.concatenate([places[:16], places[48:], places[16:48]])
    power = beams_of(places, early, parts[1], parts[2], spectra)
    power = power.reshape(2, 32, -1)
    own = jnp.where(core == 0, power[0], power[1])
    given = jnp.where(core == 0, power[1], power[0])
    taken = lax.ppermute(given, "grp", SWAP)
    return jnp.where(core == 0, jnp.stack([own, taken]), jnp.stack([taken, own]))


def solution(mesh):
    return jax.shard_map(
        on_device,
        mesh=mesh,
        in_specs=(
            P(("grp", "dev"), None),
            P(("grp", "dev"), None),
            P(),
            P("dev", None, None),
            P("dev", None, None),
            P(),
            P(),
        ),
        out_specs=P(None, ("grp", "dev"), None),
        check_vma=False,
    )
```

```python
import functools
import math

import jax
import jax.numpy as jnp
import numpy as np
from jax import lax
from jax.experimental import pallas as pl
from jax.experimental.pallas import tpu as pltpu
from jax.sharding import PartitionSpec as P

CHANNELS = 4096
TAPS = 16
SPECTRA = 6
STEPS = 2
FRAMES = STEPS * SPECTRA
BLOCKS = FRAMES + TAPS - 1
OUTER = 32
INNER = 128
SLOTS = 16
DEVICES = 128
ROW_STRIDE = 24
GROUPS = ((0, 1, 6, 7), (2, 3, 8, 9), (4, 5, 10, 11))
MESSAGES = ((2,), (0, 1))
ALL = ("grp", "dev")
MIB = 1 << 20


def twist_tables():
    products = np.outer(np.arange(OUTER), np.arange(INNER)) % CHANNELS
    angles = products * (2.0 * math.pi / CHANNELS)
    return np.cos(angles).astype(np.float32), np.sin(angles).astype(np.float32)


def inner_matrix():
    products = np.outer(np.arange(INNER), np.arange(INNER)) % INNER
    angles = products * (2.0 * math.pi / INNER)
    norm = CHANNELS ** (-0.5)
    c, s = np.cos(angles) * norm, np.sin(angles) * norm
    return np.block([[c, s], [-s, c]]).astype(np.float32)


def small_fft(points):
    count = len(points)
    if count == 1:
        return points
    even = small_fft(points[0::2])
    odd = small_fft(points[1::2])
    half = count // 2
    result = [None] * count
    for k in range(half):
        er, ei = even[k]
        xr, xi = odd[k]
        if k == 0:
            tr, ti = xr, xi
        elif 4 * k == count:
            tr, ti = xi, -xr
        elif 8 * k == count:
            r = math.sqrt(0.5)
            tr, ti = (xr + xi) * r, (xi - xr) * r
        elif 8 * k == 3 * count:
            r = math.sqrt(0.5)
            tr, ti = (xi - xr) * r, (xr + xi) * (-r)
        else:
            c = math.cos(2.0 * math.pi * k / count)
            s = math.sin(2.0 * math.pi * k / count)
            tr, ti = xr * c + xi * s, xi * c - xr * s
        result[k] = (er + tr, ei + ti)
        result[k + half] = (er - tr, ei - ti)
    return result


def spectra_kernel(messages, *refs):
    groups = [group for message in messages for group in message]
    count = len(groups)
    sources, outs = refs[:6], refs[6 : 6 + len(messages)]
    vre, vim, taps, cos_t, sin_t, mat, frames, turned, packed, ready, sems = refs[6 + len(messages) :]
    chosen = [u for group in groups for u in GROUPS[group]]
    first, last = min(chosen), max(chosen) + TAPS
    rows_per_slot = 32 * len(chosen)
    slot_stride = rows_per_slot + 8

    loads = []
    for i in (2, 0, 1, 3, 4, 5):
        source = sources[i]
        if i < 2:
            source = source.at[:, first * CHANNELS : last * CHANNELS]
        loads.append(pltpu.make_async_copy(source, (vre, vim, taps, cos_t, sin_t, mat)[i], sems.at[i]))
        loads[-1].start()
    loads[0].wait()

    for c, volts in ((0, vre), (1, vim)):
        loads[1 + c].wait()

        def fir(n1, _, c=c, volts=volts):
            rows = [taps[k : k + 1, pl.ds(pl.multiple_of(n1 * INNER, INNER), INNER)] for k in range(TAPS)]
            needed = sorted({u + k for u in chosen for k in range(TAPS)})
            window = {
                b: volts[
                    :, pl.ds(pl.multiple_of((b - first) * CHANNELS + n1 * INNER, INNER), INNER)
                ].astype(jnp.float32)
                for b in needed
            }
            for i, u in enumerate(chosen):
                total = window[u] * rows[0]
                for k in range(1, TAPS):
                    total = total + window[u + k] * rows[k]
                frames[c, i, n1] = total
            return 0

        lax.fori_loop(0, OUTER, fir, 0)

    for load in loads[3:]:
        load.wait()

    def outer(i, _):
        u = i // 2
        low = pl.multiple_of((i % 2) * 8, 8)
        points = [
            (frames[0, u, n1, pl.ds(low, 8), :], frames[1, u, n1, pl.ds(low, 8), :]) for n1 in range(OUTER)
        ]
        points = small_fft(points)
        for f1 in range(OUTER):
            re, im = points[f1]
            if f1:
                c, d = cos_t[f1 : f1 + 1, :], sin_t[f1 : f1 + 1, :]
                re, im = re * c + im * d, im * c - re * d
            at = low * slot_stride + u * 32 + f1
            turned[0, pl.ds(at, 8, stride=slot_stride), :] = re
            turned[1, pl.ds(at, 8, stride=slot_stride), :] = im
        return 0

    lax.fori_loop(0, 2 * len(chosen), outer, 0)

    matrix = mat[...]
    lane = lax.broadcasted_iota(jnp.int32, (32, INNER), 1)

    def inner(a, _):
        base = pl.multiple_of(a * slot_stride, 8)
        rows = jnp.concatenate(
            [turned[0, pl.ds(base, rows_per_slot), :], turned[1, pl.ds(base, rows_per_slot), :]], axis=1
        ).astype(jnp.bfloat16)
        spec = lax.dot_general(
            matrix, rows, (((1,), (1,)), ((), ())), preferred_element_type=jnp.float32
        )
        for g in range(count):
            for y in range(2):
                for c in range(2):
                    to = [pl.ds((y * 2 + s) * 32 * ROW_STRIDE + a, 32, stride=ROW_STRIDE) for s in range(2)]
                    at = [c * 128 + (y * 2 + pair) * 32 for pair in range(2)]
                    mixed = [spec[f2 : f2 + 32, g * INNER : (g + 1) * INNER] for f2 in at]
                    packed[g * 2 + c, to[0], :] = jnp.where(lane < 64, mixed[0], pltpu.roll(mixed[1], 64, 1))
                    packed[g * 2 + c, to[1], :] = jnp.where(lane < 64, pltpu.roll(mixed[0], 64, 1), mixed[1])
        return 0

    lax.fori_loop(0, SLOTS, inner, 0, unroll=4)

    stores = []
    tile = 0
    for message, to in zip(messages, outs):
        for quarter in range(4):

            def emit(p, _, tile=tile, wide=2 * len(message)):
                for i in range(tile, tile + wide):
                    ready[p, :, i * INNER : (i + 1) * INNER] = packed[
                        i, pl.ds(pl.multiple_of(p * ROW_STRIDE, 8), SLOTS), :
                    ].astype(jnp.bfloat16)
                return 0

            lax.fori_loop(quarter * 32, quarter * 32 + 32, emit, 0, unroll=4)
            part = pl.ds(quarter * 32, 32)
            lanes = slice(tile * INNER, (tile + 2 * len(message)) * INNER)
            stores.append(
                pltpu.make_async_copy(ready.at[part, :, lanes], to.at[part], sems.at[6 + len(stores)])
            )
            stores[-1].start()
        tile += 2 * len(message)
    for store in stores:
        store.wait()


def spectra_of(messages, vre, vim, taps, interpret=False):
    cos_t, sin_t = twist_tables()
    mat = inner_matrix().astype(jnp.bfloat16)
    groups = [group for message in messages for group in message]
    count = len(groups)
    many = 4 * count
    chosen = [u for group in groups for u in GROUPS[group]]
    samples = (max(chosen) + TAPS - min(chosen)) * CHANNELS
    return pl.pallas_call(
        functools.partial(spectra_kernel, messages),
        out_shape=[jax.ShapeDtypeStruct((DEVICES, SLOTS, 2 * INNER * len(m)), jnp.bfloat16) for m in messages],
        in_specs=[pl.BlockSpec(memory_space=pltpu.HBM)] * 6,
        out_specs=[pl.BlockSpec(memory_space=pltpu.HBM)] * len(messages),
        scratch_shapes=[
            pltpu.VMEM((SLOTS, samples), jnp.bfloat16),
            pltpu.VMEM((SLOTS, samples), jnp.bfloat16),
            pltpu.VMEM((TAPS, CHANNELS), jnp.float32),
            pltpu.VMEM((OUTER, INNER), jnp.float32),
            pltpu.VMEM((OUTER, INNER), jnp.float32),
            pltpu.VMEM((256, 256), jnp.bfloat16),
            pltpu.VMEM((2, many, OUTER, SLOTS, INNER), jnp.float32),
            pltpu.VMEM((2, SLOTS * (32 * many + 8), INNER), jnp.float32),
            pltpu.VMEM((2 * count, DEVICES * ROW_STRIDE, INNER), jnp.float32),
            pltpu.VMEM((DEVICES, SLOTS, 2 * count * INNER), jnp.bfloat16),
            pltpu.SemaphoreType.DMA((6 + 4 * len(messages),)),
        ],
        compiler_params=pltpu.CompilerParams(vmem_limit_bytes=58 * MIB),
        cost_estimate=pl.CostEstimate(
            flops=8 * 10**8 * count, bytes_accessed=16 * 10**6 * count, transcendentals=0
        ),
        interpret=interpret,
        name="spectra",
    )(vre, vim, taps, jnp.asarray(cos_t), jnp.asarray(sin_t), jnp.asarray(mat))


SHIFTS = (0, -1, 1, 2)


def place():
    grp, dev = lax.axis_index("grp"), lax.axis_index("dev")
    return grp % 2, {"z": dev // 8, "x": dev // 2 % 4, "y": dev % 2 * 2 + grp // 2}


def quarter_kernel(wre, wim, slots, out0, out1, out2, out3, buf, names, chosen, turned, sems):
    grp = lax.axis_index("grp")
    y_lo, core = grp // 2, grp % 2
    antennas, beams = wre.shape
    half = antennas // 2
    name_copy = pltpu.make_async_copy(slots.at[core], names, sems.at[4])
    name_copy.start()
    for y, source in ((0, wre), (1, wim)):

        @pl.when(y_lo == y)
        def _():
            for i in range(4):
                part = pl.ds(i * half // 2, half // 2)
                pltpu.make_async_copy(source.at[part], buf.at[part], sems.at[i]).start()
    name_copy.wait()
    row = names[...]

    def build(i, _):
        antenna = lax.broadcasted_iota(jnp.int32, (16, half), 0) + i * 16
        chosen[pl.ds(pl.multiple_of(i * 16, 16), 16), :] = jnp.where(antenna == row, 1.0, 0.0).astype(jnp.bfloat16)
        return 0
    lax.fori_loop(0, antennas // 16, build, 0, unroll=4)
    for y, source in ((0, wre), (1, wim)):

        @pl.when(y_lo == y)
        def _():
            for i in range(4):
                part = pl.ds(i * half // 2, half // 2)
                pltpu.make_async_copy(source.at[part], buf.at[part], sems.at[i]).wait()
    for j in range(0, beams, 256):
        w = buf[:, j : j + 256].astype(jnp.bfloat16)
        for k in range(0, half, 512):
            turned[j : j + 256, k : k + 512] = lax.dot_general(
                w, chosen[:, k : k + 512], (((0,), (0,)), ((), ())), preferred_element_type=jnp.float32
            ).astype(jnp.bfloat16)
    quarter_finish(turned, (out0, out1, out2, out3))


def quarter_finish(turned, outs):
    core, coordinate = place()
    mine = jnp.where(core == 0, coordinate["z"], coordinate["x"])
    for shift, out in zip(SHIFTS, outs):
        block = (mine - shift + 4) % 4
        for j in range(4):
            at = jnp.where(core == 0, block * 128 + j * 32, j * 128 + block * 32)
            out[j * 32 : j * 32 + 32, :] = turned[pl.ds(pl.multiple_of(at, 32), 32), :]


def quarter_of(wre, wim, antenna_map, interpret=False):
    antennas, beams = wre.shape
    half = antennas // 2
    return pl.pallas_call(
        quarter_kernel,
        in_specs=[pl.BlockSpec(memory_space=pltpu.HBM)] * 3,
        out_specs=[pl.BlockSpec(memory_space=pltpu.VMEM)] * 4,
        out_shape=[jax.ShapeDtypeStruct((beams // 4, half), jnp.bfloat16)] * 4,
        scratch_shapes=[
            pltpu.VMEM((antennas, beams), jnp.float32),
            pltpu.VMEM((1, half), jnp.int32),
            pltpu.VMEM((antennas, half), jnp.bfloat16),
            pltpu.VMEM((beams, half), jnp.bfloat16),
            pltpu.SemaphoreType.DMA((5,)),
        ],
        compiler_params=pltpu.CompilerParams(vmem_limit_bytes=58 * MIB),
        cost_estimate=pl.CostEstimate(flops=2 * 10**9, bytes_accessed=6 * 10**6, transcendentals=0),
        interpret=interpret,
        name="quarter",
    )(wre, wim, antenna_map.reshape(2, 1, half))


def pick_kernel(kind, owners, *refs):
    inputs, outs = refs[:4], refs[4:]
    core, here = place()

    def copy_from(coordinate, position, copy):
        for shift, source in zip(SHIFTS, inputs):

            @pl.when((coordinate - position - shift + 8) % 4 == 0)
            def _():
                copy(source)

    for i in range(2):
        step = (core + i) % 2 if kind == "third" else i
        owner = owners[step]
        there = {"z": owner // 8, "x": owner // 2 % 4}
        if kind == "first":

            def copy(source):
                mine = jnp.where(core == 0, here["x"], here["z"])
                for shift, out in zip(SHIFTS, outs):
                    at = pl.multiple_of((mine - shift + 4) % 4 * 32, 32)
                    out[i * 32 : i * 32 + 32, :] = source[pl.ds(at, 32), :]

            copy_from(
                jnp.where(core == 0, there["z"], there["x"]), jnp.where(core == 0, here["z"], here["x"]), copy
            )
        elif kind == "second":

            def copy(source):
                outs[0][i * 32 : i * 32 + 32, :] = source[i * 32 : i * 32 + 32, :]

            copy_from(
                jnp.where(core == 0, there["x"], there["z"]), jnp.where(core == 0, here["x"], here["z"]), copy
            )
        else:
            for y_lo in range(2):

                def copy(source):
                    at = pl.multiple_of(step * 32, 32)
                    outs[i][y_lo * 32 : y_lo * 32 + 32, :] = source[pl.ds(at, 32), :]

                copy_from(owner % 2 * 2 + y_lo, here["y"], copy)


def pick_of(kind, owners, parts, interpret=False):
    columns = parts[0].shape[1]
    count = {"first": 4, "second": 1, "third": 2}[kind]
    return pl.pallas_call(
        functools.partial(pick_kernel, kind),
        in_specs=[pl.BlockSpec(memory_space=pltpu.SMEM)] + [pl.BlockSpec(memory_space=pltpu.VMEM)] * 4,
        out_specs=[pl.BlockSpec(memory_space=pltpu.VMEM)] * count,
        out_shape=[jax.ShapeDtypeStruct((64, columns), parts[0].dtype)] * count,
        compiler_params=pltpu.CompilerParams(vmem_limit_bytes=8 * MIB),
        interpret=interpret,
        name="pick_" + kind,
    )(owners, *parts)


def join_kernel(axis, *refs):
    parts, out = refs[:-1], refs[-1]
    at = 0
    for part in parts:
        size = part.shape[axis]
        if axis == 0:
            out[at : at + size, :] = part[...]
        else:
            out[:, at : at + size] = part[...]
        at += size


def join_of(parts, axis, interpret=False):
    shape = list(parts[0].shape)
    shape[axis] = sum(p.shape[axis] for p in parts)
    return pl.pallas_call(
        functools.partial(join_kernel, axis),
        out_shape=jax.ShapeDtypeStruct(tuple(shape), parts[0].dtype),
        in_specs=[pl.BlockSpec(memory_space=pltpu.VMEM)] * len(parts),
        out_specs=pl.BlockSpec(memory_space=pltpu.VMEM),
        compiler_params=pltpu.CompilerParams(vmem_limit_bytes=8 * MIB),
        interpret=interpret,
        name="join",
    )(*parts)


def choose_matrix():
    chosen = np.zeros((2, 32, 3, 2, 2, 32), np.float32)
    for pair in range(2):
        for f1 in range(32):
            chosen[pair, f1, :, pair, :, f1] = 1.0
    return chosen.reshape(64, 384)


def products(core, part, spectra):
    half = part.shape[1] // 2
    near = pl.ds(pl.multiple_of(core * half, half), half)
    far = pl.ds(pl.multiple_of((1 - core) * half, half), half)
    left, right = part[:, :half], part[:, half:]
    return [
        jnp.dot(left, z[near, :], preferred_element_type=jnp.float32)
        + jnp.dot(right, z[far, :], preferred_element_type=jnp.float32)
        for z in spectra
    ]


def early_kernel(w0, w1, za, zb, out):
    core = lax.axis_index("grp") % 2
    wide = za.shape[1]
    for i, part in enumerate((w0, w1)):
        n = part.shape[0]
        first, second = products(core, part, (za, zb))
        out[i * n : (i + 1) * n, :wide] = first
        out[i * n : (i + 1) * n, wide:] = second


def early_of(w0, w1, spectra, interpret=False):
    return pl.pallas_call(
        early_kernel,
        out_shape=jax.ShapeDtypeStruct((2 * w0.shape[0], 768), jnp.float32),
        in_specs=[pl.BlockSpec(memory_space=pltpu.VMEM)] * 4,
        out_specs=pl.BlockSpec(memory_space=pltpu.VMEM),
        compiler_params=pltpu.CompilerParams(vmem_limit_bytes=24 * MIB),
        cost_estimate=pl.CostEstimate(flops=17 * 10**8, bytes_accessed=8 * 10**6, transcendentals=0),
        interpret=interpret,
        name="early",
    )(w0, w1, *spectra)


def beams_kernel(early, w2, w3, za, zb, choose, out, sums):
    core, here = place()
    wide = za.shape[1]

    def row_of(part, k):
        first, y_lo = SHIFTS[k // 2], k % 2
        second = SHIFTS[part]
        z = (here["z"] + jnp.where(core == 0, second, first) + 4) % 4
        x = (here["x"] + jnp.where(core == 0, first, second) + 4) % 4
        return pl.ds(pl.multiple_of(y_lo * 512 + z * 128 + x * 32, 32), 32)

    for part in range(2):
        for k in range(8):
            sums[row_of(part, k), :] = early[part * 256 + k * 32 : part * 256 + (k + 1) * 32, :]
    for part, w in ((2, w2), (3, w3)):
        first, second = products(core, w, (za, zb))
        for k in range(8):
            sums[row_of(part, k), :wide] = first[k * 32 : (k + 1) * 32, :]
            sums[row_of(part, k), wide:] = second[k * 32 : (k + 1) * 32, :]
    beams = sums.shape[0] // 2
    powers = []
    for g in range(3):
        re_lanes, im_lanes = slice(g * 256, g * 256 + 128), slice(g * 256 + 128, g * 256 + 256)
        re = sums[:beams, re_lanes] - sums[beams:, im_lanes]
        im = sums[beams:, re_lanes] + sums[:beams, im_lanes]
        powers.append(re * re + im * im)
    total = lax.dot_general(
        choose[...],
        jnp.concatenate(powers, axis=1),
        (((1,), (1,)), ((), ())),
        preferred_element_type=jnp.float32,
        precision=lax.Precision.HIGHEST,
    )
    out[...] = total * (1.0 / SPECTRA)


def beams_of(early, w2, w3, spectra, interpret=False):
    rows = early.shape[0] + 2 * w2.shape[0]
    return pl.pallas_call(
        beams_kernel,
        out_shape=jax.ShapeDtypeStruct((64, rows // 2), jnp.float32),
        in_specs=[pl.BlockSpec(memory_space=pltpu.VMEM)] * 6,
        out_specs=pl.BlockSpec(memory_space=pltpu.VMEM),
        scratch_shapes=[pltpu.VMEM((rows, 768), jnp.float32)],
        compiler_params=pltpu.CompilerParams(vmem_limit_bytes=32 * MIB),
        cost_estimate=pl.CostEstimate(flops=17 * 10**8, bytes_accessed=8 * 10**6, transcendentals=0),
        interpret=interpret,
        name="beams",
    )(early, w2, w3, *spectra, jnp.asarray(choose_matrix()))


def index_of(z, x, y, core):
    return ((y % 2) * 2 + core) * 32 + (z % 4) * 8 + (x % 4) * 2 + (y % 4) // 2


EVERY = [(z, x, y, c) for z in range(4) for x in range(4) for y in range(4) for c in range(2)]
AXES = (("z", "x", "y", "x", "z"), ("x", "z", "y", "z", "x"))


def permutation(stage, shift):
    pairs = []
    for z, x, y, core in EVERY:
        axis = AXES[core][stage]
        source = {"z": z, "x": x, "y": y}
        source[axis] += shift
        pairs.append((index_of(source["z"], source["x"], source["y"], core), index_of(z, x, y, core)))
    return pairs


def exchange(blocks, stage):
    return [blocks[0]] + [
        lax.ppermute(block, ALL, permutation(stage, shift)) for block, shift in zip(blocks[1:], SHIFTS[1:])
    ]


SWAP = [(0, 1), (1, 0), (2, 3), (3, 2)]


def on_device(voltage_real, voltage_imaginary, filter_taps, weights_re, weights_im, owners, antenna_map):
    core = lax.axis_index("grp") % 2
    tie = lax.optimization_barrier

    def turn(message):
        moved = lax.all_to_all(message, ALL, split_axis=0, concat_axis=0, tiled=True)
        return moved.reshape(DEVICES * SLOTS, -1)

    volts = (voltage_real, voltage_imaginary, filter_taps)
    blocks = quarter_of(weights_re[0], weights_im[0], antenna_map)
    blocks, volts = tie((blocks, volts))
    blocks = exchange(blocks, 0)
    (late,) = spectra_of(((2,),), *volts)
    blocks, late, volts = tie((blocks, late, volts))
    blocks = pick_of("first", owners, blocks)
    blocks, late, volts = tie((blocks, late, volts))
    blocks = exchange(blocks, 1)
    late = turn(late)
    (soon,) = spectra_of(((0, 1),), *volts)
    blocks, soon, late = tie((blocks, soon, late))
    (block,) = pick_of("second", owners, blocks)
    blocks = exchange([block] * 4, 2)
    blocks, soon = tie((blocks, soon))
    soon = turn(soon)
    mine, other = pick_of("third", owners, blocks)
    other = lax.ppermute(other, "grp", SWAP)
    block = join_of([mine, other], 1)
    block = join_of(exchange([block] * 4, 3), 0)
    block, soon = tie((block, soon))
    parts = exchange([block] * 4, 4)

    spectra = (soon, late)
    early = early_of(parts[0], parts[1], spectra)
    power = beams_of(early, parts[2], parts[3], spectra)
    power = power.reshape(2, 32, -1)
    own = jnp.where(core == 0, power[0], power[1])
    given = jnp.where(core == 0, power[1], power[0])
    taken = lax.ppermute(given, "grp", SWAP)
    return jnp.where(core == 0, jnp.stack([own, taken]), jnp.stack([taken, own]))


def solution(mesh):
    return jax.shard_map(
        on_device,
        mesh=mesh,
        in_specs=(
            P(("grp", "dev"), None),
            P(("grp", "dev"), None),
            P(),
            P("dev", None, None),
            P("dev", None, None),
            P(),
            P(),
        ),
        out_specs=P(None, ("grp", "dev"), None),
        check_vma=False,
    )
```

```python
import functools
import math

import jax
import jax.numpy as jnp
import numpy as np
from jax import lax
from jax.experimental import pallas as pl
from jax.experimental.pallas import tpu as pltpu
from jax.sharding import PartitionSpec as P

CHANNELS = 4096
TAPS = 16
SPECTRA = 6
STEPS = 2
FRAMES = STEPS * SPECTRA
BLOCKS = FRAMES + TAPS - 1
OUTER = 32
INNER = 128
SLOTS = 16
DEVICES = 128
ROW_STRIDE = 24
GROUPS = ((0, 1, 6, 7), (2, 3, 8, 9), (4, 5, 10, 11))
MESSAGES = ((2,), (0, 1))
ALL = ("grp", "dev")
MIB = 1 << 20


def twist_tables():
    products = np.outer(np.arange(OUTER), np.arange(INNER)) % CHANNELS
    angles = products * (2.0 * math.pi / CHANNELS)
    return np.cos(angles).astype(np.float32), np.sin(angles).astype(np.float32)


def inner_matrix():
    products = np.outer(np.arange(INNER), np.arange(INNER)) % INNER
    angles = products * (2.0 * math.pi / INNER)
    norm = CHANNELS ** (-0.5)
    c, s = np.cos(angles) * norm, np.sin(angles) * norm
    return np.block([[c, s], [-s, c]]).astype(np.float32)


def small_fft(points):
    count = len(points)
    if count == 1:
        return points
    even = small_fft(points[0::2])
    odd = small_fft(points[1::2])
    half = count // 2
    result = [None] * count
    for k in range(half):
        er, ei = even[k]
        xr, xi = odd[k]
        if k == 0:
            tr, ti = xr, xi
        elif 4 * k == count:
            tr, ti = xi, -xr
        elif 8 * k == count:
            r = math.sqrt(0.5)
            tr, ti = (xr + xi) * r, (xi - xr) * r
        elif 8 * k == 3 * count:
            r = math.sqrt(0.5)
            tr, ti = (xi - xr) * r, (xr + xi) * (-r)
        else:
            c = math.cos(2.0 * math.pi * k / count)
            s = math.sin(2.0 * math.pi * k / count)
            tr, ti = xr * c + xi * s, xi * c - xr * s
        result[k] = (er + tr, ei + ti)
        result[k + half] = (er - tr, ei - ti)
    return result


def spectra_kernel(messages, *refs):
    groups = [group for message in messages for group in message]
    count = len(groups)
    sources, outs = refs[:6], refs[6 : 6 + len(messages)]
    vre, vim, taps, cos_t, sin_t, mat, frames, turned, packed, ready, sems = refs[6 + len(messages) :]
    chosen = [u for group in groups for u in GROUPS[group]]
    first, last = min(chosen), max(chosen) + TAPS
    rows_per_slot = 32 * len(chosen)
    slot_stride = rows_per_slot + 8

    loads = []
    for i in (2, 0, 1, 3, 4, 5):
        source = sources[i]
        if i < 2:
            source = source.at[:, first * CHANNELS : last * CHANNELS]
        loads.append(pltpu.make_async_copy(source, (vre, vim, taps, cos_t, sin_t, mat)[i], sems.at[i]))
        loads[-1].start()
    loads[0].wait()

    for c, volts in ((0, vre), (1, vim)):
        loads[1 + c].wait()

        def fir(n1, _, c=c, volts=volts):
            rows = [taps[k : k + 1, pl.ds(pl.multiple_of(n1 * INNER, INNER), INNER)] for k in range(TAPS)]
            needed = sorted({u + k for u in chosen for k in range(TAPS)})
            window = {
                b: volts[
                    :, pl.ds(pl.multiple_of((b - first) * CHANNELS + n1 * INNER, INNER), INNER)
                ].astype(jnp.float32)
                for b in needed
            }
            for i, u in enumerate(chosen):
                total = window[u] * rows[0]
                for k in range(1, TAPS):
                    total = total + window[u + k] * rows[k]
                frames[c, i, n1] = total
            return 0

        lax.fori_loop(0, OUTER, fir, 0)

    for load in loads[3:]:
        load.wait()

    def outer(i, _):
        u = i // 2
        low = pl.multiple_of((i % 2) * 8, 8)
        points = [
            (frames[0, u, n1, pl.ds(low, 8), :], frames[1, u, n1, pl.ds(low, 8), :]) for n1 in range(OUTER)
        ]
        points = small_fft(points)
        for f1 in range(OUTER):
            re, im = points[f1]
            if f1:
                c, d = cos_t[f1 : f1 + 1, :], sin_t[f1 : f1 + 1, :]
                re, im = re * c + im * d, im * c - re * d
            at = low * slot_stride + u * 32 + f1
            turned[0, pl.ds(at, 8, stride=slot_stride), :] = re
            turned[1, pl.ds(at, 8, stride=slot_stride), :] = im
        return 0

    lax.fori_loop(0, 2 * len(chosen), outer, 0)

    matrix = mat[...]
    lane = lax.broadcasted_iota(jnp.int32, (32, INNER), 1)

    def inner(a, _):
        base = pl.multiple_of(a * slot_stride, 8)
        rows = jnp.concatenate(
            [turned[0, pl.ds(base, rows_per_slot), :], turned[1, pl.ds(base, rows_per_slot), :]], axis=1
        ).astype(jnp.bfloat16)
        spec = lax.dot_general(
            matrix, rows, (((1,), (1,)), ((), ())), preferred_element_type=jnp.float32
        )
        for g in range(count):
            for y in range(2):
                for c in range(2):
                    to = [pl.ds((y * 2 + s) * 32 * ROW_STRIDE + a, 32, stride=ROW_STRIDE) for s in range(2)]
                    at = [c * 128 + (y * 2 + pair) * 32 for pair in range(2)]
                    mixed = [spec[f2 : f2 + 32, g * INNER : (g + 1) * INNER] for f2 in at]
                    packed[g * 2 + c, to[0], :] = jnp.where(lane < 64, mixed[0], pltpu.roll(mixed[1], 64, 1))
                    packed[g * 2 + c, to[1], :] = jnp.where(lane < 64, pltpu.roll(mixed[0], 64, 1), mixed[1])
        return 0

    lax.fori_loop(0, SLOTS, inner, 0, unroll=4)

    stores = []
    tile = 0
    for message, to in zip(messages, outs):
        for quarter in range(4):

            def emit(p, _, tile=tile, wide=2 * len(message)):
                for i in range(tile, tile + wide):
                    ready[p, :, i * INNER : (i + 1) * INNER] = packed[
                        i, pl.ds(pl.multiple_of(p * ROW_STRIDE, 8), SLOTS), :
                    ].astype(jnp.bfloat16)
                return 0

            lax.fori_loop(quarter * 32, quarter * 32 + 32, emit, 0, unroll=4)
            part = pl.ds(quarter * 32, 32)
            lanes = slice(tile * INNER, (tile + 2 * len(message)) * INNER)
            stores.append(
                pltpu.make_async_copy(ready.at[part, :, lanes], to.at[part], sems.at[6 + len(stores)])
            )
            stores[-1].start()
        tile += 2 * len(message)
    for store in stores:
        store.wait()


def spectra_of(messages, vre, vim, taps, interpret=False):
    cos_t, sin_t = twist_tables()
    mat = inner_matrix().astype(jnp.bfloat16)
    groups = [group for message in messages for group in message]
    count = len(groups)
    many = 4 * count
    chosen = [u for group in groups for u in GROUPS[group]]
    samples = (max(chosen) + TAPS - min(chosen)) * CHANNELS
    return pl.pallas_call(
        functools.partial(spectra_kernel, messages),
        out_shape=[jax.ShapeDtypeStruct((DEVICES, SLOTS, 2 * INNER * len(m)), jnp.bfloat16) for m in messages],
        in_specs=[pl.BlockSpec(memory_space=pltpu.HBM)] * 6,
        out_specs=[pl.BlockSpec(memory_space=pltpu.HBM)] * len(messages),
        scratch_shapes=[
            pltpu.VMEM((SLOTS, samples), jnp.bfloat16),
            pltpu.VMEM((SLOTS, samples), jnp.bfloat16),
            pltpu.VMEM((TAPS, CHANNELS), jnp.float32),
            pltpu.VMEM((OUTER, INNER), jnp.float32),
            pltpu.VMEM((OUTER, INNER), jnp.float32),
            pltpu.VMEM((256, 256), jnp.bfloat16),
            pltpu.VMEM((2, many, OUTER, SLOTS, INNER), jnp.float32),
            pltpu.VMEM((2, SLOTS * (32 * many + 8), INNER), jnp.float32),
            pltpu.VMEM((2 * count, DEVICES * ROW_STRIDE, INNER), jnp.float32),
            pltpu.VMEM((DEVICES, SLOTS, 2 * count * INNER), jnp.bfloat16),
            pltpu.SemaphoreType.DMA((6 + 4 * len(messages),)),
        ],
        compiler_params=pltpu.CompilerParams(vmem_limit_bytes=58 * MIB),
        cost_estimate=pl.CostEstimate(
            flops=8 * 10**8 * count, bytes_accessed=16 * 10**6 * count, transcendentals=0
        ),
        interpret=interpret,
        name="spectra",
    )(vre, vim, taps, jnp.asarray(cos_t), jnp.asarray(sin_t), jnp.asarray(mat))


SHIFTS = (0, -1, 1, 2)


def place():
    grp, dev = lax.axis_index("grp"), lax.axis_index("dev")
    return grp % 2, {"z": dev // 8, "x": dev // 2 % 4, "y": dev % 2 * 2 + grp // 2}


def quarter_kernel(wre, wim, slots, out0, out1, out2, out3, buf, names, chosen, turned, sems):
    grp = lax.axis_index("grp")
    y_lo, core = grp // 2, grp % 2
    antennas, beams = wre.shape
    half = antennas // 2
    name_copy = pltpu.make_async_copy(slots.at[core], names, sems.at[4])
    name_copy.start()
    for y, source in ((0, wre), (1, wim)):

        @pl.when(y_lo == y)
        def _():
            for i in range(4):
                part = pl.ds(i * half // 2, half // 2)
                pltpu.make_async_copy(source.at[part], buf.at[part], sems.at[i]).start()
    name_copy.wait()
    row = names[...]

    def build(i, _):
        antenna = lax.broadcasted_iota(jnp.int32, (16, half), 0) + i * 16
        chosen[pl.ds(pl.multiple_of(i * 16, 16), 16), :] = jnp.where(antenna == row, 1.0, 0.0).astype(jnp.bfloat16)
        return 0
    lax.fori_loop(0, antennas // 16, build, 0, unroll=4)
    for y, source in ((0, wre), (1, wim)):

        @pl.when(y_lo == y)
        def _():
            for i in range(4):
                part = pl.ds(i * half // 2, half // 2)
                pltpu.make_async_copy(source.at[part], buf.at[part], sems.at[i]).wait()
    for j in range(0, beams, 256):
        w = buf[:, j : j + 256].astype(jnp.bfloat16)
        for k in range(0, half, 512):
            turned[j : j + 256, k : k + 512] = lax.dot_general(
                w, chosen[:, k : k + 512], (((0,), (0,)), ((), ())), preferred_element_type=jnp.float32
            ).astype(jnp.bfloat16)
    quarter_finish(turned, (out0, out1, out2, out3))


def quarter_finish(turned, outs):
    core, coordinate = place()
    mine = jnp.where(core == 0, coordinate["z"], coordinate["x"])
    for shift, out in zip(SHIFTS, outs):
        block = (mine - shift + 4) % 4
        for j in range(4):
            at = jnp.where(core == 0, block * 128 + j * 32, j * 128 + block * 32)
            out[j * 32 : j * 32 + 32, :] = turned[pl.ds(pl.multiple_of(at, 32), 32), :]


def quarter_of(wre, wim, antenna_map, interpret=False):
    antennas, beams = wre.shape
    half = antennas // 2
    return pl.pallas_call(
        quarter_kernel,
        in_specs=[pl.BlockSpec(memory_space=pltpu.HBM)] * 3,
        out_specs=[pl.BlockSpec(memory_space=pltpu.VMEM)] * 4,
        out_shape=[jax.ShapeDtypeStruct((beams // 4, half), jnp.bfloat16)] * 4,
        scratch_shapes=[
            pltpu.VMEM((antennas, beams), jnp.float32),
            pltpu.VMEM((1, half), jnp.int32),
            pltpu.VMEM((antennas, half), jnp.bfloat16),
            pltpu.VMEM((beams, half), jnp.bfloat16),
            pltpu.SemaphoreType.DMA((5,)),
        ],
        compiler_params=pltpu.CompilerParams(vmem_limit_bytes=58 * MIB),
        cost_estimate=pl.CostEstimate(flops=2 * 10**9, bytes_accessed=6 * 10**6, transcendentals=0),
        interpret=interpret,
        name="quarter",
    )(wre, wim, antenna_map.reshape(2, 1, half))


def pick_kernel(kind, owners, *refs):
    inputs, outs = refs[:4], refs[4:]
    core, here = place()

    def copy_from(coordinate, position, copy):
        for shift, source in zip(SHIFTS, inputs):

            @pl.when((coordinate - position - shift + 8) % 4 == 0)
            def _():
                copy(source)

    for i in range(2):
        step = (core + i) % 2 if kind == "third" else i
        owner = owners[step]
        there = {"z": owner // 8, "x": owner // 2 % 4}
        if kind == "first":

            def copy(source):
                mine = jnp.where(core == 0, here["x"], here["z"])
                for shift, out in zip(SHIFTS, outs):
                    at = pl.multiple_of((mine - shift + 4) % 4 * 32, 32)
                    out[i * 32 : i * 32 + 32, :] = source[pl.ds(at, 32), :]

            copy_from(
                jnp.where(core == 0, there["z"], there["x"]), jnp.where(core == 0, here["z"], here["x"]), copy
            )
        elif kind == "second":

            def copy(source):
                outs[0][i * 32 : i * 32 + 32, :] = source[i * 32 : i * 32 + 32, :]

            copy_from(
                jnp.where(core == 0, there["x"], there["z"]), jnp.where(core == 0, here["x"], here["z"]), copy
            )
        else:
            for y_lo in range(2):

                def copy(source):
                    at = pl.multiple_of(step * 32, 32)
                    outs[i][y_lo * 32 : y_lo * 32 + 32, :] = source[pl.ds(at, 32), :]

                copy_from(owner % 2 * 2 + y_lo, here["y"], copy)


def pick_of(kind, owners, parts, interpret=False):
    columns = parts[0].shape[1]
    count = {"first": 4, "second": 1, "third": 2}[kind]
    return pl.pallas_call(
        functools.partial(pick_kernel, kind),
        in_specs=[pl.BlockSpec(memory_space=pltpu.SMEM)] + [pl.BlockSpec(memory_space=pltpu.VMEM)] * 4,
        out_specs=[pl.BlockSpec(memory_space=pltpu.VMEM)] * count,
        out_shape=[jax.ShapeDtypeStruct((64, columns), parts[0].dtype)] * count,
        compiler_params=pltpu.CompilerParams(vmem_limit_bytes=8 * MIB),
        interpret=interpret,
        name="pick_" + kind,
    )(owners, *parts)


def join_kernel(axis, *refs):
    parts, out = refs[:-1], refs[-1]
    at = 0
    for part in parts:
        size = part.shape[axis]
        if axis == 0:
            out[at : at + size, :] = part[...]
        else:
            out[:, at : at + size] = part[...]
        at += size


def join_of(parts, axis, interpret=False):
    shape = list(parts[0].shape)
    shape[axis] = sum(p.shape[axis] for p in parts)
    return pl.pallas_call(
        functools.partial(join_kernel, axis),
        out_shape=jax.ShapeDtypeStruct(tuple(shape), parts[0].dtype),
        in_specs=[pl.BlockSpec(memory_space=pltpu.VMEM)] * len(parts),
        out_specs=pl.BlockSpec(memory_space=pltpu.VMEM),
        compiler_params=pltpu.CompilerParams(vmem_limit_bytes=8 * MIB),
        interpret=interpret,
        name="join",
    )(*parts)


def choose_matrix():
    chosen = np.zeros((2, 32, 3, 2, 2, 32), np.float32)
    for pair in range(2):
        for f1 in range(32):
            chosen[pair, f1, :, pair, :, f1] = 1.0
    return chosen.reshape(64, 384)


def products(core, part, spectra):
    half = part.shape[1] // 2
    near = pl.ds(pl.multiple_of(core * half, half), half)
    far = pl.ds(pl.multiple_of((1 - core) * half, half), half)
    left, right = part[:, :half], part[:, half:]
    return [
        jnp.dot(left, z[near, :], preferred_element_type=jnp.float32)
        + jnp.dot(right, z[far, :], preferred_element_type=jnp.float32)
        for z in spectra
    ]


def early_kernel(*refs):
    *weights, za, zb, zc, out = refs
    core, _ = place()
    rows = jnp.concatenate([w[...] for w in weights], axis=0)
    for g, result in enumerate(products(core, rows, (za, zb, zc))):
        out[:, g * 256 : (g + 1) * 256] = result


def early_of(weights, spectra, interpret=False):
    rows = sum(w.shape[0] for w in weights)
    return pl.pallas_call(
        early_kernel,
        out_shape=jax.ShapeDtypeStruct((rows, 768), jnp.float32),
        in_specs=[pl.BlockSpec(memory_space=pltpu.VMEM)] * 7,
        out_specs=pl.BlockSpec(memory_space=pltpu.VMEM),
        compiler_params=pltpu.CompilerParams(vmem_limit_bytes=28 * MIB),
        cost_estimate=pl.CostEstimate(flops=17 * 10**8, bytes_accessed=8 * 10**6, transcendentals=0),
        interpret=interpret,
        name="early",
    )(*weights, *spectra)


def beams_kernel(early, *refs):
    *weights, za, zb, zc, choose, own, given, sums = refs
    core, here = place()

    def row_of(part, k):
        first, y_lo = SHIFTS[k // 2], k % 2
        second = SHIFTS[part]
        z = (here["z"] + jnp.where(core == 0, second, first) + 4) % 4
        x = (here["x"] + jnp.where(core == 0, first, second) + 4) % 4
        return pl.ds(pl.multiple_of(y_lo * 512 + z * 128 + x * 32, 32), 32)

    for k in range(16):
        sums[row_of(k // 8, k % 8), :] = early[k * 32 : (k + 1) * 32, :]
    rows = jnp.concatenate([w[...] for w in weights], axis=0)
    for g, result in enumerate(products(core, rows, (za, zb, zc))):
        for k in range(16):
            sums[row_of(2 + k // 8, k % 8), g * 256 : (g + 1) * 256] = result[k * 32 : (k + 1) * 32, :]
    beams = sums.shape[0] // 2
    powers = []
    for g in range(3):
        re_lanes, im_lanes = slice(g * 256, g * 256 + 128), slice(g * 256 + 128, g * 256 + 256)
        re = sums[:beams, re_lanes] - sums[beams:, im_lanes]
        im = sums[beams:, re_lanes] + sums[:beams, im_lanes]
        powers.append(re * re + im * im)
    total = lax.dot_general(
        choose[...],
        jnp.concatenate(powers, axis=1),
        (((1,), (1,)), ((), ())),
        preferred_element_type=jnp.float32,
        precision=lax.Precision.HIGHEST,
    ) * (1.0 / SPECTRA)
    own[...] = jnp.where(core == 0, total[:32], total[32:])
    given[...] = jnp.where(core == 0, total[32:], total[:32])


def beams_of(early, weights, spectra, interpret=False):
    beams = early.shape[0]
    return pl.pallas_call(
        beams_kernel,
        out_shape=[jax.ShapeDtypeStruct((32, beams), jnp.float32)] * 2,
        in_specs=[pl.BlockSpec(memory_space=pltpu.VMEM)] * 9,
        out_specs=[pl.BlockSpec(memory_space=pltpu.VMEM)] * 2,
        scratch_shapes=[pltpu.VMEM((2 * beams, 768), jnp.float32)],
        compiler_params=pltpu.CompilerParams(vmem_limit_bytes=28 * MIB),
        cost_estimate=pl.CostEstimate(flops=17 * 10**8, bytes_accessed=8 * 10**6, transcendentals=0),
        interpret=interpret,
        name="beams",
    )(early, *weights, *spectra, jnp.asarray(choose_matrix()))


def index_of(z, x, y, core):
    return ((y % 2) * 2 + core) * 32 + (z % 4) * 8 + (x % 4) * 2 + (y % 4) // 2


EVERY = [(z, x, y, c) for z in range(4) for x in range(4) for y in range(4) for c in range(2)]
AXES = (("z", "x", "y", "x", "z"), ("x", "z", "y", "z", "x"))


def permutation(stage, shift):
    pairs = []
    for z, x, y, core in EVERY:
        axis = AXES[core][stage]
        source = {"z": z, "x": x, "y": y}
        source[axis] += shift
        pairs.append((index_of(source["z"], source["x"], source["y"], core), index_of(z, x, y, core)))
    return pairs


def exchange(blocks, stage):
    return [blocks[0]] + [
        lax.ppermute(block, ALL, permutation(stage, shift)) for block, shift in zip(blocks[1:], SHIFTS[1:])
    ]


SWAP = [(0, 1), (1, 0), (2, 3), (3, 2)]


def on_device(voltage_real, voltage_imaginary, filter_taps, weights_re, weights_im, owners, antenna_map):
    core = lax.axis_index("grp") % 2
    tie = lax.optimization_barrier

    def turn(message):
        moved = lax.all_to_all(message, ALL, split_axis=0, concat_axis=0, tiled=True)
        return moved.reshape(DEVICES * SLOTS, -1)

    volts = (voltage_real, voltage_imaginary, filter_taps)
    blocks = quarter_of(weights_re[0], weights_im[0], antenna_map)
    blocks, volts = tie((blocks, volts))
    blocks = exchange(blocks, 0)
    (late,) = spectra_of(((2,),), *volts)
    blocks, late, volts = tie((blocks, late, volts))
    blocks = pick_of("first", owners, blocks)
    blocks, late, volts = tie((blocks, late, volts))
    blocks = exchange(blocks, 1)
    late = turn(late)
    soon, last = spectra_of(((0,), (1,)), *volts)
    blocks, soon, last, late = tie((blocks, soon, last, late))
    (block,) = pick_of("second", owners, blocks)
    block, soon = tie((block, soon))
    soon = turn(soon)
    blocks = exchange([block] * 4, 2)
    mine, other = pick_of("third", owners, blocks)
    other = lax.ppermute(other, "grp", SWAP)
    block = join_of([mine, other], 1)
    near = exchange([block] * 4, 3)
    first = exchange([block] * 4, 4)
    block = join_of(near[1:], 0)
    block, first, last, soon = tie((block, first, last, soon))
    last = turn(last)
    second = exchange([block] * 4, 4)

    spectra = (soon, last, late)
    early = early_of([first[0], second[0], first[1], second[1]], spectra)
    own, given = beams_of(early, [first[2], second[2], first[3], second[3]], spectra)
    taken = lax.ppermute(given, "grp", SWAP)
    return jnp.where(core == 0, jnp.stack([own, taken]), jnp.stack([taken, own]))


def solution(mesh):
    return jax.shard_map(
        on_device,
        mesh=mesh,
        in_specs=(
            P(("grp", "dev"), None),
            P(("grp", "dev"), None),
            P(),
            P("dev", None, None),
            P("dev", None, None),
            P(),
            P(),
        ),
        out_specs=P(None, ("grp", "dev"), None),
        check_vma=False,
    )
```

```python
import functools
import math

import jax
import jax.numpy as jnp
import numpy as np
from jax import lax
from jax.experimental import pallas as pl
from jax.experimental.pallas import tpu as pltpu
from jax.sharding import PartitionSpec as P

CHANNELS = 4096
TAPS = 16
SPECTRA = 6
STEPS = 2
FRAMES = STEPS * SPECTRA
BLOCKS = FRAMES + TAPS - 1
OUTER = 32
INNER = 128
SLOTS = 16
DEVICES = 128
ROW_STRIDE = 24
GROUPS = ((0, 1, 6, 7), (2, 3, 8, 9), (4, 5, 10, 11))
MESSAGES = ((2,), (0, 1))
ALL = ("grp", "dev")
MIB = 1 << 20


def twist_tables():
    products = np.outer(np.arange(OUTER), np.arange(INNER)) % CHANNELS
    angles = products * (2.0 * math.pi / CHANNELS)
    return np.cos(angles).astype(np.float32), np.sin(angles).astype(np.float32)


def inner_matrix():
    products = np.outer(np.arange(INNER), np.arange(INNER)) % INNER
    angles = products * (2.0 * math.pi / INNER)
    norm = CHANNELS ** (-0.5)
    c, s = np.cos(angles) * norm, np.sin(angles) * norm
    return np.block([[c, s], [-s, c]]).astype(np.float32)


def small_fft(points):
    count = len(points)
    if count == 1:
        return points
    even = small_fft(points[0::2])
    odd = small_fft(points[1::2])
    half = count // 2
    result = [None] * count
    for k in range(half):
        er, ei = even[k]
        xr, xi = odd[k]
        if k == 0:
            tr, ti = xr, xi
        elif 4 * k == count:
            tr, ti = xi, -xr
        elif 8 * k == count:
            r = math.sqrt(0.5)
            tr, ti = (xr + xi) * r, (xi - xr) * r
        elif 8 * k == 3 * count:
            r = math.sqrt(0.5)
            tr, ti = (xi - xr) * r, (xr + xi) * (-r)
        else:
            c = math.cos(2.0 * math.pi * k / count)
            s = math.sin(2.0 * math.pi * k / count)
            tr, ti = xr * c + xi * s, xi * c - xr * s
        result[k] = (er + tr, ei + ti)
        result[k + half] = (er - tr, ei - ti)
    return result


def spectra_kernel(messages, *refs):
    groups = [group for message in messages for group in message]
    count = len(groups)
    sources, outs = refs[:6], refs[6 : 6 + len(messages)]
    vre, vim, taps, cos_t, sin_t, mat, frames, turned, packed, ready, sems = refs[6 + len(messages) :]
    chosen = [u for group in groups for u in GROUPS[group]]
    first, last = min(chosen), max(chosen) + TAPS
    rows_per_slot = 32 * len(chosen)
    slot_stride = rows_per_slot + 8

    loads = []
    for i in (2, 0, 1, 3, 4, 5):
        source = sources[i]
        if i < 2:
            source = source.at[:, first * CHANNELS : last * CHANNELS]
        loads.append(pltpu.make_async_copy(source, (vre, vim, taps, cos_t, sin_t, mat)[i], sems.at[i]))
        loads[-1].start()
    loads[0].wait()

    for c, volts in ((0, vre), (1, vim)):
        loads[1 + c].wait()

        def fir(n1, _, c=c, volts=volts):
            rows = [taps[k : k + 1, pl.ds(pl.multiple_of(n1 * INNER, INNER), INNER)] for k in range(TAPS)]
            needed = sorted({u + k for u in chosen for k in range(TAPS)})
            window = {
                b: volts[
                    :, pl.ds(pl.multiple_of((b - first) * CHANNELS + n1 * INNER, INNER), INNER)
                ].astype(jnp.float32)
                for b in needed
            }
            for i, u in enumerate(chosen):
                total = window[u] * rows[0]
                for k in range(1, TAPS):
                    total = total + window[u + k] * rows[k]
                frames[c, i, n1] = total
            return 0

        lax.fori_loop(0, OUTER, fir, 0)

    for load in loads[3:]:
        load.wait()

    def outer(i, _):
        u = i // 2
        low = pl.multiple_of((i % 2) * 8, 8)
        points = [
            (frames[0, u, n1, pl.ds(low, 8), :], frames[1, u, n1, pl.ds(low, 8), :]) for n1 in range(OUTER)
        ]
        points = small_fft(points)
        for f1 in range(OUTER):
            re, im = points[f1]
            if f1:
                c, d = cos_t[f1 : f1 + 1, :], sin_t[f1 : f1 + 1, :]
                re, im = re * c + im * d, im * c - re * d
            at = low * slot_stride + u * 32 + f1
            turned[0, pl.ds(at, 8, stride=slot_stride), :] = re
            turned[1, pl.ds(at, 8, stride=slot_stride), :] = im
        return 0

    lax.fori_loop(0, 2 * len(chosen), outer, 0)

    matrix = mat[...]
    lane = lax.broadcasted_iota(jnp.int32, (32, INNER), 1)

    def inner(a, _):
        base = pl.multiple_of(a * slot_stride, 8)
        rows = jnp.concatenate(
            [turned[0, pl.ds(base, rows_per_slot), :], turned[1, pl.ds(base, rows_per_slot), :]], axis=1
        ).astype(jnp.bfloat16)
        spec = lax.dot_general(
            matrix, rows, (((1,), (1,)), ((), ())), preferred_element_type=jnp.float32
        )
        for g in range(count):
            for y in range(2):
                for c in range(2):
                    to = [pl.ds((y * 2 + s) * 32 * ROW_STRIDE + a, 32, stride=ROW_STRIDE) for s in range(2)]
                    at = [c * 128 + (y * 2 + pair) * 32 for pair in range(2)]
                    mixed = [spec[f2 : f2 + 32, g * INNER : (g + 1) * INNER] for f2 in at]
                    packed[g * 2 + c, to[0], :] = jnp.where(lane < 64, mixed[0], pltpu.roll(mixed[1], 64, 1))
                    packed[g * 2 + c, to[1], :] = jnp.where(lane < 64, pltpu.roll(mixed[0], 64, 1), mixed[1])
        return 0

    lax.fori_loop(0, SLOTS, inner, 0, unroll=4)

    stores = []
    tile = 0
    for message, to in zip(messages, outs):
        for quarter in range(4):

            def emit(p, _, tile=tile, wide=2 * len(message)):
                for i in range(tile, tile + wide):
                    ready[p, :, i * INNER : (i + 1) * INNER] = packed[
                        i, pl.ds(pl.multiple_of(p * ROW_STRIDE, 8), SLOTS), :
                    ].astype(jnp.bfloat16)
                return 0

            lax.fori_loop(quarter * 32, quarter * 32 + 32, emit, 0, unroll=4)
            part = pl.ds(quarter * 32, 32)
            lanes = slice(tile * INNER, (tile + 2 * len(message)) * INNER)
            stores.append(
                pltpu.make_async_copy(ready.at[part, :, lanes], to.at[part], sems.at[6 + len(stores)])
            )
            stores[-1].start()
        tile += 2 * len(message)
    for store in stores:
        store.wait()


def spectra_of(messages, vre, vim, taps, interpret=False):
    cos_t, sin_t = twist_tables()
    mat = inner_matrix().astype(jnp.bfloat16)
    groups = [group for message in messages for group in message]
    count = len(groups)
    many = 4 * count
    chosen = [u for group in groups for u in GROUPS[group]]
    samples = (max(chosen) + TAPS - min(chosen)) * CHANNELS
    return pl.pallas_call(
        functools.partial(spectra_kernel, messages),
        out_shape=[jax.ShapeDtypeStruct((DEVICES, SLOTS, 2 * INNER * len(m)), jnp.bfloat16) for m in messages],
        in_specs=[pl.BlockSpec(memory_space=pltpu.HBM)] * 6,
        out_specs=[pl.BlockSpec(memory_space=pltpu.HBM)] * len(messages),
        scratch_shapes=[
            pltpu.VMEM((SLOTS, samples), jnp.bfloat16),
            pltpu.VMEM((SLOTS, samples), jnp.bfloat16),
            pltpu.VMEM((TAPS, CHANNELS), jnp.float32),
            pltpu.VMEM((OUTER, INNER), jnp.float32),
            pltpu.VMEM((OUTER, INNER), jnp.float32),
            pltpu.VMEM((256, 256), jnp.bfloat16),
            pltpu.VMEM((2, many, OUTER, SLOTS, INNER), jnp.float32),
            pltpu.VMEM((2, SLOTS * (32 * many + 8), INNER), jnp.float32),
            pltpu.VMEM((2 * count, DEVICES * ROW_STRIDE, INNER), jnp.float32),
            pltpu.VMEM((DEVICES, SLOTS, 2 * count * INNER), jnp.bfloat16),
            pltpu.SemaphoreType.DMA((6 + 4 * len(messages),)),
        ],
        compiler_params=pltpu.CompilerParams(vmem_limit_bytes=58 * MIB),
        cost_estimate=pl.CostEstimate(
            flops=8 * 10**8 * count, bytes_accessed=16 * 10**6 * count, transcendentals=0
        ),
        interpret=interpret,
        name="spectra",
    )(vre, vim, taps, jnp.asarray(cos_t), jnp.asarray(sin_t), jnp.asarray(mat))


SHIFTS = (0, -1, 1, 2)


def place():
    grp, dev = lax.axis_index("grp"), lax.axis_index("dev")
    return grp % 2, {"z": dev // 8, "x": dev // 2 % 4, "y": dev % 2 * 2 + grp // 2}


def quarter_kernel(wre, wim, slots, out0, out1, out2, out3, buf, names, chosen, turned, sems):
    grp = lax.axis_index("grp")
    y_lo, core = grp // 2, grp % 2
    antennas, beams = wre.shape
    half = antennas // 2
    name_copy = pltpu.make_async_copy(slots.at[core], names, sems.at[4])
    name_copy.start()
    for y, source in ((0, wre), (1, wim)):

        @pl.when(y_lo == y)
        def _():
            for i in range(4):
                part = pl.ds(i * half // 2, half // 2)
                pltpu.make_async_copy(source.at[part], buf.at[part], sems.at[i]).start()
    name_copy.wait()
    row = names[...]

    def build(i, _):
        antenna = lax.broadcasted_iota(jnp.int32, (16, half), 0) + i * 16
        chosen[pl.ds(pl.multiple_of(i * 16, 16), 16), :] = jnp.where(antenna == row, 1.0, 0.0).astype(jnp.bfloat16)
        return 0
    lax.fori_loop(0, antennas // 16, build, 0, unroll=4)
    for y, source in ((0, wre), (1, wim)):

        @pl.when(y_lo == y)
        def _():
            for i in range(4):
                part = pl.ds(i * half // 2, half // 2)
                pltpu.make_async_copy(source.at[part], buf.at[part], sems.at[i]).wait()
    for j in range(0, beams, 256):
        w = buf[:, j : j + 256].astype(jnp.bfloat16)
        for k in range(0, half, 512):
            turned[j : j + 256, k : k + 512] = lax.dot_general(
                w, chosen[:, k : k + 512], (((0,), (0,)), ((), ())), preferred_element_type=jnp.float32
            ).astype(jnp.bfloat16)
    quarter_finish(turned, (out0, out1, out2, out3))


def quarter_finish(turned, outs):
    core, coordinate = place()
    mine = jnp.where(core == 0, coordinate["z"], coordinate["x"])
    for shift, out in zip(SHIFTS, outs):
        block = (mine - shift + 4) % 4
        for j in range(4):
            at = jnp.where(core == 0, block * 128 + j * 32, j * 128 + block * 32)
            out[j * 32 : j * 32 + 32, :] = turned[pl.ds(pl.multiple_of(at, 32), 32), :]


def quarter_of(wre, wim, antenna_map, interpret=False):
    antennas, beams = wre.shape
    half = antennas // 2
    return pl.pallas_call(
        quarter_kernel,
        in_specs=[pl.BlockSpec(memory_space=pltpu.HBM)] * 3,
        out_specs=[pl.BlockSpec(memory_space=pltpu.VMEM)] * 4,
        out_shape=[jax.ShapeDtypeStruct((beams // 4, half), jnp.bfloat16)] * 4,
        scratch_shapes=[
            pltpu.VMEM((antennas, beams), jnp.float32),
            pltpu.VMEM((1, half), jnp.int32),
            pltpu.VMEM((antennas, half), jnp.bfloat16),
            pltpu.VMEM((beams, half), jnp.bfloat16),
            pltpu.SemaphoreType.DMA((5,)),
        ],
        compiler_params=pltpu.CompilerParams(vmem_limit_bytes=58 * MIB),
        cost_estimate=pl.CostEstimate(flops=2 * 10**9, bytes_accessed=6 * 10**6, transcendentals=0),
        interpret=interpret,
        name="quarter",
    )(wre, wim, antenna_map.reshape(2, 1, half))


def pick_kernel(kind, owners, *refs):
    inputs, outs = refs[:4], refs[4:]
    core, here = place()

    def copy_from(coordinate, position, copy):
        for shift, source in zip(SHIFTS, inputs):

            @pl.when((coordinate - position - shift + 8) % 4 == 0)
            def _():
                copy(source)

    for i in range(2):
        step = (core + i) % 2 if kind == "third" else i
        owner = owners[step]
        there = {"z": owner // 8, "x": owner // 2 % 4}
        if kind == "first":

            def copy(source):
                mine = jnp.where(core == 0, here["x"], here["z"])
                for shift, out in zip(SHIFTS, outs):
                    at = pl.multiple_of((mine - shift + 4) % 4 * 32, 32)
                    out[i * 32 : i * 32 + 32, :] = source[pl.ds(at, 32), :]

            copy_from(
                jnp.where(core == 0, there["z"], there["x"]), jnp.where(core == 0, here["z"], here["x"]), copy
            )
        elif kind == "second":

            def copy(source):
                outs[0][i * 32 : i * 32 + 32, :] = source[i * 32 : i * 32 + 32, :]

            copy_from(
                jnp.where(core == 0, there["x"], there["z"]), jnp.where(core == 0, here["x"], here["z"]), copy
            )
        else:
            for y_lo in range(2):

                def copy(source):
                    at = pl.multiple_of(step * 32, 32)
                    outs[i][y_lo * 32 : y_lo * 32 + 32, :] = source[pl.ds(at, 32), :]

                copy_from(owner % 2 * 2 + y_lo, here["y"], copy)


def pick_of(kind, owners, parts, interpret=False):
    columns = parts[0].shape[1]
    count = {"first": 4, "second": 1, "third": 2}[kind]
    return pl.pallas_call(
        functools.partial(pick_kernel, kind),
        in_specs=[pl.BlockSpec(memory_space=pltpu.SMEM)] + [pl.BlockSpec(memory_space=pltpu.VMEM)] * 4,
        out_specs=[pl.BlockSpec(memory_space=pltpu.VMEM)] * count,
        out_shape=[jax.ShapeDtypeStruct((64, columns), parts[0].dtype)] * count,
        compiler_params=pltpu.CompilerParams(vmem_limit_bytes=8 * MIB),
        interpret=interpret,
        name="pick_" + kind,
    )(owners, *parts)


def join_kernel(axis, *refs):
    parts, out = refs[:-1], refs[-1]
    at = 0
    for part in parts:
        size = part.shape[axis]
        if axis == 0:
            out[at : at + size, :] = part[...]
        else:
            out[:, at : at + size] = part[...]
        at += size


def join_of(parts, axis, interpret=False):
    shape = list(parts[0].shape)
    shape[axis] = sum(p.shape[axis] for p in parts)
    return pl.pallas_call(
        functools.partial(join_kernel, axis),
        out_shape=jax.ShapeDtypeStruct(tuple(shape), parts[0].dtype),
        in_specs=[pl.BlockSpec(memory_space=pltpu.VMEM)] * len(parts),
        out_specs=pl.BlockSpec(memory_space=pltpu.VMEM),
        compiler_params=pltpu.CompilerParams(vmem_limit_bytes=8 * MIB),
        interpret=interpret,
        name="join",
    )(*parts)


def choose_matrix():
    chosen = np.zeros((2, 32, 3, 2, 2, 32), np.float32)
    for pair in range(2):
        for f1 in range(32):
            chosen[pair, f1, :, pair, :, f1] = 1.0
    return chosen.reshape(64, 384)


def products(core, part, spectra):
    half = part.shape[1] // 2
    near = pl.ds(pl.multiple_of(core * half, half), half)
    far = pl.ds(pl.multiple_of((1 - core) * half, half), half)
    left, right = part[:, :half], part[:, half:]
    return [
        jnp.dot(left, z[near, :], preferred_element_type=jnp.float32)
        + jnp.dot(right, z[far, :], preferred_element_type=jnp.float32)
        for z in spectra
    ]


def early_kernel(w0, w1, za, zb, out):
    core = lax.axis_index("grp") % 2
    wide = za.shape[1]
    for i, part in enumerate((w0, w1)):
        n = part.shape[0]
        first, second = products(core, part, (za, zb))
        out[i * n : (i + 1) * n, :wide] = first
        out[i * n : (i + 1) * n, wide:] = second


def early_of(w0, w1, spectra, interpret=False):
    return pl.pallas_call(
        early_kernel,
        out_shape=jax.ShapeDtypeStruct((2 * w0.shape[0], 768), jnp.float32),
        in_specs=[pl.BlockSpec(memory_space=pltpu.VMEM)] * 4,
        out_specs=pl.BlockSpec(memory_space=pltpu.VMEM),
        compiler_params=pltpu.CompilerParams(vmem_limit_bytes=24 * MIB),
        cost_estimate=pl.CostEstimate(flops=17 * 10**8, bytes_accessed=8 * 10**6, transcendentals=0),
        interpret=interpret,
        name="early",
    )(w0, w1, *spectra)


def beams_kernel(early, w2, w3, za, zb, choose, out, sums):
    core, here = place()
    wide = za.shape[1]

    def row_of(part, k):
        first, y_lo = SHIFTS[k // 2], k % 2
        second = SHIFTS[part]
        z = (here["z"] + jnp.where(core == 0, second, first) + 4) % 4
        x = (here["x"] + jnp.where(core == 0, first, second) + 4) % 4
        return pl.ds(pl.multiple_of(y_lo * 512 + z * 128 + x * 32, 32), 32)

    for part in range(2):
        for k in range(8):
            sums[row_of(part, k), :] = early[part * 256 + k * 32 : part * 256 + (k + 1) * 32, :]
    for part, w in ((2, w2), (3, w3)):
        first, second = products(core, w, (za, zb))
        for k in range(8):
            sums[row_of(part, k), :wide] = first[k * 32 : (k + 1) * 32, :]
            sums[row_of(part, k), wide:] = second[k * 32 : (k + 1) * 32, :]
    beams = sums.shape[0] // 2
    powers = []
    for g in range(3):
        re_lanes, im_lanes = slice(g * 256, g * 256 + 128), slice(g * 256 + 128, g * 256 + 256)
        re = sums[:beams, re_lanes] - sums[beams:, im_lanes]
        im = sums[beams:, re_lanes] + sums[:beams, im_lanes]
        powers.append(re * re + im * im)
    total = lax.dot_general(
        choose[...],
        jnp.concatenate(powers, axis=1),
        (((1,), (1,)), ((), ())),
        preferred_element_type=jnp.float32,
        precision=lax.Precision.HIGHEST,
    )
    out[...] = total * (1.0 / SPECTRA)


def beams_of(early, w2, w3, spectra, interpret=False):
    rows = early.shape[0] + 2 * w2.shape[0]
    return pl.pallas_call(
        beams_kernel,
        out_shape=jax.ShapeDtypeStruct((64, rows // 2), jnp.float32),
        in_specs=[pl.BlockSpec(memory_space=pltpu.VMEM)] * 6,
        out_specs=pl.BlockSpec(memory_space=pltpu.VMEM),
        scratch_shapes=[pltpu.VMEM((rows, 768), jnp.float32)],
        compiler_params=pltpu.CompilerParams(vmem_limit_bytes=32 * MIB),
        cost_estimate=pl.CostEstimate(flops=17 * 10**8, bytes_accessed=8 * 10**6, transcendentals=0),
        interpret=interpret,
        name="beams",
    )(early, w2, w3, *spectra, jnp.asarray(choose_matrix()))


def index_of(z, x, y, core):
    return ((y % 2) * 2 + core) * 32 + (z % 4) * 8 + (x % 4) * 2 + (y % 4) // 2


EVERY = [(z, x, y, c) for z in range(4) for x in range(4) for y in range(4) for c in range(2)]
AXES = (("z", "x", "y", "x", "z"), ("x", "z", "y", "z", "x"))


def permutation(stage, shift):
    pairs = []
    for z, x, y, core in EVERY:
        axis = AXES[core][stage]
        source = {"z": z, "x": x, "y": y}
        source[axis] += shift
        pairs.append((index_of(source["z"], source["x"], source["y"], core), index_of(z, x, y, core)))
    return pairs


def exchange(blocks, stage):
    return [blocks[0]] + [
        lax.ppermute(block, ALL, permutation(stage, shift)) for block, shift in zip(blocks[1:], SHIFTS[1:])
    ]


SWAP = [(0, 1), (1, 0), (2, 3), (3, 2)]


def on_device(voltage_real, voltage_imaginary, filter_taps, weights_re, weights_im, owners, antenna_map):
    core = lax.axis_index("grp") % 2
    tie = lax.optimization_barrier

    def turn(message):
        moved = lax.all_to_all(message, ALL, split_axis=0, concat_axis=0, tiled=True)
        return moved.reshape(DEVICES * SLOTS, -1)

    volts = (voltage_real, voltage_imaginary, filter_taps)
    blocks = quarter_of(weights_re[0], weights_im[0], antenna_map)
    blocks, volts = tie((blocks, volts))
    blocks = exchange(blocks, 0)
    (late,) = spectra_of(((2,),), *volts)
    blocks, late, volts = tie((blocks, late, volts))
    blocks = pick_of("first", owners, blocks)
    blocks, late, volts = tie((blocks, late, volts))
    blocks = exchange(blocks, 1)
    late = turn(late)
    (soon,) = spectra_of(((0, 1),), *volts)
    blocks, soon, late = tie((blocks, soon, late))
    (block,) = pick_of("second", owners, blocks)
    blocks = exchange([block] * 4, 2)
    mine, other = pick_of("third", owners, blocks)
    other = lax.ppermute(other, "grp", SWAP)
    block = join_of([mine, other], 1)
    block = join_of(exchange([block] * 4, 3), 0)
    block, soon = tie((block, soon))
    soon = turn(soon)
    parts = exchange([block] * 4, 4)

    spectra = (soon, late)
    early = early_of(parts[0], parts[1], spectra)
    power = beams_of(early, parts[2], parts[3], spectra)
    power = power.reshape(2, 32, -1)
    own = jnp.where(core == 0, power[0], power[1])
    given = jnp.where(core == 0, power[1], power[0])
    taken = lax.ppermute(given, "grp", SWAP)
    return jnp.where(core == 0, jnp.stack([own, taken]), jnp.stack([taken, own]))


def solution(mesh):
    return jax.shard_map(
        on_device,
        mesh=mesh,
        in_specs=(
            P(("grp", "dev"), None),
            P(("grp", "dev"), None),
            P(),
            P("dev", None, None),
            P("dev", None, None),
            P(),
            P(),
        ),
        out_specs=P(None, ("grp", "dev"), None),
        check_vma=False,
    )
```

```python
import functools
import math

import jax
import jax.numpy as jnp
import numpy as np
from jax import lax
from jax.experimental import pallas as pl
from jax.experimental.pallas import tpu as pltpu
from jax.sharding import PartitionSpec as P

CHANNELS = 4096
TAPS = 16
SPECTRA = 6
STEPS = 2
FRAMES = STEPS * SPECTRA
BLOCKS = FRAMES + TAPS - 1
OUTER = 32
INNER = 128
SLOTS = 16
DEVICES = 128
ROW_STRIDE = 24
GROUPS = ((0, 1, 6, 7), (2, 3, 8, 9), (4, 5, 10, 11))
MESSAGES = ((0, 1, 2),)
ALL = ("grp", "dev")
MIB = 1 << 20


def twist_tables():
    products = np.outer(np.arange(OUTER), np.arange(INNER)) % CHANNELS
    angles = products * (2.0 * math.pi / CHANNELS)
    return np.cos(angles).astype(np.float32), np.sin(angles).astype(np.float32)


def inner_matrix():
    products = np.outer(np.arange(INNER), np.arange(INNER)) % INNER
    angles = products * (2.0 * math.pi / INNER)
    norm = CHANNELS ** (-0.5)
    c, s = np.cos(angles) * norm, np.sin(angles) * norm
    return np.block([[c, s], [-s, c]]).astype(np.float32)


def small_fft(points):
    count = len(points)
    if count == 1:
        return points
    even = small_fft(points[0::2])
    odd = small_fft(points[1::2])
    half = count // 2
    result = [None] * count
    for k in range(half):
        er, ei = even[k]
        xr, xi = odd[k]
        if k == 0:
            tr, ti = xr, xi
        elif 4 * k == count:
            tr, ti = xi, -xr
        elif 8 * k == count:
            r = math.sqrt(0.5)
            tr, ti = (xr + xi) * r, (xi - xr) * r
        elif 8 * k == 3 * count:
            r = math.sqrt(0.5)
            tr, ti = (xi - xr) * r, (xr + xi) * (-r)
        else:
            c = math.cos(2.0 * math.pi * k / count)
            s = math.sin(2.0 * math.pi * k / count)
            tr, ti = xr * c + xi * s, xi * c - xr * s
        result[k] = (er + tr, ei + ti)
        result[k + half] = (er - tr, ei - ti)
    return result


def spectra_kernel(messages, *refs):
    groups = [group for message in messages for group in message]
    count = len(groups)
    sources, outs = refs[:6], refs[6 : 6 + len(messages)]
    vre, vim, taps, cos_t, sin_t, mat, frames, turned, packed, ready, sems = refs[6 + len(messages) :]
    chosen = [u for group in groups for u in GROUPS[group]]
    first, last = min(chosen), max(chosen) + TAPS
    rows_per_slot = 32 * len(chosen)
    slot_stride = rows_per_slot + 8

    loads = []
    for i in (2, 0, 1, 3, 4, 5):
        source = sources[i]
        if i < 2:
            source = source.at[:, first * CHANNELS : last * CHANNELS]
        loads.append(pltpu.make_async_copy(source, (vre, vim, taps, cos_t, sin_t, mat)[i], sems.at[i]))
        loads[-1].start()
    loads[0].wait()

    for c, volts in ((0, vre), (1, vim)):
        loads[1 + c].wait()

        def fir(n1, _, c=c, volts=volts):
            rows = [taps[k : k + 1, pl.ds(pl.multiple_of(n1 * INNER, INNER), INNER)] for k in range(TAPS)]
            needed = sorted({u + k for u in chosen for k in range(TAPS)})
            window = {
                b: volts[
                    :, pl.ds(pl.multiple_of((b - first) * CHANNELS + n1 * INNER, INNER), INNER)
                ].astype(jnp.float32)
                for b in needed
            }
            for i, u in enumerate(chosen):
                total = window[u] * rows[0]
                for k in range(1, TAPS):
                    total = total + window[u + k] * rows[k]
                frames[c, i, n1] = total
            return 0

        lax.fori_loop(0, OUTER, fir, 0)

    for load in loads[3:]:
        load.wait()

    def outer(i, _):
        u = i // 2
        low = pl.multiple_of((i % 2) * 8, 8)
        points = [
            (frames[0, u, n1, pl.ds(low, 8), :], frames[1, u, n1, pl.ds(low, 8), :]) for n1 in range(OUTER)
        ]
        points = small_fft(points)
        for f1 in range(OUTER):
            re, im = points[f1]
            if f1:
                c, d = cos_t[f1 : f1 + 1, :], sin_t[f1 : f1 + 1, :]
                re, im = re * c + im * d, im * c - re * d
            at = low * slot_stride + u * 32 + f1
            turned[0, pl.ds(at, 8, stride=slot_stride), :] = re
            turned[1, pl.ds(at, 8, stride=slot_stride), :] = im
        return 0

    lax.fori_loop(0, 2 * len(chosen), outer, 0)

    matrix = mat[...]
    lane = lax.broadcasted_iota(jnp.int32, (32, INNER), 1)

    def inner(a, _):
        base = pl.multiple_of(a * slot_stride, 8)
        rows = jnp.concatenate(
            [turned[0, pl.ds(base, rows_per_slot), :], turned[1, pl.ds(base, rows_per_slot), :]], axis=1
        ).astype(jnp.bfloat16)
        spec = lax.dot_general(
            matrix, rows, (((1,), (1,)), ((), ())), preferred_element_type=jnp.float32
        )
        for g in range(count):
            for y in range(2):
                for c in range(2):
                    to = [pl.ds((y * 2 + s) * 32 * ROW_STRIDE + a, 32, stride=ROW_STRIDE) for s in range(2)]
                    at = [c * 128 + (y * 2 + pair) * 32 for pair in range(2)]
                    mixed = [spec[f2 : f2 + 32, g * INNER : (g + 1) * INNER] for f2 in at]
                    packed[g * 2 + c, to[0], :] = jnp.where(lane < 64, mixed[0], pltpu.roll(mixed[1], 64, 1))
                    packed[g * 2 + c, to[1], :] = jnp.where(lane < 64, pltpu.roll(mixed[0], 64, 1), mixed[1])
        return 0

    lax.fori_loop(0, SLOTS, inner, 0, unroll=4)

    stores = []
    tile = 0
    for message, to in zip(messages, outs):
        for quarter in range(4):

            def emit(p, _, tile=tile, wide=2 * len(message)):
                for i in range(tile, tile + wide):
                    ready[p, :, i * INNER : (i + 1) * INNER] = packed[
                        i, pl.ds(pl.multiple_of(p * ROW_STRIDE, 8), SLOTS), :
                    ].astype(jnp.bfloat16)
                return 0

            lax.fori_loop(quarter * 32, quarter * 32 + 32, emit, 0, unroll=4)
            part = pl.ds(quarter * 32, 32)
            lanes = slice(tile * INNER, (tile + 2 * len(message)) * INNER)
            stores.append(
                pltpu.make_async_copy(ready.at[part, :, lanes], to.at[part], sems.at[6 + len(stores)])
            )
            stores[-1].start()
        tile += 2 * len(message)
    for store in stores:
        store.wait()


def spectra_of(messages, vre, vim, taps, interpret=False):
    cos_t, sin_t = twist_tables()
    mat = inner_matrix().astype(jnp.bfloat16)
    groups = [group for message in messages for group in message]
    count = len(groups)
    many = 4 * count
    chosen = [u for group in groups for u in GROUPS[group]]
    samples = (max(chosen) + TAPS - min(chosen)) * CHANNELS
    return pl.pallas_call(
        functools.partial(spectra_kernel, messages),
        out_shape=[jax.ShapeDtypeStruct((DEVICES, SLOTS, 2 * INNER * len(m)), jnp.bfloat16) for m in messages],
        in_specs=[pl.BlockSpec(memory_space=pltpu.HBM)] * 6,
        out_specs=[pl.BlockSpec(memory_space=pltpu.HBM)] * len(messages),
        scratch_shapes=[
            pltpu.VMEM((SLOTS, samples), jnp.bfloat16),
            pltpu.VMEM((SLOTS, samples), jnp.bfloat16),
            pltpu.VMEM((TAPS, CHANNELS), jnp.float32),
            pltpu.VMEM((OUTER, INNER), jnp.float32),
            pltpu.VMEM((OUTER, INNER), jnp.float32),
            pltpu.VMEM((256, 256), jnp.bfloat16),
            pltpu.VMEM((2, many, OUTER, SLOTS, INNER), jnp.float32),
            pltpu.VMEM((2, SLOTS * (32 * many + 8), INNER), jnp.float32),
            pltpu.VMEM((2 * count, DEVICES * ROW_STRIDE, INNER), jnp.float32),
            pltpu.VMEM((DEVICES, SLOTS, 2 * count * INNER), jnp.bfloat16),
            pltpu.SemaphoreType.DMA((6 + 4 * len(messages),)),
        ],
        compiler_params=pltpu.CompilerParams(vmem_limit_bytes=58 * MIB),
        cost_estimate=pl.CostEstimate(
            flops=8 * 10**8 * count, bytes_accessed=16 * 10**6 * count, transcendentals=0
        ),
        interpret=interpret,
        name="spectra",
    )(vre, vim, taps, jnp.asarray(cos_t), jnp.asarray(sin_t), jnp.asarray(mat))


def quarter_kernel(wre, wim, slots, out, buf, names, chosen, sems):
    grp = lax.axis_index("grp")
    y_lo, core = grp // 2, grp % 2
    antennas, beams = wre.shape
    half = antennas // 2
    name_copy = pltpu.make_async_copy(slots.at[core], names, sems.at[4])
    name_copy.start()
    for y, source in ((0, wre), (1, wim)):

        @pl.when(y_lo == y)
        def _():
            for i in range(4):
                part = pl.ds(i * half // 2, half // 2)
                pltpu.make_async_copy(source.at[part], buf.at[part], sems.at[i]).start()
    name_copy.wait()
    row = names[...]

    def build(i, _):
        antenna = lax.broadcasted_iota(jnp.int32, (16, half), 0) + i * 16
        chosen[pl.ds(pl.multiple_of(i * 16, 16), 16), :] = jnp.where(antenna == row, 1.0, 0.0).astype(jnp.bfloat16)
        return 0
    lax.fori_loop(0, antennas // 16, build, 0, unroll=4)
    for y, source in ((0, wre), (1, wim)):

        @pl.when(y_lo == y)
        def _():
            for i in range(4):
                part = pl.ds(i * half // 2, half // 2)
                pltpu.make_async_copy(source.at[part], buf.at[part], sems.at[i]).wait()
    for j in range(0, beams, 256):
        w = buf[:, j : j + 256].astype(jnp.bfloat16)
        for k in range(0, half, 512):
            out[j : j + 256, k : k + 512] = lax.dot_general(
                w, chosen[:, k : k + 512], (((0,), (0,)), ((), ())), preferred_element_type=jnp.float32
            ).astype(jnp.bfloat16)


def quarter_of(wre, wim, antenna_map, interpret=False):
    antennas, beams = wre.shape
    half = antennas // 2
    return pl.pallas_call(
        quarter_kernel,
        in_specs=[pl.BlockSpec(memory_space=pltpu.HBM)] * 3,
        out_specs=pl.BlockSpec(memory_space=pltpu.VMEM),
        out_shape=jax.ShapeDtypeStruct((beams, half), jnp.bfloat16),
        scratch_shapes=[
            pltpu.VMEM((antennas, beams), jnp.float32),
            pltpu.VMEM((1, half), jnp.int32),
            pltpu.VMEM((antennas, half), jnp.bfloat16),
            pltpu.SemaphoreType.DMA((5,)),
        ],
        compiler_params=pltpu.CompilerParams(vmem_limit_bytes=58 * MIB),
        cost_estimate=pl.CostEstimate(flops=2 * 10**9, bytes_accessed=6 * 10**6, transcendentals=0),
        interpret=interpret,
        name="quarter",
    )(wre, wim, antenna_map.reshape(2, 1, half))


def pick_kernel(owners, offers, mine, other, sems):
    core = lax.axis_index("grp") % 2
    copies = [
        pltpu.make_async_copy(offers.at[owners[core]], mine, sems.at[0]),
        pltpu.make_async_copy(offers.at[owners[1 - core]], other, sems.at[1]),
    ]
    for copy in copies:
        copy.start()
    for copy in copies:
        copy.wait()


def pick_of(owners, offers, interpret=False):
    _, rows, columns = offers.shape
    return pl.pallas_call(
        pick_kernel,
        in_specs=[pl.BlockSpec(memory_space=pltpu.SMEM), pl.BlockSpec(memory_space=pltpu.HBM)],
        out_specs=[pl.BlockSpec(memory_space=pltpu.VMEM)] * 2,
        out_shape=[jax.ShapeDtypeStruct((rows, columns), offers.dtype)] * 2,
        scratch_shapes=[pltpu.SemaphoreType.DMA((2,))],
        compiler_params=pltpu.CompilerParams(vmem_limit_bytes=58 * MIB),
        interpret=interpret,
        name="pick",
    )(owners, offers)


def join_kernel(axis, *refs):
    parts, out = refs[:-1], refs[-1]
    at = 0
    for part in parts:
        size = part.shape[axis]
        if axis == 0:
            out[at : at + size, :] = part[...]
        else:
            out[:, at : at + size] = part[...]
        at += size


def join_of(parts, axis, interpret=False):
    shape = list(parts[0].shape)
    shape[axis] = sum(p.shape[axis] for p in parts)
    return pl.pallas_call(
        functools.partial(join_kernel, axis),
        out_shape=jax.ShapeDtypeStruct(tuple(shape), parts[0].dtype),
        in_specs=[pl.BlockSpec(memory_space=pltpu.VMEM)] * len(parts),
        out_specs=pl.BlockSpec(memory_space=pltpu.VMEM),
        compiler_params=pltpu.CompilerParams(vmem_limit_bytes=8 * MIB),
        interpret=interpret,
        name="join",
    )(*parts)


def choose_matrix():
    chosen = np.zeros((2, 32, 3, 2, 2, 32), np.float32)
    for pair in range(2):
        for f1 in range(32):
            chosen[pair, f1, :, pair, :, f1] = 1.0
    return chosen.reshape(64, 384)


def products(core, part, spectra):
    half = part.shape[1] // 2
    near = pl.ds(pl.multiple_of(core * half, half), half)
    far = pl.ds(pl.multiple_of((1 - core) * half, half), half)
    left, right = part[:, :half], part[:, half:]
    return jnp.dot(left, spectra[near, :], preferred_element_type=jnp.float32) + jnp.dot(
        right, spectra[far, :], preferred_element_type=jnp.float32
    )


def early_kernel(w0, w1, za, out):
    core = lax.axis_index("grp") % 2
    n = w0.shape[0]
    for i, part in enumerate((w0, w1)):
        out[i * n : (i + 1) * n, :] = products(core, part, za)


def early_of(w0, w1, spectra, interpret=False):
    return pl.pallas_call(
        early_kernel,
        out_shape=jax.ShapeDtypeStruct((2 * w0.shape[0], 768), jnp.float32),
        in_specs=[pl.BlockSpec(memory_space=pltpu.VMEM)] * 3,
        out_specs=pl.BlockSpec(memory_space=pltpu.VMEM),
        compiler_params=pltpu.CompilerParams(vmem_limit_bytes=24 * MIB),
        cost_estimate=pl.CostEstimate(flops=17 * 10**8, bytes_accessed=8 * 10**6, transcendentals=0),
        interpret=interpret,
        name="early",
    )(w0, w1, spectra)


def beams_kernel(places, early, w2, w3, za, choose, out, sums):
    for k in range(32):
        at = pl.multiple_of(places[k], 16)
        sums[pl.ds(at, 16), :] = early[k * 16 : (k + 1) * 16, :]
    core = lax.axis_index("grp") % 2
    for i, part in enumerate((w2, w3)):
        result = products(core, part, za)
        for k in range(16):
            at = pl.multiple_of(places[(i + 2) * 16 + k], 16)
            sums[pl.ds(at, 16), :] = result[k * 16 : (k + 1) * 16, :]
    beams = sums.shape[0] // 2
    powers = []
    for g in range(3):
        re_lanes, im_lanes = slice(g * 256, g * 256 + 128), slice(g * 256 + 128, g * 256 + 256)
        re = sums[:beams, re_lanes] - sums[beams:, im_lanes]
        im = sums[beams:, re_lanes] + sums[:beams, im_lanes]
        powers.append(re * re + im * im)
    total = lax.dot_general(
        choose[...],
        jnp.concatenate(powers, axis=1),
        (((1,), (1,)), ((), ())),
        preferred_element_type=jnp.float32,
        precision=lax.Precision.HIGHEST,
    )
    out[...] = total * (1.0 / SPECTRA)


def beams_of(places, early, w2, w3, spectra, interpret=False):
    rows = early.shape[0] + 2 * w2.shape[0]
    return pl.pallas_call(
        beams_kernel,
        out_shape=jax.ShapeDtypeStruct((64, rows // 2), jnp.float32),
        in_specs=[pl.BlockSpec(memory_space=pltpu.SMEM)] + [pl.BlockSpec(memory_space=pltpu.VMEM)] * 5,
        out_specs=pl.BlockSpec(memory_space=pltpu.VMEM),
        scratch_shapes=[pltpu.VMEM((rows, 768), jnp.float32)],
        compiler_params=pltpu.CompilerParams(vmem_limit_bytes=32 * MIB),
        cost_estimate=pl.CostEstimate(flops=17 * 10**8, bytes_accessed=8 * 10**6, transcendentals=0),
        interpret=interpret,
        name="beams",
    )(places, early, w2, w3, spectra, jnp.asarray(choose_matrix()))


def index_of(z, x, y, core):
    return ((y % 2) * 2 + core) * 32 + (z % 4) * 8 + (x % 4) * 2 + (y % 4) // 2


EVERY = [(z, x, y, c) for z in range(4) for x in range(4) for y in range(4) for c in range(2)]
ORDER = (("y", "x", "z"), ("z", "y", "x"))
SHIFTS = (0, -1, 1, 2)


def permutation(stage, shift):
    pairs = []
    for z, x, y, core in EVERY:
        axis = ORDER[core][stage]
        source = {"z": z, "x": x, "y": y}
        source[axis] += shift
        pairs.append((index_of(source["z"], source["x"], source["y"], core), index_of(z, x, y, core)))
    return pairs


def gather_stage(block, stage):
    return [block] + [lax.ppermute(block, ALL, permutation(stage, shift)) for shift in SHIFTS[1:]]


def block_places(grp, dev):
    core = grp % 2
    z, x, y = dev // 8, dev // 2 % 4, dev % 2 * 2 + grp // 2
    k = np.arange(64)
    shift = np.array(SHIFTS)
    first, second, third = shift[k % 4], shift[k // 4 % 4], shift[k // 16]
    by_core = []
    for order in ORDER:
        moved = dict(zip(order, (first, second, third)))
        by_core.append([moved[axis] for axis in "zxy"])
    is_first = core == 0
    mz, mx, my = [jnp.where(is_first, jnp.asarray(a), jnp.asarray(b)) for a, b in zip(*by_core)]
    fz, fx, fy = (z + mz + 4) % 4, (x + mx + 4) % 4, (y + my + 4) % 4
    return (((fy % 2) * 32 + fz * 8 + fx * 2 + fy // 2) * 16).astype(jnp.int32)


SWAP = [(0, 1), (1, 0), (2, 3), (3, 2)]


def on_device(voltage_real, voltage_imaginary, filter_taps, weights_re, weights_im, owners, antenna_map):
    grp, dev = lax.axis_index("grp"), lax.axis_index("dev")
    core = grp % 2

    quarter = quarter_of(weights_re[0], weights_im[0], antenna_map)
    offers = lax.all_to_all(quarter.reshape(32, 16, -1), "dev", split_axis=0, concat_axis=0, tiled=True)

    volts = (voltage_real, voltage_imaginary, filter_taps)
    quarter, *volts = lax.optimization_barrier((quarter, *volts))
    (message,) = spectra_of(MESSAGES, *volts)
    message, offers = lax.optimization_barrier((message, offers))
    spectra = lax.all_to_all(message, ALL, split_axis=0, concat_axis=0, tiled=True)
    spectra = spectra.reshape(DEVICES * SLOTS, -1)

    mine, other = pick_of(owners, offers)
    other = lax.ppermute(other, "grp", SWAP)
    block = join_of([mine, other], 1)
    block = join_of(gather_stage(block, 0), 0)
    block = join_of(gather_stage(block, 1), 0)
    parts = gather_stage(block, 2)

    early = early_of(parts[0], parts[3], spectra)
    places = block_places(grp, dev)
    places = jnp.concatenate([places[:16], places[48:], places[16:48]])
    power = beams_of(places, early, parts[1], parts[2], spectra)
    power = power.reshape(2, 32, -1)
    own = jnp.where(core == 0, power[0], power[1])
    given = jnp.where(core == 0, power[1], power[0])
    taken = lax.ppermute(given, "grp", SWAP)
    return jnp.where(core == 0, jnp.stack([own, taken]), jnp.stack([taken, own]))


def solution(mesh):
    return jax.shard_map(
        on_device,
        mesh=mesh,
        in_specs=(
            P(("grp", "dev"), None),
            P(("grp", "dev"), None),
            P(),
            P("dev", None, None),
            P("dev", None, None),
            P(),
            P(),
        ),
        out_specs=P(None, ("grp", "dev"), None),
        check_vma=False,
    )
```

```python
import functools
import math

import jax
import jax.numpy as jnp
import numpy as np
from jax import lax
from jax.experimental import pallas as pl
from jax.experimental.pallas import tpu as pltpu
from jax.sharding import PartitionSpec as P

CHANNELS = 4096
TAPS = 16
SPECTRA = 6
STEPS = 2
FRAMES = STEPS * SPECTRA
BLOCKS = FRAMES + TAPS - 1
OUTER = 32
INNER = 128
SLOTS = 16
DEVICES = 128
ROW_STRIDE = 24
GROUPS = ((0, 1, 6, 7), (2, 3, 8, 9), (4, 5, 10, 11))
MESSAGES = ((0, 1, 2),)
ALL = ("grp", "dev")
MIB = 1 << 20


def twist_tables():
    products = np.outer(np.arange(OUTER), np.arange(INNER)) % CHANNELS
    angles = products * (2.0 * math.pi / CHANNELS)
    return np.cos(angles).astype(np.float32), np.sin(angles).astype(np.float32)


def inner_matrix():
    products = np.outer(np.arange(INNER), np.arange(INNER)) % INNER
    angles = products * (2.0 * math.pi / INNER)
    norm = CHANNELS ** (-0.5)
    c, s = np.cos(angles) * norm, np.sin(angles) * norm
    return np.block([[c, s], [-s, c]]).astype(np.float32)


def small_fft(points):
    count = len(points)
    if count == 1:
        return points
    even = small_fft(points[0::2])
    odd = small_fft(points[1::2])
    half = count // 2
    result = [None] * count
    for k in range(half):
        er, ei = even[k]
        xr, xi = odd[k]
        if k == 0:
            tr, ti = xr, xi
        elif 4 * k == count:
            tr, ti = xi, -xr
        elif 8 * k == count:
            r = math.sqrt(0.5)
            tr, ti = (xr + xi) * r, (xi - xr) * r
        elif 8 * k == 3 * count:
            r = math.sqrt(0.5)
            tr, ti = (xi - xr) * r, (xr + xi) * (-r)
        else:
            c = math.cos(2.0 * math.pi * k / count)
            s = math.sin(2.0 * math.pi * k / count)
            tr, ti = xr * c + xi * s, xi * c - xr * s
        result[k] = (er + tr, ei + ti)
        result[k + half] = (er - tr, ei - ti)
    return result


def spectra_kernel(messages, *refs):
    groups = [group for message in messages for group in message]
    count = len(groups)
    sources, outs = refs[:6], refs[6 : 6 + len(messages)]
    vre, vim, taps, cos_t, sin_t, mat, frames, turned, packed, ready, sems = refs[6 + len(messages) :]
    chosen = [u for group in groups for u in GROUPS[group]]
    first, last = min(chosen), max(chosen) + TAPS
    rows_per_slot = 32 * len(chosen)
    slot_stride = rows_per_slot + 8

    loads = []
    for i in (2, 0, 1, 3, 4, 5):
        source = sources[i]
        if i < 2:
            source = source.at[:, first * CHANNELS : last * CHANNELS]
        loads.append(pltpu.make_async_copy(source, (vre, vim, taps, cos_t, sin_t, mat)[i], sems.at[i]))
        loads[-1].start()
    loads[0].wait()

    for c, volts in ((0, vre), (1, vim)):
        loads[1 + c].wait()

        def fir(n1, _, c=c, volts=volts):
            rows = [taps[k : k + 1, pl.ds(pl.multiple_of(n1 * INNER, INNER), INNER)] for k in range(TAPS)]
            needed = sorted({u + k for u in chosen for k in range(TAPS)})
            window = {
                b: volts[
                    :, pl.ds(pl.multiple_of((b - first) * CHANNELS + n1 * INNER, INNER), INNER)
                ].astype(jnp.float32)
                for b in needed
            }
            for i, u in enumerate(chosen):
                total = window[u] * rows[0]
                for k in range(1, TAPS):
                    total = total + window[u + k] * rows[k]
                frames[c, i, n1] = total
            return 0

        lax.fori_loop(0, OUTER, fir, 0)

    for load in loads[3:]:
        load.wait()

    def outer(i, _):
        u = i // 2
        low = pl.multiple_of((i % 2) * 8, 8)
        points = [
            (frames[0, u, n1, pl.ds(low, 8), :], frames[1, u, n1, pl.ds(low, 8), :]) for n1 in range(OUTER)
        ]
        points = small_fft(points)
        for f1 in range(OUTER):
            re, im = points[f1]
            if f1:
                c, d = cos_t[f1 : f1 + 1, :], sin_t[f1 : f1 + 1, :]
                re, im = re * c + im * d, im * c - re * d
            at = low * slot_stride + u * 32 + f1
            turned[0, pl.ds(at, 8, stride=slot_stride), :] = re
            turned[1, pl.ds(at, 8, stride=slot_stride), :] = im
        return 0

    lax.fori_loop(0, 2 * len(chosen), outer, 0)

    matrix = mat[...]
    lane = lax.broadcasted_iota(jnp.int32, (32, INNER), 1)

    def inner(a, _):
        base = pl.multiple_of(a * slot_stride, 8)
        rows = jnp.concatenate(
            [turned[0, pl.ds(base, rows_per_slot), :], turned[1, pl.ds(base, rows_per_slot), :]], axis=1
        ).astype(jnp.bfloat16)
        spec = lax.dot_general(
            matrix, rows, (((1,), (1,)), ((), ())), preferred_element_type=jnp.float32
        )
        for g in range(count):
            for y in range(2):
                for c in range(2):
                    to = [pl.ds((y * 2 + s) * 32 * ROW_STRIDE + a, 32, stride=ROW_STRIDE) for s in range(2)]
                    at = [c * 128 + (y * 2 + pair) * 32 for pair in range(2)]
                    mixed = [spec[f2 : f2 + 32, g * INNER : (g + 1) * INNER] for f2 in at]
                    packed[g * 2 + c, to[0], :] = jnp.where(lane < 64, mixed[0], pltpu.roll(mixed[1], 64, 1))
                    packed[g * 2 + c, to[1], :] = jnp.where(lane < 64, pltpu.roll(mixed[0], 64, 1), mixed[1])
        return 0

    lax.fori_loop(0, SLOTS, inner, 0, unroll=4)

    stores = []
    tile = 0
    for message, to in zip(messages, outs):
        for quarter in range(4):

            def emit(p, _, tile=tile, wide=2 * len(message)):
                for i in range(tile, tile + wide):
                    ready[p, :, i * INNER : (i + 1) * INNER] = packed[
                        i, pl.ds(pl.multiple_of(p * ROW_STRIDE, 8), SLOTS), :
                    ].astype(jnp.bfloat16)
                return 0

            lax.fori_loop(quarter * 32, quarter * 32 + 32, emit, 0, unroll=4)
            part = pl.ds(quarter * 32, 32)
            lanes = slice(tile * INNER, (tile + 2 * len(message)) * INNER)
            stores.append(
                pltpu.make_async_copy(ready.at[part, :, lanes], to.at[part], sems.at[6 + len(stores)])
            )
            stores[-1].start()
        tile += 2 * len(message)
    for store in stores:
        store.wait()


def spectra_of(messages, vre, vim, taps, interpret=False):
    cos_t, sin_t = twist_tables()
    mat = inner_matrix().astype(jnp.bfloat16)
    groups = [group for message in messages for group in message]
    count = len(groups)
    many = 4 * count
    chosen = [u for group in groups for u in GROUPS[group]]
    samples = (max(chosen) + TAPS - min(chosen)) * CHANNELS
    return pl.pallas_call(
        functools.partial(spectra_kernel, messages),
        out_shape=[jax.ShapeDtypeStruct((DEVICES, SLOTS, 2 * INNER * len(m)), jnp.bfloat16) for m in messages],
        in_specs=[pl.BlockSpec(memory_space=pltpu.HBM)] * 6,
        out_specs=[pl.BlockSpec(memory_space=pltpu.HBM)] * len(messages),
        scratch_shapes=[
            pltpu.VMEM((SLOTS, samples), jnp.bfloat16),
            pltpu.VMEM((SLOTS, samples), jnp.bfloat16),
            pltpu.VMEM((TAPS, CHANNELS), jnp.float32),
            pltpu.VMEM((OUTER, INNER), jnp.float32),
            pltpu.VMEM((OUTER, INNER), jnp.float32),
            pltpu.VMEM((256, 256), jnp.bfloat16),
            pltpu.VMEM((2, many, OUTER, SLOTS, INNER), jnp.float32),
            pltpu.VMEM((2, SLOTS * (32 * many + 8), INNER), jnp.float32),
            pltpu.VMEM((2 * count, DEVICES * ROW_STRIDE, INNER), jnp.float32),
            pltpu.VMEM((DEVICES, SLOTS, 2 * count * INNER), jnp.bfloat16),
            pltpu.SemaphoreType.DMA((6 + 4 * len(messages),)),
        ],
        compiler_params=pltpu.CompilerParams(vmem_limit_bytes=58 * MIB),
        cost_estimate=pl.CostEstimate(
            flops=8 * 10**8 * count, bytes_accessed=16 * 10**6 * count, transcendentals=0
        ),
        interpret=interpret,
        name="spectra",
    )(vre, vim, taps, jnp.asarray(cos_t), jnp.asarray(sin_t), jnp.asarray(mat))


def quarter_kernel(wre, wim, slots, out, buf, names, chosen, sems):
    grp = lax.axis_index("grp")
    y_lo, core = grp // 2, grp % 2
    antennas, beams = wre.shape
    half = antennas // 2
    name_copy = pltpu.make_async_copy(slots.at[core], names, sems.at[4])
    name_copy.start()
    for y, source in ((0, wre), (1, wim)):

        @pl.when(y_lo == y)
        def _():
            for i in range(4):
                part = pl.ds(i * half // 2, half // 2)
                pltpu.make_async_copy(source.at[part], buf.at[part], sems.at[i]).start()
    name_copy.wait()
    row = names[...]

    def build(i, _):
        antenna = lax.broadcasted_iota(jnp.int32, (16, half), 0) + i * 16
        chosen[pl.ds(pl.multiple_of(i * 16, 16), 16), :] = jnp.where(antenna == row, 1.0, 0.0).astype(jnp.bfloat16)
        return 0
    lax.fori_loop(0, antennas // 16, build, 0, unroll=4)
    for y, source in ((0, wre), (1, wim)):

        @pl.when(y_lo == y)
        def _():
            for i in range(4):
                part = pl.ds(i * half // 2, half // 2)
                pltpu.make_async_copy(source.at[part], buf.at[part], sems.at[i]).wait()
    for j in range(0, beams, 256):
        w = buf[:, j : j + 256].astype(jnp.bfloat16)
        for k in range(0, half, 512):
            out[j : j + 256, k : k + 512] = lax.dot_general(
                w, chosen[:, k : k + 512], (((0,), (0,)), ((), ())), preferred_element_type=jnp.float32
            ).astype(jnp.bfloat16)


def quarter_of(wre, wim, antenna_map, interpret=False):
    antennas, beams = wre.shape
    half = antennas // 2
    return pl.pallas_call(
        quarter_kernel,
        in_specs=[pl.BlockSpec(memory_space=pltpu.HBM)] * 3,
        out_specs=pl.BlockSpec(memory_space=pltpu.VMEM),
        out_shape=jax.ShapeDtypeStruct((beams, half), jnp.bfloat16),
        scratch_shapes=[
            pltpu.VMEM((antennas, beams), jnp.float32),
            pltpu.VMEM((1, half), jnp.int32),
            pltpu.VMEM((antennas, half), jnp.bfloat16),
            pltpu.SemaphoreType.DMA((5,)),
        ],
        compiler_params=pltpu.CompilerParams(vmem_limit_bytes=58 * MIB),
        cost_estimate=pl.CostEstimate(flops=2 * 10**9, bytes_accessed=6 * 10**6, transcendentals=0),
        interpret=interpret,
        name="quarter",
    )(wre, wim, antenna_map.reshape(2, 1, half))


def pick_kernel(owners, offers, mine, other):
    core = lax.axis_index("grp") % 2
    mine[...] = offers[owners[core]]
    other[...] = offers[owners[1 - core]]


def pick_of(owners, offers, interpret=False):
    _, rows, columns = offers.shape
    return pl.pallas_call(
        pick_kernel,
        in_specs=[pl.BlockSpec(memory_space=pltpu.SMEM), pl.BlockSpec(memory_space=pltpu.VMEM)],
        out_specs=[pl.BlockSpec(memory_space=pltpu.VMEM)] * 2,
        out_shape=[jax.ShapeDtypeStruct((rows, columns), offers.dtype)] * 2,
        compiler_params=pltpu.CompilerParams(vmem_limit_bytes=8 * MIB),
        interpret=interpret,
        name="pick",
    )(owners, offers)


def join_kernel(axis, *refs):
    parts, out = refs[:-1], refs[-1]
    at = 0
    for part in parts:
        size = part.shape[axis]
        if axis == 0:
            out[at : at + size, :] = part[...]
        else:
            out[:, at : at + size] = part[...]
        at += size


def join_of(parts, axis, interpret=False):
    shape = list(parts[0].shape)
    shape[axis] = sum(p.shape[axis] for p in parts)
    return pl.pallas_call(
        functools.partial(join_kernel, axis),
        out_shape=jax.ShapeDtypeStruct(tuple(shape), parts[0].dtype),
        in_specs=[pl.BlockSpec(memory_space=pltpu.VMEM)] * len(parts),
        out_specs=pl.BlockSpec(memory_space=pltpu.VMEM),
        compiler_params=pltpu.CompilerParams(vmem_limit_bytes=8 * MIB),
        interpret=interpret,
        name="join",
    )(*parts)


def choose_matrix():
    chosen = np.zeros((2, 32, 3, 2, 2, 32), np.float32)
    for pair in range(2):
        for f1 in range(32):
            chosen[pair, f1, :, pair, :, f1] = 1.0
    return chosen.reshape(64, 384)


def products(core, part, spectra):
    half = part.shape[1] // 2
    near = pl.ds(pl.multiple_of(core * half, half), half)
    far = pl.ds(pl.multiple_of((1 - core) * half, half), half)
    left, right = part[:, :half], part[:, half:]
    return jnp.dot(left, spectra[near, :], preferred_element_type=jnp.float32) + jnp.dot(
        right, spectra[far, :], preferred_element_type=jnp.float32
    )


def early_kernel(w0, w1, za, out):
    core = lax.axis_index("grp") % 2
    n = w0.shape[0]
    for i, part in enumerate((w0, w1)):
        out[i * n : (i + 1) * n, :] = products(core, part, za)


def early_of(w0, w1, spectra, interpret=False):
    return pl.pallas_call(
        early_kernel,
        out_shape=jax.ShapeDtypeStruct((2 * w0.shape[0], 768), jnp.float32),
        in_specs=[pl.BlockSpec(memory_space=pltpu.VMEM)] * 3,
        out_specs=pl.BlockSpec(memory_space=pltpu.VMEM),
        compiler_params=pltpu.CompilerParams(vmem_limit_bytes=24 * MIB),
        cost_estimate=pl.CostEstimate(flops=17 * 10**8, bytes_accessed=8 * 10**6, transcendentals=0),
        interpret=interpret,
        name="early",
    )(w0, w1, spectra)


def beams_kernel(places, early, w2, w3, za, choose, out, sums):
    for k in range(32):
        at = pl.multiple_of(places[k], 16)
        sums[pl.ds(at, 16), :] = early[k * 16 : (k + 1) * 16, :]
    core = lax.axis_index("grp") % 2
    for i, part in enumerate((w2, w3)):
        result = products(core, part, za)
        for k in range(16):
            at = pl.multiple_of(places[(i + 2) * 16 + k], 16)
            sums[pl.ds(at, 16), :] = result[k * 16 : (k + 1) * 16, :]
    beams = sums.shape[0] // 2
    powers = []
    for g in range(3):
        re_lanes, im_lanes = slice(g * 256, g * 256 + 128), slice(g * 256 + 128, g * 256 + 256)
        re = sums[:beams, re_lanes] - sums[beams:, im_lanes]
        im = sums[beams:, re_lanes] + sums[:beams, im_lanes]
        powers.append(re * re + im * im)
    total = lax.dot_general(
        choose[...],
        jnp.concatenate(powers, axis=1),
        (((1,), (1,)), ((), ())),
        preferred_element_type=jnp.float32,
        precision=lax.Precision.HIGHEST,
    )
    out[...] = total * (1.0 / SPECTRA)


def beams_of(places, early, w2, w3, spectra, interpret=False):
    rows = early.shape[0] + 2 * w2.shape[0]
    return pl.pallas_call(
        beams_kernel,
        out_shape=jax.ShapeDtypeStruct((64, rows // 2), jnp.float32),
        in_specs=[pl.BlockSpec(memory_space=pltpu.SMEM)] + [pl.BlockSpec(memory_space=pltpu.VMEM)] * 5,
        out_specs=pl.BlockSpec(memory_space=pltpu.VMEM),
        scratch_shapes=[pltpu.VMEM((rows, 768), jnp.float32)],
        compiler_params=pltpu.CompilerParams(vmem_limit_bytes=32 * MIB),
        cost_estimate=pl.CostEstimate(flops=17 * 10**8, bytes_accessed=8 * 10**6, transcendentals=0),
        interpret=interpret,
        name="beams",
    )(places, early, w2, w3, spectra, jnp.asarray(choose_matrix()))


def index_of(z, x, y, core):
    return ((y % 2) * 2 + core) * 32 + (z % 4) * 8 + (x % 4) * 2 + (y % 4) // 2


EVERY = [(z, x, y, c) for z in range(4) for x in range(4) for y in range(4) for c in range(2)]
ORDER = (("y", "x", "z"), ("z", "y", "x"))
SHIFTS = (0, -1, 1, 2)


def permutation(stage, shift):
    pairs = []
    for z, x, y, core in EVERY:
        axis = ORDER[core][stage]
        source = {"z": z, "x": x, "y": y}
        source[axis] += shift
        pairs.append((index_of(source["z"], source["x"], source["y"], core), index_of(z, x, y, core)))
    return pairs


def gather_stage(block, stage):
    return [block] + [lax.ppermute(block, ALL, permutation(stage, shift)) for shift in SHIFTS[1:]]


def plane_groups():
    groups = [[index_of(z, x, y, 0) for y in range(4) for x in range(4)] for z in range(4)]
    return groups + [[index_of(z, x, y, 1) for y in range(4) for z in range(4)] for x in range(4)]


def block_places(grp, dev):
    core = grp % 2
    z, x = dev // 8, dev // 2 % 4
    k = np.arange(64)
    shift, y, other = np.array(SHIFTS)[k // 16], k % 16 // 4, k % 4
    fz = jnp.where(core == 0, (z + shift + 4) % 4, other)
    fx = jnp.where(core == 0, other, (x + shift + 4) % 4)
    return (((y % 2) * 32 + fz * 8 + fx * 2 + y // 2) * 16).astype(jnp.int32)


SWAP = [(0, 1), (1, 0), (2, 3), (3, 2)]


def on_device(voltage_real, voltage_imaginary, filter_taps, weights_re, weights_im, owners, antenna_map):
    grp, dev = lax.axis_index("grp"), lax.axis_index("dev")
    core = grp % 2

    quarter = quarter_of(weights_re[0], weights_im[0], antenna_map)
    offers = lax.all_to_all(quarter.reshape(32, 16, -1), "dev", split_axis=0, concat_axis=0, tiled=True)

    volts = (voltage_real, voltage_imaginary, filter_taps)
    quarter, *volts = lax.optimization_barrier((quarter, *volts))
    (message,) = spectra_of(MESSAGES, *volts)
    message, offers = lax.optimization_barrier((message, offers))
    spectra = lax.all_to_all(message, ALL, split_axis=0, concat_axis=0, tiled=True)
    spectra = spectra.reshape(DEVICES * SLOTS, -1)

    mine, other = pick_of(owners, offers)
    other = lax.ppermute(other, "grp", SWAP)
    block = join_of([mine, other], 1)
    block = lax.all_gather(block, ALL, axis=0, tiled=True, axis_index_groups=plane_groups())
    parts = gather_stage(block, 2)

    early = early_of(parts[0], parts[3], spectra)
    places = block_places(grp, dev)
    places = jnp.concatenate([places[:16], places[48:], places[16:48]])
    power = beams_of(places, early, parts[1], parts[2], spectra)
    power = power.reshape(2, 32, -1)
    own = jnp.where(core == 0, power[0], power[1])
    given = jnp.where(core == 0, power[1], power[0])
    taken = lax.ppermute(given, "grp", SWAP)
    return jnp.where(core == 0, jnp.stack([own, taken]), jnp.stack([taken, own]))


def solution(mesh):
    return jax.shard_map(
        on_device,
        mesh=mesh,
        in_specs=(
            P(("grp", "dev"), None),
            P(("grp", "dev"), None),
            P(),
            P("dev", None, None),
            P("dev", None, None),
            P(),
            P(),
        ),
        out_specs=P(None, ("grp", "dev"), None),
        check_vma=False,
    )
```

```python
import functools
import math

import jax
import jax.numpy as jnp
import numpy as np
from jax import lax
from jax.experimental import pallas as pl
from jax.experimental.pallas import tpu as pltpu
from jax.sharding import PartitionSpec as P

CHANNELS = 4096
TAPS = 16
SPECTRA = 6
STEPS = 2
FRAMES = STEPS * SPECTRA
BLOCKS = FRAMES + TAPS - 1
OUTER = 32
INNER = 128
SLOTS = 16
DEVICES = 128
ROW_STRIDE = 24
GROUPS = ((0, 1, 6, 7), (2, 3, 8, 9), (4, 5, 10, 11))
MESSAGES = ((0, 1, 2),)
ALL = ("grp", "dev")
MIB = 1 << 20


def twist_tables():
    products = np.outer(np.arange(OUTER), np.arange(INNER)) % CHANNELS
    angles = products * (2.0 * math.pi / CHANNELS)
    return np.cos(angles).astype(np.float32), np.sin(angles).astype(np.float32)


def inner_matrix():
    products = np.outer(np.arange(INNER), np.arange(INNER)) % INNER
    angles = products * (2.0 * math.pi / INNER)
    norm = CHANNELS ** (-0.5)
    c, s = np.cos(angles) * norm, np.sin(angles) * norm
    return np.block([[c, s], [-s, c]]).astype(np.float32)


def small_fft(points):
    count = len(points)
    if count == 1:
        return points
    even = small_fft(points[0::2])
    odd = small_fft(points[1::2])
    half = count // 2
    result = [None] * count
    for k in range(half):
        er, ei = even[k]
        xr, xi = odd[k]
        if k == 0:
            tr, ti = xr, xi
        elif 4 * k == count:
            tr, ti = xi, -xr
        elif 8 * k == count:
            r = math.sqrt(0.5)
            tr, ti = (xr + xi) * r, (xi - xr) * r
        elif 8 * k == 3 * count:
            r = math.sqrt(0.5)
            tr, ti = (xi - xr) * r, (xr + xi) * (-r)
        else:
            c = math.cos(2.0 * math.pi * k / count)
            s = math.sin(2.0 * math.pi * k / count)
            tr, ti = xr * c + xi * s, xi * c - xr * s
        result[k] = (er + tr, ei + ti)
        result[k + half] = (er - tr, ei - ti)
    return result


def spectra_kernel(messages, *refs):
    groups = [group for message in messages for group in message]
    count = len(groups)
    sources, outs = refs[:6], refs[6 : 6 + len(messages)]
    vre, vim, taps, cos_t, sin_t, mat, frames, turned, packed, ready, sems = refs[6 + len(messages) :]
    chosen = [u for group in groups for u in GROUPS[group]]
    first, last = min(chosen), max(chosen) + TAPS
    rows_per_slot = 32 * len(chosen)
    slot_stride = rows_per_slot + 8

    loads = []
    for i in (2, 0, 1, 3, 4, 5):
        source = sources[i]
        if i < 2:
            source = source.at[:, first * CHANNELS : last * CHANNELS]
        loads.append(pltpu.make_async_copy(source, (vre, vim, taps, cos_t, sin_t, mat)[i], sems.at[i]))
        loads[-1].start()
    loads[0].wait()

    for c, volts in ((0, vre), (1, vim)):
        loads[1 + c].wait()

        def fir(n1, _, c=c, volts=volts):
            rows = [taps[k : k + 1, pl.ds(pl.multiple_of(n1 * INNER, INNER), INNER)] for k in range(TAPS)]
            needed = sorted({u + k for u in chosen for k in range(TAPS)})
            window = {
                b: volts[
                    :, pl.ds(pl.multiple_of((b - first) * CHANNELS + n1 * INNER, INNER), INNER)
                ].astype(jnp.float32)
                for b in needed
            }
            for i, u in enumerate(chosen):
                total = window[u] * rows[0]
                for k in range(1, TAPS):
                    total = total + window[u + k] * rows[k]
                frames[c, i, n1] = total
            return 0

        lax.fori_loop(0, OUTER, fir, 0)

    for load in loads[3:]:
        load.wait()

    def outer(i, _):
        u = i // 2
        low = pl.multiple_of((i % 2) * 8, 8)
        points = [
            (frames[0, u, n1, pl.ds(low, 8), :], frames[1, u, n1, pl.ds(low, 8), :]) for n1 in range(OUTER)
        ]
        points = small_fft(points)
        for f1 in range(OUTER):
            re, im = points[f1]
            if f1:
                c, d = cos_t[f1 : f1 + 1, :], sin_t[f1 : f1 + 1, :]
                re, im = re * c + im * d, im * c - re * d
            at = low * slot_stride + u * 32 + f1
            turned[0, pl.ds(at, 8, stride=slot_stride), :] = re
            turned[1, pl.ds(at, 8, stride=slot_stride), :] = im
        return 0

    lax.fori_loop(0, 2 * len(chosen), outer, 0)

    matrix, matrix_low = mat[:256, :], mat[256:, :]
    lane = lax.broadcasted_iota(jnp.int32, (32, INNER), 1)

    def inner(a, _):
        base = pl.multiple_of(a * slot_stride, 8)
        rows = jnp.concatenate(
            [turned[0, pl.ds(base, rows_per_slot), :], turned[1, pl.ds(base, rows_per_slot), :]], axis=1
        )
        high = rows.astype(jnp.bfloat16)
        low = (rows - high.astype(jnp.float32)).astype(jnp.bfloat16)

        def product(left, right):
            return lax.dot_general(left, right, (((1,), (1,)), ((), ())), preferred_element_type=jnp.float32)

        spec = product(matrix, high) + (product(matrix_low, high) + product(matrix, low))
        for g in range(count):
            for y in range(2):
                for c in range(2):
                    to = [pl.ds((y * 2 + s) * 32 * ROW_STRIDE + a, 32, stride=ROW_STRIDE) for s in range(2)]
                    at = [c * 128 + (y * 2 + pair) * 32 for pair in range(2)]
                    mixed = [spec[f2 : f2 + 32, g * INNER : (g + 1) * INNER] for f2 in at]
                    packed[g * 2 + c, to[0], :] = jnp.where(lane < 64, mixed[0], pltpu.roll(mixed[1], 64, 1))
                    packed[g * 2 + c, to[1], :] = jnp.where(lane < 64, pltpu.roll(mixed[0], 64, 1), mixed[1])
        return 0

    lax.fori_loop(0, SLOTS, inner, 0, unroll=4)

    stores = []
    tile = 0
    for message, to in zip(messages, outs):
        for quarter in range(4):

            def emit(p, _, tile=tile, wide=2 * len(message)):
                for i in range(tile, tile + wide):
                    ready[p, :, i * INNER : (i + 1) * INNER] = packed[
                        i, pl.ds(pl.multiple_of(p * ROW_STRIDE, 8), SLOTS), :
                    ].astype(jnp.bfloat16)
                return 0

            lax.fori_loop(quarter * 32, quarter * 32 + 32, emit, 0, unroll=4)
            part = pl.ds(quarter * 32, 32)
            lanes = slice(tile * INNER, (tile + 2 * len(message)) * INNER)
            stores.append(
                pltpu.make_async_copy(ready.at[part, :, lanes], to.at[part], sems.at[6 + len(stores)])
            )
            stores[-1].start()
        tile += 2 * len(message)
    for store in stores:
        store.wait()


def spectra_of(messages, vre, vim, taps, interpret=False):
    cos_t, sin_t = twist_tables()
    mat = inner_matrix()
    high = mat.astype(jnp.bfloat16)
    mat = np.concatenate([high, (mat - high.astype(np.float32)).astype(jnp.bfloat16)])
    groups = [group for message in messages for group in message]
    count = len(groups)
    many = 4 * count
    chosen = [u for group in groups for u in GROUPS[group]]
    samples = (max(chosen) + TAPS - min(chosen)) * CHANNELS
    return pl.pallas_call(
        functools.partial(spectra_kernel, messages),
        out_shape=[jax.ShapeDtypeStruct((DEVICES, SLOTS, 2 * INNER * len(m)), jnp.bfloat16) for m in messages],
        in_specs=[pl.BlockSpec(memory_space=pltpu.HBM)] * 6,
        out_specs=[pl.BlockSpec(memory_space=pltpu.HBM)] * len(messages),
        scratch_shapes=[
            pltpu.VMEM((SLOTS, samples), jnp.bfloat16),
            pltpu.VMEM((SLOTS, samples), jnp.bfloat16),
            pltpu.VMEM((TAPS, CHANNELS), jnp.float32),
            pltpu.VMEM((OUTER, INNER), jnp.float32),
            pltpu.VMEM((OUTER, INNER), jnp.float32),
            pltpu.VMEM((512, 256), jnp.bfloat16),
            pltpu.VMEM((2, many, OUTER, SLOTS, INNER), jnp.float32),
            pltpu.VMEM((2, SLOTS * (32 * many + 8), INNER), jnp.float32),
            pltpu.VMEM((2 * count, DEVICES * ROW_STRIDE, INNER), jnp.float32),
            pltpu.VMEM((DEVICES, SLOTS, 2 * count * INNER), jnp.bfloat16),
            pltpu.SemaphoreType.DMA((6 + 4 * len(messages),)),
        ],
        compiler_params=pltpu.CompilerParams(vmem_limit_bytes=58 * MIB),
        cost_estimate=pl.CostEstimate(
            flops=8 * 10**8 * count, bytes_accessed=16 * 10**6 * count, transcendentals=0
        ),
        interpret=interpret,
        name="spectra",
    )(vre, vim, taps, jnp.asarray(cos_t), jnp.asarray(sin_t), jnp.asarray(mat))


def quarter_kernel(wre, wim, slots, out, buf, names, chosen, sems):
    grp = lax.axis_index("grp")
    y_lo, core = grp // 2, grp % 2
    antennas, beams = wre.shape
    half = antennas // 2
    name_copy = pltpu.make_async_copy(slots.at[core], names, sems.at[4])
    name_copy.start()
    for y, source in ((0, wre), (1, wim)):

        @pl.when(y_lo == y)
        def _():
            for i in range(4):
                part = pl.ds(i * half // 2, half // 2)
                pltpu.make_async_copy(source.at[part], buf.at[part], sems.at[i]).start()
    name_copy.wait()
    row = names[...]

    def build(i, _):
        antenna = lax.broadcasted_iota(jnp.int32, (16, half), 0) + i * 16
        chosen[pl.ds(pl.multiple_of(i * 16, 16), 16), :] = jnp.where(antenna == row, 1.0, 0.0).astype(jnp.bfloat16)
        return 0
    lax.fori_loop(0, antennas // 16, build, 0, unroll=4)
    for y, source in ((0, wre), (1, wim)):

        @pl.when(y_lo == y)
        def _():
            for i in range(4):
                part = pl.ds(i * half // 2, half // 2)
                pltpu.make_async_copy(source.at[part], buf.at[part], sems.at[i]).wait()
    for j in range(0, beams, 256):
        w = buf[:, j : j + 256].astype(jnp.bfloat16)
        for k in range(0, half, 512):
            out[j : j + 256, k : k + 512] = lax.dot_general(
                w, chosen[:, k : k + 512], (((0,), (0,)), ((), ())), preferred_element_type=jnp.float32
            ).astype(jnp.bfloat16)


def quarter_of(wre, wim, antenna_map, interpret=False):
    antennas, beams = wre.shape
    half = antennas // 2
    return pl.pallas_call(
        quarter_kernel,
        in_specs=[pl.BlockSpec(memory_space=pltpu.HBM)] * 3,
        out_specs=pl.BlockSpec(memory_space=pltpu.VMEM),
        out_shape=jax.ShapeDtypeStruct((beams, half), jnp.bfloat16),
        scratch_shapes=[
            pltpu.VMEM((antennas, beams), jnp.float32),
            pltpu.VMEM((1, half), jnp.int32),
            pltpu.VMEM((antennas, half), jnp.bfloat16),
            pltpu.SemaphoreType.DMA((5,)),
        ],
        compiler_params=pltpu.CompilerParams(vmem_limit_bytes=58 * MIB),
        cost_estimate=pl.CostEstimate(flops=2 * 10**9, bytes_accessed=6 * 10**6, transcendentals=0),
        interpret=interpret,
        name="quarter",
    )(wre, wim, antenna_map.reshape(2, 1, half))


def pick_kernel(owners, offers, mine, other, sems):
    core = lax.axis_index("grp") % 2
    copies = [
        pltpu.make_async_copy(offers.at[owners[core]], mine, sems.at[0]),
        pltpu.make_async_copy(offers.at[owners[1 - core]], other, sems.at[1]),
    ]
    for copy in copies:
        copy.start()
    for copy in copies:
        copy.wait()


def pick_of(owners, offers, interpret=False):
    _, rows, columns = offers.shape
    return pl.pallas_call(
        pick_kernel,
        in_specs=[pl.BlockSpec(memory_space=pltpu.SMEM), pl.BlockSpec(memory_space=pltpu.HBM)],
        out_specs=[pl.BlockSpec(memory_space=pltpu.VMEM)] * 2,
        out_shape=[jax.ShapeDtypeStruct((rows, columns), offers.dtype)] * 2,
        scratch_shapes=[pltpu.SemaphoreType.DMA((2,))],
        compiler_params=pltpu.CompilerParams(vmem_limit_bytes=58 * MIB),
        interpret=interpret,
        name="pick",
    )(owners, offers)


def join_kernel(axis, *refs):
    parts, out = refs[:-1], refs[-1]
    at = 0
    for part in parts:
        size = part.shape[axis]
        if axis == 0:
            out[at : at + size, :] = part[...]
        else:
            out[:, at : at + size] = part[...]
        at += size


def join_of(parts, axis, interpret=False):
    shape = list(parts[0].shape)
    shape[axis] = sum(p.shape[axis] for p in parts)
    return pl.pallas_call(
        functools.partial(join_kernel, axis),
        out_shape=jax.ShapeDtypeStruct(tuple(shape), parts[0].dtype),
        in_specs=[pl.BlockSpec(memory_space=pltpu.VMEM)] * len(parts),
        out_specs=pl.BlockSpec(memory_space=pltpu.VMEM),
        compiler_params=pltpu.CompilerParams(vmem_limit_bytes=8 * MIB),
        interpret=interpret,
        name="join",
    )(*parts)


def choose_matrix():
    chosen = np.zeros((2, 32, 3, 2, 2, 32), np.float32)
    for pair in range(2):
        for f1 in range(32):
            chosen[pair, f1, :, pair, :, f1] = 1.0
    return chosen.reshape(64, 384)


def products(core, part, spectra):
    half = part.shape[1] // 2
    near = pl.ds(pl.multiple_of(core * half, half), half)
    far = pl.ds(pl.multiple_of((1 - core) * half, half), half)
    left, right = part[:, :half], part[:, half:]
    return jnp.dot(left, spectra[near, :], preferred_element_type=jnp.float32) + jnp.dot(
        right, spectra[far, :], preferred_element_type=jnp.float32
    )


def early_kernel(w0, w1, za, out):
    core = lax.axis_index("grp") % 2
    n = w0.shape[0]
    for i, part in enumerate((w0, w1)):
        out[i * n : (i + 1) * n, :] = products(core, part, za)


def early_of(w0, w1, spectra, interpret=False):
    return pl.pallas_call(
        early_kernel,
        out_shape=jax.ShapeDtypeStruct((2 * w0.shape[0], 768), jnp.float32),
        in_specs=[pl.BlockSpec(memory_space=pltpu.VMEM)] * 3,
        out_specs=pl.BlockSpec(memory_space=pltpu.VMEM),
        compiler_params=pltpu.CompilerParams(vmem_limit_bytes=24 * MIB),
        cost_estimate=pl.CostEstimate(flops=17 * 10**8, bytes_accessed=8 * 10**6, transcendentals=0),
        interpret=interpret,
        name="early",
    )(w0, w1, spectra)


def beams_kernel(places, early, w2, w3, za, choose, own, given, sums):
    for k in range(32):
        at = pl.multiple_of(places[k], 16)
        sums[pl.ds(at, 16), :] = early[k * 16 : (k + 1) * 16, :]
    core = lax.axis_index("grp") % 2
    for i, part in enumerate((w2, w3)):
        result = products(core, part, za)
        for k in range(16):
            at = pl.multiple_of(places[(i + 2) * 16 + k], 16)
            sums[pl.ds(at, 16), :] = result[k * 16 : (k + 1) * 16, :]
    beams = sums.shape[0] // 2
    powers = []
    for g in range(3):
        re_lanes, im_lanes = slice(g * 256, g * 256 + 128), slice(g * 256 + 128, g * 256 + 256)
        re = sums[:beams, re_lanes] - sums[beams:, im_lanes]
        im = sums[beams:, re_lanes] + sums[:beams, im_lanes]
        powers.append(re * re + im * im)
    total = lax.dot_general(
        choose[...],
        jnp.concatenate(powers, axis=1),
        (((1,), (1,)), ((), ())),
        preferred_element_type=jnp.float32,
        precision=lax.Precision.HIGHEST,
    )
    total = total * (1.0 / SPECTRA)
    own[...] = jnp.where(core == 0, total[:32], total[32:])
    given[...] = jnp.where(core == 0, total[32:], total[:32])


def beams_of(places, early, w2, w3, spectra, interpret=False):
    rows = early.shape[0] + 2 * w2.shape[0]
    return pl.pallas_call(
        beams_kernel,
        out_shape=[jax.ShapeDtypeStruct((32, rows // 2), jnp.float32)] * 2,
        in_specs=[pl.BlockSpec(memory_space=pltpu.SMEM)] + [pl.BlockSpec(memory_space=pltpu.VMEM)] * 5,
        out_specs=[pl.BlockSpec(memory_space=pltpu.VMEM)] * 2,
        scratch_shapes=[pltpu.VMEM((rows, 768), jnp.float32)],
        compiler_params=pltpu.CompilerParams(vmem_limit_bytes=32 * MIB),
        cost_estimate=pl.CostEstimate(flops=17 * 10**8, bytes_accessed=8 * 10**6, transcendentals=0),
        interpret=interpret,
        name="beams",
    )(places, early, w2, w3, spectra, jnp.asarray(choose_matrix()))


def index_of(z, x, y, core):
    return ((y % 2) * 2 + core) * 32 + (z % 4) * 8 + (x % 4) * 2 + (y % 4) // 2


EVERY = [(z, x, y, c) for z in range(4) for x in range(4) for y in range(4) for c in range(2)]
ORDER = (("y", "x", "z"), ("z", "y", "x"))
SHIFTS = (0, -1, 1, 2)


def permutation(stage, shift):
    pairs = []
    for z, x, y, core in EVERY:
        axis = ORDER[core][stage]
        source = {"z": z, "x": x, "y": y}
        source[axis] += shift
        pairs.append((index_of(source["z"], source["x"], source["y"], core), index_of(z, x, y, core)))
    return pairs


def gather_stage(block, stage):
    return [block] + [lax.ppermute(block, ALL, permutation(stage, shift)) for shift in SHIFTS[1:]]


def block_places(grp, dev):
    core = grp % 2
    z, x, y = dev // 8, dev // 2 % 4, dev % 2 * 2 + grp // 2
    k = np.arange(64)
    shift = np.array(SHIFTS)
    first, second, third = shift[k % 4], shift[k // 4 % 4], shift[k // 16]
    by_core = []
    for order in ORDER:
        moved = dict(zip(order, (first, second, third)))
        by_core.append([moved[axis] for axis in "zxy"])
    is_first = core == 0
    mz, mx, my = [jnp.where(is_first, jnp.asarray(a), jnp.asarray(b)) for a, b in zip(*by_core)]
    fz, fx, fy = (z + mz + 4) % 4, (x + mx + 4) % 4, (y + my + 4) % 4
    return (((fy % 2) * 32 + fz * 8 + fx * 2 + fy // 2) * 16).astype(jnp.int32)


SWAP = [(0, 1), (1, 0), (2, 3), (3, 2)]


def on_device(voltage_real, voltage_imaginary, filter_taps, weights_re, weights_im, owners, antenna_map):
    grp, dev = lax.axis_index("grp"), lax.axis_index("dev")
    core = grp % 2

    quarter = quarter_of(weights_re[0], weights_im[0], antenna_map)
    offers = lax.all_to_all(quarter.reshape(32, 16, -1), "dev", split_axis=0, concat_axis=0, tiled=True)

    volts = (voltage_real, voltage_imaginary, filter_taps)
    quarter, *volts = lax.optimization_barrier((quarter, *volts))
    (message,) = spectra_of(MESSAGES, *volts)
    message, offers = lax.optimization_barrier((message, offers))
    spectra = lax.all_to_all(message, ALL, split_axis=0, concat_axis=0, tiled=True)
    spectra = spectra.reshape(DEVICES * SLOTS, -1)

    mine, other = pick_of(owners, offers)
    other = lax.ppermute(other, "grp", SWAP)
    block = join_of([mine, other], 1)
    block = join_of(gather_stage(block, 0), 0)
    block = join_of(gather_stage(block, 1), 0)
    parts = gather_stage(block, 2)

    early = early_of(parts[0], parts[3], spectra)
    places = block_places(grp, dev)
    places = jnp.concatenate([places[:16], places[48:], places[16:48]])
    own, given = beams_of(places, early, parts[1], parts[2], spectra)
    taken = lax.ppermute(given, "grp", SWAP)
    return jnp.where(core == 0, jnp.stack([own, taken]), jnp.stack([taken, own]))


def solution(mesh):
    return jax.shard_map(
        on_device,
        mesh=mesh,
        in_specs=(
            P(("grp", "dev"), None),
            P(("grp", "dev"), None),
            P(),
            P("dev", None, None),
            P("dev", None, None),
            P(),
            P(),
        ),
        out_specs=P(None, ("grp", "dev"), None),
        check_vma=False,
    )
```

```python
import functools
import math

import jax
import jax.numpy as jnp
import numpy as np
from jax import lax
from jax.experimental import pallas as pl
from jax.experimental.pallas import tpu as pltpu
from jax.sharding import PartitionSpec as P

CHANNELS = 4096
TAPS = 16
SPECTRA = 6
STEPS = 2
FRAMES = STEPS * SPECTRA
BLOCKS = FRAMES + TAPS - 1
OUTER = 32
INNER = 128
SLOTS = 16
DEVICES = 128
ROW_STRIDE = 24
GROUPS = ((0, 1, 6, 7), (2, 3, 8, 9), (4, 5, 10, 11))
MESSAGES = ((0, 1, 2),)
ALL = ("grp", "dev")
MIB = 1 << 20


def twist_tables():
    products = np.outer(np.arange(OUTER), np.arange(INNER)) % CHANNELS
    angles = products * (2.0 * math.pi / CHANNELS)
    return np.cos(angles).astype(np.float32), np.sin(angles).astype(np.float32)


def inner_matrix():
    products = np.outer(np.arange(INNER), np.arange(INNER)) % INNER
    angles = products * (2.0 * math.pi / INNER)
    norm = CHANNELS ** (-0.5)
    c, s = np.cos(angles) * norm, np.sin(angles) * norm
    return np.block([[c, s], [-s, c]]).astype(np.float32)


def small_fft(points):
    count = len(points)
    if count == 1:
        return points
    even = small_fft(points[0::2])
    odd = small_fft(points[1::2])
    half = count // 2
    result = [None] * count
    for k in range(half):
        er, ei = even[k]
        xr, xi = odd[k]
        if k == 0:
            tr, ti = xr, xi
        elif 4 * k == count:
            tr, ti = xi, -xr
        elif 8 * k == count:
            r = math.sqrt(0.5)
            tr, ti = (xr + xi) * r, (xi - xr) * r
        elif 8 * k == 3 * count:
            r = math.sqrt(0.5)
            tr, ti = (xi - xr) * r, (xr + xi) * (-r)
        else:
            c = math.cos(2.0 * math.pi * k / count)
            s = math.sin(2.0 * math.pi * k / count)
            tr, ti = xr * c + xi * s, xi * c - xr * s
        result[k] = (er + tr, ei + ti)
        result[k + half] = (er - tr, ei - ti)
    return result


def spectra_kernel(messages, *refs):
    groups = [group for message in messages for group in message]
    count = len(groups)
    sources, outs = refs[:6], refs[6 : 6 + len(messages)]
    vre, vim, taps, cos_t, sin_t, mat, frames, turned, packed, ready, sems = refs[6 + len(messages) :]
    chosen = [u for group in groups for u in GROUPS[group]]
    first, last = min(chosen), max(chosen) + TAPS
    rows_per_slot = 32 * len(chosen)
    slot_stride = rows_per_slot + 8

    loads = []
    for i in (2, 0, 1, 3, 4, 5):
        source = sources[i]
        if i < 2:
            source = source.at[:, first * CHANNELS : last * CHANNELS]
        loads.append(pltpu.make_async_copy(source, (vre, vim, taps, cos_t, sin_t, mat)[i], sems.at[i]))
        loads[-1].start()
    loads[0].wait()

    for c, volts in ((0, vre), (1, vim)):
        loads[1 + c].wait()

        def fir(n1, _, c=c, volts=volts):
            rows = [taps[k : k + 1, pl.ds(pl.multiple_of(n1 * INNER, INNER), INNER)] for k in range(TAPS)]
            needed = sorted({u + k for u in chosen for k in range(TAPS)})
            window = {
                b: volts[
                    :, pl.ds(pl.multiple_of((b - first) * CHANNELS + n1 * INNER, INNER), INNER)
                ].astype(jnp.float32)
                for b in needed
            }
            for i, u in enumerate(chosen):
                total = window[u] * rows[0]
                for k in range(1, TAPS):
                    total = total + window[u + k] * rows[k]
                frames[c, i, n1] = total
            return 0

        lax.fori_loop(0, OUTER, fir, 0, unroll=2)

    for load in loads[3:]:
        load.wait()

    def outer(i, _):
        u = i // 2
        low = pl.multiple_of((i % 2) * 8, 8)
        points = [
            (frames[0, u, n1, pl.ds(low, 8), :], frames[1, u, n1, pl.ds(low, 8), :]) for n1 in range(OUTER)
        ]
        points = small_fft(points)
        for f1 in range(OUTER):
            re, im = points[f1]
            if f1:
                c, d = cos_t[f1 : f1 + 1, :], sin_t[f1 : f1 + 1, :]
                re, im = re * c + im * d, im * c - re * d
            at = low * slot_stride + u * 32 + f1
            turned[0, pl.ds(at, 8, stride=slot_stride), :] = re
            turned[1, pl.ds(at, 8, stride=slot_stride), :] = im
        return 0

    lax.fori_loop(0, 2 * len(chosen), outer, 0, unroll=2)

    matrix = mat[...]
    lane = lax.broadcasted_iota(jnp.int32, (32, INNER), 1)

    def inner(a, _):
        base = pl.multiple_of(a * slot_stride, 8)
        rows = jnp.concatenate(
            [turned[0, pl.ds(base, rows_per_slot), :], turned[1, pl.ds(base, rows_per_slot), :]], axis=1
        ).astype(jnp.bfloat16)
        spec = lax.dot_general(
            matrix, rows, (((1,), (1,)), ((), ())), preferred_element_type=jnp.float32
        )
        for g in range(count):
            for y in range(2):
                for c in range(2):
                    to = [pl.ds((y * 2 + s) * 32 * ROW_STRIDE + a, 32, stride=ROW_STRIDE) for s in range(2)]
                    at = [c * 128 + (y * 2 + pair) * 32 for pair in range(2)]
                    mixed = [spec[f2 : f2 + 32, g * INNER : (g + 1) * INNER] for f2 in at]
                    packed[g * 2 + c, to[0], :] = jnp.where(lane < 64, mixed[0], pltpu.roll(mixed[1], 64, 1))
                    packed[g * 2 + c, to[1], :] = jnp.where(lane < 64, pltpu.roll(mixed[0], 64, 1), mixed[1])
        return 0

    lax.fori_loop(0, SLOTS, inner, 0, unroll=8)

    stores = []
    tile = 0
    for message, to in zip(messages, outs):
        for quarter in range(4):

            def emit(p, _, tile=tile, wide=2 * len(message)):
                for i in range(tile, tile + wide):
                    ready[p, :, i * INNER : (i + 1) * INNER] = packed[
                        i, pl.ds(pl.multiple_of(p * ROW_STRIDE, 8), SLOTS), :
                    ].astype(jnp.bfloat16)
                return 0

            lax.fori_loop(quarter * 32, quarter * 32 + 32, emit, 0, unroll=4)
            part = pl.ds(quarter * 32, 32)
            lanes = slice(tile * INNER, (tile + 2 * len(message)) * INNER)
            stores.append(
                pltpu.make_async_copy(ready.at[part, :, lanes], to.at[part], sems.at[6 + len(stores)])
            )
            stores[-1].start()
        tile += 2 * len(message)
    for store in stores:
        store.wait()


def spectra_of(messages, vre, vim, taps, interpret=False):
    cos_t, sin_t = twist_tables()
    mat = inner_matrix().astype(jnp.bfloat16)
    groups = [group for message in messages for group in message]
    count = len(groups)
    many = 4 * count
    chosen = [u for group in groups for u in GROUPS[group]]
    samples = (max(chosen) + TAPS - min(chosen)) * CHANNELS
    return pl.pallas_call(
        functools.partial(spectra_kernel, messages),
        out_shape=[jax.ShapeDtypeStruct((DEVICES, SLOTS, 2 * INNER * len(m)), jnp.bfloat16) for m in messages],
        in_specs=[pl.BlockSpec(memory_space=pltpu.HBM)] * 6,
        out_specs=[pl.BlockSpec(memory_space=pltpu.HBM)] * len(messages),
        scratch_shapes=[
            pltpu.VMEM((SLOTS, samples), jnp.bfloat16),
            pltpu.VMEM((SLOTS, samples), jnp.bfloat16),
            pltpu.VMEM((TAPS, CHANNELS), jnp.float32),
            pltpu.VMEM((OUTER, INNER), jnp.float32),
            pltpu.VMEM((OUTER, INNER), jnp.float32),
            pltpu.VMEM((256, 256), jnp.bfloat16),
            pltpu.VMEM((2, many, OUTER, SLOTS, INNER), jnp.float32),
            pltpu.VMEM((2, SLOTS * (32 * many + 8), INNER), jnp.float32),
            pltpu.VMEM((2 * count, DEVICES * ROW_STRIDE, INNER), jnp.float32),
            pltpu.VMEM((DEVICES, SLOTS, 2 * count * INNER), jnp.bfloat16),
            pltpu.SemaphoreType.DMA((6 + 4 * len(messages),)),
        ],
        compiler_params=pltpu.CompilerParams(vmem_limit_bytes=58 * MIB),
        cost_estimate=pl.CostEstimate(
            flops=8 * 10**8 * count, bytes_accessed=16 * 10**6 * count, transcendentals=0
        ),
        interpret=interpret,
        name="spectra",
    )(vre, vim, taps, jnp.asarray(cos_t), jnp.asarray(sin_t), jnp.asarray(mat))


def quarter_kernel(wre, wim, slots, out, buf, names, chosen, sems):
    grp = lax.axis_index("grp")
    y_lo, core = grp // 2, grp % 2
    antennas, beams = wre.shape
    half = antennas // 2
    name_copy = pltpu.make_async_copy(slots.at[core], names, sems.at[4])
    name_copy.start()
    for y, source in ((0, wre), (1, wim)):

        @pl.when(y_lo == y)
        def _():
            for i in range(4):
                part = pl.ds(i * half // 2, half // 2)
                pltpu.make_async_copy(source.at[part], buf.at[part], sems.at[i]).start()
    name_copy.wait()
    row = names[...]

    def build(i, _):
        antenna = lax.broadcasted_iota(jnp.int32, (16, half), 0) + i * 16
        chosen[pl.ds(pl.multiple_of(i * 16, 16), 16), :] = jnp.where(antenna == row, 1.0, 0.0).astype(jnp.bfloat16)
        return 0
    lax.fori_loop(0, antennas // 16, build, 0, unroll=4)
    for y, source in ((0, wre), (1, wim)):

        @pl.when(y_lo == y)
        def _():
            for i in range(4):
                part = pl.ds(i * half // 2, half // 2)
                pltpu.make_async_copy(source.at[part], buf.at[part], sems.at[i]).wait()
    for j in range(0, beams, 256):
        w = buf[:, j : j + 256].astype(jnp.bfloat16)
        for k in range(0, half, 512):
            out[j : j + 256, k : k + 512] = lax.dot_general(
                w, chosen[:, k : k + 512], (((0,), (0,)), ((), ())), preferred_element_type=jnp.float32
            ).astype(jnp.bfloat16)


def quarter_of(wre, wim, antenna_map, interpret=False):
    antennas, beams = wre.shape
    half = antennas // 2
    return pl.pallas_call(
        quarter_kernel,
        in_specs=[pl.BlockSpec(memory_space=pltpu.HBM)] * 3,
        out_specs=pl.BlockSpec(memory_space=pltpu.VMEM),
        out_shape=jax.ShapeDtypeStruct((beams, half), jnp.bfloat16),
        scratch_shapes=[
            pltpu.VMEM((antennas, beams), jnp.float32),
            pltpu.VMEM((1, half), jnp.int32),
            pltpu.VMEM((antennas, half), jnp.bfloat16),
            pltpu.SemaphoreType.DMA((5,)),
        ],
        compiler_params=pltpu.CompilerParams(vmem_limit_bytes=58 * MIB),
        cost_estimate=pl.CostEstimate(flops=2 * 10**9, bytes_accessed=6 * 10**6, transcendentals=0),
        interpret=interpret,
        name="quarter",
    )(wre, wim, antenna_map.reshape(2, 1, half))


def pick_kernel(owners, offers, mine, other):
    core = lax.axis_index("grp") % 2
    mine[...] = offers[owners[core]]
    other[...] = offers[owners[1 - core]]


def pick_of(owners, offers, interpret=False):
    _, rows, columns = offers.shape
    return pl.pallas_call(
        pick_kernel,
        in_specs=[pl.BlockSpec(memory_space=pltpu.SMEM), pl.BlockSpec(memory_space=pltpu.VMEM)],
        out_specs=[pl.BlockSpec(memory_space=pltpu.VMEM)] * 2,
        out_shape=[jax.ShapeDtypeStruct((rows, columns), offers.dtype)] * 2,
        compiler_params=pltpu.CompilerParams(vmem_limit_bytes=8 * MIB),
        interpret=interpret,
        name="pick",
    )(owners, offers)


def join_kernel(axis, *refs):
    parts, out = refs[:-1], refs[-1]
    at = 0
    for part in parts:
        size = part.shape[axis]
        if axis == 0:
            out[at : at + size, :] = part[...]
        else:
            out[:, at : at + size] = part[...]
        at += size


def join_of(parts, axis, interpret=False):
    shape = list(parts[0].shape)
    shape[axis] = sum(p.shape[axis] for p in parts)
    return pl.pallas_call(
        functools.partial(join_kernel, axis),
        out_shape=jax.ShapeDtypeStruct(tuple(shape), parts[0].dtype),
        in_specs=[pl.BlockSpec(memory_space=pltpu.VMEM)] * len(parts),
        out_specs=pl.BlockSpec(memory_space=pltpu.VMEM),
        compiler_params=pltpu.CompilerParams(vmem_limit_bytes=8 * MIB),
        interpret=interpret,
        name="join",
    )(*parts)


def choose_matrix():
    chosen = np.zeros((2, 32, 3, 2, 2, 32), np.float32)
    for pair in range(2):
        for f1 in range(32):
            chosen[pair, f1, :, pair, :, f1] = 1.0
    return chosen.reshape(64, 384)


def products(core, part, spectra):
    half = part.shape[1] // 2
    near = pl.ds(pl.multiple_of(core * half, half), half)
    far = pl.ds(pl.multiple_of((1 - core) * half, half), half)
    left, right = part[:, :half], part[:, half:]
    return jnp.dot(left, spectra[near, :], preferred_element_type=jnp.float32) + jnp.dot(
        right, spectra[far, :], preferred_element_type=jnp.float32
    )


def early_kernel(w0, w1, za, out):
    core = lax.axis_index("grp") % 2
    n = w0.shape[0]
    for i, part in enumerate((w0, w1)):
        out[i * n : (i + 1) * n, :] = products(core, part, za)


def early_of(w0, w1, spectra, interpret=False):
    return pl.pallas_call(
        early_kernel,
        out_shape=jax.ShapeDtypeStruct((2 * w0.shape[0], 768), jnp.float32),
        in_specs=[pl.BlockSpec(memory_space=pltpu.VMEM)] * 3,
        out_specs=pl.BlockSpec(memory_space=pltpu.VMEM),
        compiler_params=pltpu.CompilerParams(vmem_limit_bytes=24 * MIB),
        cost_estimate=pl.CostEstimate(flops=17 * 10**8, bytes_accessed=8 * 10**6, transcendentals=0),
        interpret=interpret,
        name="early",
    )(w0, w1, spectra)


def beams_kernel(places, early, w2, w3, za, choose, own, given, sums):
    for k in range(32):
        at = pl.multiple_of(places[k], 16)
        sums[pl.ds(at, 16), :] = early[k * 16 : (k + 1) * 16, :]
    core = lax.axis_index("grp") % 2
    for i, part in enumerate((w2, w3)):
        result = products(core, part, za)
        for k in range(16):
            at = pl.multiple_of(places[(i + 2) * 16 + k], 16)
            sums[pl.ds(at, 16), :] = result[k * 16 : (k + 1) * 16, :]
    beams = sums.shape[0] // 2
    powers = []
    for g in range(3):
        re_lanes, im_lanes = slice(g * 256, g * 256 + 128), slice(g * 256 + 128, g * 256 + 256)
        re = sums[:beams, re_lanes] - sums[beams:, im_lanes]
        im = sums[beams:, re_lanes] + sums[:beams, im_lanes]
        powers.append(re * re + im * im)
    total = lax.dot_general(
        choose[...],
        jnp.concatenate(powers, axis=1),
        (((1,), (1,)), ((), ())),
        preferred_element_type=jnp.float32,
        precision=lax.Precision.HIGHEST,
    )
    total = total * (1.0 / SPECTRA)
    own[...] = jnp.where(core == 0, total[:32], total[32:])
    given[...] = jnp.where(core == 0, total[32:], total[:32])


def beams_of(places, early, w2, w3, spectra, interpret=False):
    rows = early.shape[0] + 2 * w2.shape[0]
    return pl.pallas_call(
        beams_kernel,
        out_shape=[jax.ShapeDtypeStruct((32, rows // 2), jnp.float32)] * 2,
        in_specs=[pl.BlockSpec(memory_space=pltpu.SMEM)] + [pl.BlockSpec(memory_space=pltpu.VMEM)] * 5,
        out_specs=[pl.BlockSpec(memory_space=pltpu.VMEM)] * 2,
        scratch_shapes=[pltpu.VMEM((rows, 768), jnp.float32)],
        compiler_params=pltpu.CompilerParams(vmem_limit_bytes=32 * MIB),
        cost_estimate=pl.CostEstimate(flops=17 * 10**8, bytes_accessed=8 * 10**6, transcendentals=0),
        interpret=interpret,
        name="beams",
    )(places, early, w2, w3, spectra, jnp.asarray(choose_matrix()))


def index_of(z, x, y, core):
    return ((y % 2) * 2 + core) * 32 + (z % 4) * 8 + (x % 4) * 2 + (y % 4) // 2


EVERY = [(z, x, y, c) for z in range(4) for x in range(4) for y in range(4) for c in range(2)]
ORDER = (("y", "x", "z"), ("z", "y", "x"))
SHIFTS = (0, -1, 1, 2)


def permutation(stage, shift):
    pairs = []
    for z, x, y, core in EVERY:
        axis = ORDER[core][stage]
        source = {"z": z, "x": x, "y": y}
        source[axis] += shift
        pairs.append((index_of(source["z"], source["x"], source["y"], core), index_of(z, x, y, core)))
    return pairs


def gather_stage(block, stage):
    return [block] + [lax.ppermute(block, ALL, permutation(stage, shift)) for shift in SHIFTS[1:]]


def block_places(grp, dev):
    core = grp % 2
    z, x, y = dev // 8, dev // 2 % 4, dev % 2 * 2 + grp // 2
    k = np.arange(64)
    shift = np.array(SHIFTS)
    first, second, third = shift[k % 4], shift[k // 4 % 4], shift[k // 16]
    by_core = []
    for order in ORDER:
        moved = dict(zip(order, (first, second, third)))
        by_core.append([moved[axis] for axis in "zxy"])
    is_first = core == 0
    mz, mx, my = [jnp.where(is_first, jnp.asarray(a), jnp.asarray(b)) for a, b in zip(*by_core)]
    fz, fx, fy = (z + mz + 4) % 4, (x + mx + 4) % 4, (y + my + 4) % 4
    return (((fy % 2) * 32 + fz * 8 + fx * 2 + fy // 2) * 16).astype(jnp.int32)


SWAP = [(0, 1), (1, 0), (2, 3), (3, 2)]


def on_device(voltage_real, voltage_imaginary, filter_taps, weights_re, weights_im, owners, antenna_map):
    grp, dev = lax.axis_index("grp"), lax.axis_index("dev")
    core = grp % 2

    quarter = quarter_of(weights_re[0], weights_im[0], antenna_map)
    offers = lax.all_to_all(quarter.reshape(32, 16, -1), "dev", split_axis=0, concat_axis=0, tiled=True)

    volts = (voltage_real, voltage_imaginary, filter_taps)
    quarter, *volts = lax.optimization_barrier((quarter, *volts))
    (message,) = spectra_of(MESSAGES, *volts)
    message, offers = lax.optimization_barrier((message, offers))
    mine, other = pick_of(owners, offers)
    message, mine, other = lax.optimization_barrier((message, mine, other))
    spectra = lax.all_to_all(message, ALL, split_axis=0, concat_axis=0, tiled=True)
    spectra = spectra.reshape(DEVICES * SLOTS, -1)

    other = lax.ppermute(other, "grp", SWAP)
    block = join_of([mine, other], 1)
    block = join_of(gather_stage(block, 0), 0)
    block = join_of(gather_stage(block, 1), 0)
    parts = gather_stage(block, 2)

    early = early_of(parts[0], parts[3], spectra)
    places = block_places(grp, dev)
    places = jnp.concatenate([places[:16], places[48:], places[16:48]])
    own, given = beams_of(places, early, parts[1], parts[2], spectra)
    taken = lax.ppermute(given, "grp", SWAP)
    return jnp.where(core == 0, jnp.stack([own, taken]), jnp.stack([taken, own]))


def solution(mesh):
    return jax.shard_map(
        on_device,
        mesh=mesh,
        in_specs=(
            P(("grp", "dev"), None),
            P(("grp", "dev"), None),
            P(),
            P("dev", None, None),
            P("dev", None, None),
            P(),
            P(),
        ),
        out_specs=P(None, ("grp", "dev"), None),
        check_vma=False,
    )
```

```python
import functools
import math

import jax
import jax.numpy as jnp
import numpy as np
from jax import lax
from jax.experimental import pallas as pl
from jax.experimental.pallas import tpu as pltpu
from jax.sharding import PartitionSpec as P

CHANNELS = 4096
TAPS = 16
SPECTRA = 6
STEPS = 2
FRAMES = STEPS * SPECTRA
BLOCKS = FRAMES + TAPS - 1
OUTER = 32
INNER = 128
SLOTS = 16
DEVICES = 128
ROW_STRIDE = 24
GROUPS = ((0, 1, 6, 7), (2, 3, 8, 9), (4, 5, 10, 11))
MESSAGES = ((0, 1, 2),)
ALL = ("grp", "dev")
MIB = 1 << 20


def twist_tables():
    products = np.outer(np.arange(OUTER), np.arange(INNER)) % CHANNELS
    angles = products * (2.0 * math.pi / CHANNELS)
    return np.cos(angles).astype(np.float32), np.sin(angles).astype(np.float32)


def inner_matrix():
    products = np.outer(np.arange(INNER), np.arange(INNER)) % INNER
    angles = products * (2.0 * math.pi / INNER)
    norm = CHANNELS ** (-0.5)
    c, s = np.cos(angles) * norm, np.sin(angles) * norm
    return np.block([[c, s], [-s, c]]).astype(np.float32)


def small_fft(points):
    count = len(points)
    if count == 1:
        return points
    even = small_fft(points[0::2])
    odd = small_fft(points[1::2])
    half = count // 2
    result = [None] * count
    for k in range(half):
        er, ei = even[k]
        xr, xi = odd[k]
        if k == 0:
            tr, ti = xr, xi
        elif 4 * k == count:
            tr, ti = xi, -xr
        elif 8 * k == count:
            r = math.sqrt(0.5)
            tr, ti = (xr + xi) * r, (xi - xr) * r
        elif 8 * k == 3 * count:
            r = math.sqrt(0.5)
            tr, ti = (xi - xr) * r, (xr + xi) * (-r)
        else:
            c = math.cos(2.0 * math.pi * k / count)
            s = math.sin(2.0 * math.pi * k / count)
            tr, ti = xr * c + xi * s, xi * c - xr * s
        result[k] = (er + tr, ei + ti)
        result[k + half] = (er - tr, ei - ti)
    return result


def spectra_kernel(messages, *refs):
    groups = [group for message in messages for group in message]
    count = len(groups)
    sources, outs = refs[:6], refs[6 : 6 + len(messages)]
    vre, vim, taps, cos_t, sin_t, mat, frames, turned, packed, ready, sems = refs[6 + len(messages) :]
    chosen = [u for group in groups for u in GROUPS[group]]
    first, last = min(chosen), max(chosen) + TAPS
    rows_per_slot = 32 * len(chosen)
    slot_stride = rows_per_slot + 8

    loads = []
    for i in (2, 0, 1, 3, 4, 5):
        source = sources[i]
        if i < 2:
            source = source.at[:, first * CHANNELS : last * CHANNELS]
        loads.append(pltpu.make_async_copy(source, (vre, vim, taps, cos_t, sin_t, mat)[i], sems.at[i]))
        loads[-1].start()
    loads[0].wait()

    for c, volts in ((0, vre), (1, vim)):
        loads[1 + c].wait()

        def fir(n1, _, c=c, volts=volts):
            rows = [taps[k : k + 1, pl.ds(pl.multiple_of(n1 * INNER, INNER), INNER)] for k in range(TAPS)]
            needed = sorted({u + k for u in chosen for k in range(TAPS)})
            window = {
                b: volts[
                    :, pl.ds(pl.multiple_of((b - first) * CHANNELS + n1 * INNER, INNER), INNER)
                ].astype(jnp.float32)
                for b in needed
            }
            for i, u in enumerate(chosen):
                total = window[u] * rows[0]
                for k in range(1, TAPS):
                    total = total + window[u + k] * rows[k]
                frames[c, i, n1] = total
            return 0

        lax.fori_loop(0, OUTER, fir, 0, unroll=2)

    for load in loads[3:]:
        load.wait()

    def outer(i, _):
        u = i // 2
        low = pl.multiple_of((i % 2) * 8, 8)
        points = [
            (frames[0, u, n1, pl.ds(low, 8), :], frames[1, u, n1, pl.ds(low, 8), :]) for n1 in range(OUTER)
        ]
        points = small_fft(points)
        for f1 in range(OUTER):
            re, im = points[f1]
            if f1:
                c, d = cos_t[f1 : f1 + 1, :], sin_t[f1 : f1 + 1, :]
                re, im = re * c + im * d, im * c - re * d
            at = low * slot_stride + u * 32 + f1
            turned[0, pl.ds(at, 8, stride=slot_stride), :] = re
            turned[1, pl.ds(at, 8, stride=slot_stride), :] = im
        return 0

    lax.fori_loop(0, 2 * len(chosen), outer, 0, unroll=2)

    matrix, matrix_low = mat[:256, :], mat[256:, :]
    lane = lax.broadcasted_iota(jnp.int32, (32, INNER), 1)

    def inner(a, _):
        base = pl.multiple_of(a * slot_stride, 8)
        rows = jnp.concatenate(
            [turned[0, pl.ds(base, rows_per_slot), :], turned[1, pl.ds(base, rows_per_slot), :]], axis=1
        )
        high = rows.astype(jnp.bfloat16)
        low = (rows - high.astype(jnp.float32)).astype(jnp.bfloat16)

        def product(left, right):
            return lax.dot_general(left, right, (((1,), (1,)), ((), ())), preferred_element_type=jnp.float32)

        spec = product(matrix, high) + (product(matrix_low, high) + product(matrix, low))
        for g in range(count):
            for y in range(2):
                for c in range(2):
                    to = [pl.ds((y * 2 + s) * 32 * ROW_STRIDE + a, 32, stride=ROW_STRIDE) for s in range(2)]
                    at = [c * 128 + (y * 2 + pair) * 32 for pair in range(2)]
                    mixed = [spec[f2 : f2 + 32, g * INNER : (g + 1) * INNER] for f2 in at]
                    packed[g * 2 + c, to[0], :] = jnp.where(lane < 64, mixed[0], pltpu.roll(mixed[1], 64, 1))
                    packed[g * 2 + c, to[1], :] = jnp.where(lane < 64, pltpu.roll(mixed[0], 64, 1), mixed[1])
        return 0

    lax.fori_loop(0, SLOTS, inner, 0, unroll=8)

    stores = []
    tile = 0
    for message, to in zip(messages, outs):
        for quarter in range(4):

            def emit(p, _, tile=tile, wide=2 * len(message)):
                for i in range(tile, tile + wide):
                    ready[p, :, i * INNER : (i + 1) * INNER] = packed[
                        i, pl.ds(pl.multiple_of(p * ROW_STRIDE, 8), SLOTS), :
                    ].astype(jnp.bfloat16)
                return 0

            lax.fori_loop(quarter * 32, quarter * 32 + 32, emit, 0, unroll=4)
            part = pl.ds(quarter * 32, 32)
            lanes = slice(tile * INNER, (tile + 2 * len(message)) * INNER)
            stores.append(
                pltpu.make_async_copy(ready.at[part, :, lanes], to.at[part], sems.at[6 + len(stores)])
            )
            stores[-1].start()
        tile += 2 * len(message)
    for store in stores:
        store.wait()


def spectra_of(messages, vre, vim, taps, interpret=False):
    cos_t, sin_t = twist_tables()
    mat = inner_matrix()
    high = mat.astype(jnp.bfloat16)
    mat = np.concatenate([high, (mat - high.astype(np.float32)).astype(jnp.bfloat16)])
    groups = [group for message in messages for group in message]
    count = len(groups)
    many = 4 * count
    chosen = [u for group in groups for u in GROUPS[group]]
    samples = (max(chosen) + TAPS - min(chosen)) * CHANNELS
    return pl.pallas_call(
        functools.partial(spectra_kernel, messages),
        out_shape=[jax.ShapeDtypeStruct((DEVICES, SLOTS, 2 * INNER * len(m)), jnp.bfloat16) for m in messages],
        in_specs=[pl.BlockSpec(memory_space=pltpu.HBM)] * 6,
        out_specs=[pl.BlockSpec(memory_space=pltpu.HBM)] * len(messages),
        scratch_shapes=[
            pltpu.VMEM((SLOTS, samples), jnp.bfloat16),
            pltpu.VMEM((SLOTS, samples), jnp.bfloat16),
            pltpu.VMEM((TAPS, CHANNELS), jnp.float32),
            pltpu.VMEM((OUTER, INNER), jnp.float32),
            pltpu.VMEM((OUTER, INNER), jnp.float32),
            pltpu.VMEM((512, 256), jnp.bfloat16),
            pltpu.VMEM((2, many, OUTER, SLOTS, INNER), jnp.float32),
            pltpu.VMEM((2, SLOTS * (32 * many + 8), INNER), jnp.float32),
            pltpu.VMEM((2 * count, DEVICES * ROW_STRIDE, INNER), jnp.float32),
            pltpu.VMEM((DEVICES, SLOTS, 2 * count * INNER), jnp.bfloat16),
            pltpu.SemaphoreType.DMA((6 + 4 * len(messages),)),
        ],
        compiler_params=pltpu.CompilerParams(vmem_limit_bytes=58 * MIB),
        cost_estimate=pl.CostEstimate(
            flops=8 * 10**8 * count, bytes_accessed=16 * 10**6 * count, transcendentals=0
        ),
        interpret=interpret,
        name="spectra",
    )(vre, vim, taps, jnp.asarray(cos_t), jnp.asarray(sin_t), jnp.asarray(mat))


def quarter_kernel(wre, wim, slots, out, buf, names, chosen, sems):
    grp = lax.axis_index("grp")
    y_lo, core = grp // 2, grp % 2
    antennas, beams = wre.shape
    half = antennas // 2
    name_copy = pltpu.make_async_copy(slots.at[core], names, sems.at[4])
    name_copy.start()
    for y, source in ((0, wre), (1, wim)):

        @pl.when(y_lo == y)
        def _():
            for i in range(4):
                part = pl.ds(i * half // 2, half // 2)
                pltpu.make_async_copy(source.at[part], buf.at[part], sems.at[i]).start()
    name_copy.wait()
    row = names[...]

    def build(i, _):
        antenna = lax.broadcasted_iota(jnp.int32, (16, half), 0) + i * 16
        chosen[pl.ds(pl.multiple_of(i * 16, 16), 16), :] = jnp.where(antenna == row, 1.0, 0.0).astype(jnp.bfloat16)
        return 0
    lax.fori_loop(0, antennas // 16, build, 0, unroll=4)
    for y, source in ((0, wre), (1, wim)):

        @pl.when(y_lo == y)
        def _():
            for i in range(4):
                part = pl.ds(i * half // 2, half // 2)
                pltpu.make_async_copy(source.at[part], buf.at[part], sems.at[i]).wait()
    for j in range(0, beams, 256):
        w = buf[:, j : j + 256].astype(jnp.bfloat16)
        for k in range(0, half, 512):
            out[j : j + 256, k : k + 512] = lax.dot_general(
                w, chosen[:, k : k + 512], (((0,), (0,)), ((), ())), preferred_element_type=jnp.float32
            ).astype(jnp.bfloat16)


def quarter_of(wre, wim, antenna_map, interpret=False):
    antennas, beams = wre.shape
    half = antennas // 2
    return pl.pallas_call(
        quarter_kernel,
        in_specs=[pl.BlockSpec(memory_space=pltpu.HBM)] * 3,
        out_specs=pl.BlockSpec(memory_space=pltpu.VMEM),
        out_shape=jax.ShapeDtypeStruct((beams, half), jnp.bfloat16),
        scratch_shapes=[
            pltpu.VMEM((antennas, beams), jnp.float32),
            pltpu.VMEM((1, half), jnp.int32),
            pltpu.VMEM((antennas, half), jnp.bfloat16),
            pltpu.SemaphoreType.DMA((5,)),
        ],
        compiler_params=pltpu.CompilerParams(vmem_limit_bytes=58 * MIB),
        cost_estimate=pl.CostEstimate(flops=2 * 10**9, bytes_accessed=6 * 10**6, transcendentals=0),
        interpret=interpret,
        name="quarter",
    )(wre, wim, antenna_map.reshape(2, 1, half))


def pick_kernel(owners, offers, mine, other):
    core = lax.axis_index("grp") % 2
    mine[...] = offers[owners[core]]
    other[...] = offers[owners[1 - core]]


def pick_of(owners, offers, interpret=False):
    _, rows, columns = offers.shape
    return pl.pallas_call(
        pick_kernel,
        in_specs=[pl.BlockSpec(memory_space=pltpu.SMEM), pl.BlockSpec(memory_space=pltpu.VMEM)],
        out_specs=[pl.BlockSpec(memory_space=pltpu.VMEM)] * 2,
        out_shape=[jax.ShapeDtypeStruct((rows, columns), offers.dtype)] * 2,
        compiler_params=pltpu.CompilerParams(vmem_limit_bytes=8 * MIB),
        interpret=interpret,
        name="pick",
    )(owners, offers)


def join_kernel(axis, *refs):
    parts, out = refs[:-1], refs[-1]
    at = 0
    for part in parts:
        size = part.shape[axis]
        if axis == 0:
            out[at : at + size, :] = part[...]
        else:
            out[:, at : at + size] = part[...]
        at += size


def join_of(parts, axis, interpret=False):
    shape = list(parts[0].shape)
    shape[axis] = sum(p.shape[axis] for p in parts)
    return pl.pallas_call(
        functools.partial(join_kernel, axis),
        out_shape=jax.ShapeDtypeStruct(tuple(shape), parts[0].dtype),
        in_specs=[pl.BlockSpec(memory_space=pltpu.VMEM)] * len(parts),
        out_specs=pl.BlockSpec(memory_space=pltpu.VMEM),
        compiler_params=pltpu.CompilerParams(vmem_limit_bytes=8 * MIB),
        interpret=interpret,
        name="join",
    )(*parts)


def choose_matrix():
    chosen = np.zeros((2, 32, 3, 2, 2, 32), np.float32)
    for pair in range(2):
        for f1 in range(32):
            chosen[pair, f1, :, pair, :, f1] = 1.0
    return chosen.reshape(64, 384)


def products(core, part, spectra):
    half = part.shape[1] // 2
    near = pl.ds(pl.multiple_of(core * half, half), half)
    far = pl.ds(pl.multiple_of((1 - core) * half, half), half)
    left, right = part[:, :half], part[:, half:]
    return jnp.dot(left, spectra[near, :], preferred_element_type=jnp.float32) + jnp.dot(
        right, spectra[far, :], preferred_element_type=jnp.float32
    )


def early_kernel(w0, w1, za, out):
    core = lax.axis_index("grp") % 2
    n = w0.shape[0]
    for i, part in enumerate((w0, w1)):
        out[i * n : (i + 1) * n, :] = products(core, part, za)


def early_of(w0, w1, spectra, interpret=False):
    return pl.pallas_call(
        early_kernel,
        out_shape=jax.ShapeDtypeStruct((2 * w0.shape[0], 768), jnp.float32),
        in_specs=[pl.BlockSpec(memory_space=pltpu.VMEM)] * 3,
        out_specs=pl.BlockSpec(memory_space=pltpu.VMEM),
        compiler_params=pltpu.CompilerParams(vmem_limit_bytes=24 * MIB),
        cost_estimate=pl.CostEstimate(flops=17 * 10**8, bytes_accessed=8 * 10**6, transcendentals=0),
        interpret=interpret,
        name="early",
    )(w0, w1, spectra)


def beams_kernel(places, early, w2, w3, za, choose, own, given, sums):
    for k in range(32):
        at = pl.multiple_of(places[k], 16)
        sums[pl.ds(at, 16), :] = early[k * 16 : (k + 1) * 16, :]
    core = lax.axis_index("grp") % 2
    for i, part in enumerate((w2, w3)):
        result = products(core, part, za)
        for k in range(16):
            at = pl.multiple_of(places[(i + 2) * 16 + k], 16)
            sums[pl.ds(at, 16), :] = result[k * 16 : (k + 1) * 16, :]
    beams = sums.shape[0] // 2
    powers = []
    for g in range(3):
        re_lanes, im_lanes = slice(g * 256, g * 256 + 128), slice(g * 256 + 128, g * 256 + 256)
        re = sums[:beams, re_lanes] - sums[beams:, im_lanes]
        im = sums[beams:, re_lanes] + sums[:beams, im_lanes]
        powers.append(re * re + im * im)
    total = lax.dot_general(
        choose[...],
        jnp.concatenate(powers, axis=1),
        (((1,), (1,)), ((), ())),
        preferred_element_type=jnp.float32,
        precision=lax.Precision.HIGHEST,
    )
    total = total * (1.0 / SPECTRA)
    own[...] = jnp.where(core == 0, total[:32], total[32:])
    given[...] = jnp.where(core == 0, total[32:], total[:32])


def beams_of(places, early, w2, w3, spectra, interpret=False):
    rows = early.shape[0] + 2 * w2.shape[0]
    return pl.pallas_call(
        beams_kernel,
        out_shape=[jax.ShapeDtypeStruct((32, rows // 2), jnp.float32)] * 2,
        in_specs=[pl.BlockSpec(memory_space=pltpu.SMEM)] + [pl.BlockSpec(memory_space=pltpu.VMEM)] * 5,
        out_specs=[pl.BlockSpec(memory_space=pltpu.VMEM)] * 2,
        scratch_shapes=[pltpu.VMEM((rows, 768), jnp.float32)],
        compiler_params=pltpu.CompilerParams(vmem_limit_bytes=32 * MIB),
        cost_estimate=pl.CostEstimate(flops=17 * 10**8, bytes_accessed=8 * 10**6, transcendentals=0),
        interpret=interpret,
        name="beams",
    )(places, early, w2, w3, spectra, jnp.asarray(choose_matrix()))


def index_of(z, x, y, core):
    return ((y % 2) * 2 + core) * 32 + (z % 4) * 8 + (x % 4) * 2 + (y % 4) // 2


EVERY = [(z, x, y, c) for z in range(4) for x in range(4) for y in range(4) for c in range(2)]
ORDER = (("y", "x", "z"), ("z", "y", "x"))
SHIFTS = (0, -1, 1, 2)


def permutation(stage, shift):
    pairs = []
    for z, x, y, core in EVERY:
        axis = ORDER[core][stage]
        source = {"z": z, "x": x, "y": y}
        source[axis] += shift
        pairs.append((index_of(source["z"], source["x"], source["y"], core), index_of(z, x, y, core)))
    return pairs


def gather_stage(block, stage):
    return [block] + [lax.ppermute(block, ALL, permutation(stage, shift)) for shift in SHIFTS[1:]]


def block_places(grp, dev):
    core = grp % 2
    z, x, y = dev // 8, dev // 2 % 4, dev % 2 * 2 + grp // 2
    k = np.arange(64)
    shift = np.array(SHIFTS)
    first, second, third = shift[k % 4], shift[k // 4 % 4], shift[k // 16]
    by_core = []
    for order in ORDER:
        moved = dict(zip(order, (first, second, third)))
        by_core.append([moved[axis] for axis in "zxy"])
    is_first = core == 0
    mz, mx, my = [jnp.where(is_first, jnp.asarray(a), jnp.asarray(b)) for a, b in zip(*by_core)]
    fz, fx, fy = (z + mz + 4) % 4, (x + mx + 4) % 4, (y + my + 4) % 4
    return (((fy % 2) * 32 + fz * 8 + fx * 2 + fy // 2) * 16).astype(jnp.int32)


SWAP = [(0, 1), (1, 0), (2, 3), (3, 2)]


def on_device(voltage_real, voltage_imaginary, filter_taps, weights_re, weights_im, owners, antenna_map):
    grp, dev = lax.axis_index("grp"), lax.axis_index("dev")
    core = grp % 2

    quarter = quarter_of(weights_re[0], weights_im[0], antenna_map)
    offers = lax.all_to_all(quarter.reshape(32, 16, -1), "dev", split_axis=0, concat_axis=0, tiled=True)

    volts = (voltage_real, voltage_imaginary, filter_taps)
    quarter, *volts = lax.optimization_barrier((quarter, *volts))
    (message,) = spectra_of(MESSAGES, *volts)
    message, offers = lax.optimization_barrier((message, offers))
    mine, other = pick_of(owners, offers)
    message, mine, other = lax.optimization_barrier((message, mine, other))
    spectra = lax.all_to_all(message, ALL, split_axis=0, concat_axis=0, tiled=True)
    spectra = spectra.reshape(DEVICES * SLOTS, -1)

    other = lax.ppermute(other, "grp", SWAP)
    block = join_of([mine, other], 1)
    block = join_of(gather_stage(block, 0), 0)
    block = join_of(gather_stage(block, 1), 0)
    parts = gather_stage(block, 2)

    early = early_of(parts[0], parts[3], spectra)
    places = block_places(grp, dev)
    places = jnp.concatenate([places[:16], places[48:], places[16:48]])
    own, given = beams_of(places, early, parts[1], parts[2], spectra)
    taken = lax.ppermute(given, "grp", SWAP)
    return jnp.where(core == 0, jnp.stack([own, taken]), jnp.stack([taken, own]))


def solution(mesh):
    return jax.shard_map(
        on_device,
        mesh=mesh,
        in_specs=(
            P(("grp", "dev"), None),
            P(("grp", "dev"), None),
            P(),
            P("dev", None, None),
            P("dev", None, None),
            P(),
            P(),
        ),
        out_specs=P(None, ("grp", "dev"), None),
        check_vma=False,
    )
```

```python
import functools
import math

import jax
import jax.numpy as jnp
import numpy as np
from jax import lax
from jax.experimental import pallas as pl
from jax.experimental.pallas import tpu as pltpu
from jax.sharding import PartitionSpec as P

CHANNELS = 4096
TAPS = 16
SPECTRA = 6
STEPS = 2
FRAMES = STEPS * SPECTRA
BLOCKS = FRAMES + TAPS - 1
OUTER = 32
INNER = 128
SLOTS = 16
DEVICES = 128
ROW_STRIDE = 24
GROUPS = ((0, 1, 6, 7), (2, 3, 8, 9), (4, 5, 10, 11))
MESSAGES = ((0, 1, 2),)
ALL = ("grp", "dev")
MIB = 1 << 20


def twist_tables():
    products = np.outer(np.arange(OUTER), np.arange(INNER)) % CHANNELS
    angles = products * (2.0 * math.pi / CHANNELS)
    return np.cos(angles).astype(np.float32), np.sin(angles).astype(np.float32)


def inner_matrix():
    products = np.outer(np.arange(INNER), np.arange(INNER)) % INNER
    angles = products * (2.0 * math.pi / INNER)
    norm = CHANNELS ** (-0.5)
    c, s = np.cos(angles) * norm, np.sin(angles) * norm
    return np.block([[c, s], [-s, c]]).astype(np.float32)


def small_fft(points):
    count = len(points)
    if count == 1:
        return points
    even = small_fft(points[0::2])
    odd = small_fft(points[1::2])
    half = count // 2
    result = [None] * count
    for k in range(half):
        er, ei = even[k]
        xr, xi = odd[k]
        if k == 0:
            tr, ti = xr, xi
        elif 4 * k == count:
            tr, ti = xi, -xr
        elif 8 * k == count:
            r = math.sqrt(0.5)
            tr, ti = (xr + xi) * r, (xi - xr) * r
        elif 8 * k == 3 * count:
            r = math.sqrt(0.5)
            tr, ti = (xi - xr) * r, (xr + xi) * (-r)
        else:
            c = math.cos(2.0 * math.pi * k / count)
            s = math.sin(2.0 * math.pi * k / count)
            tr, ti = xr * c + xi * s, xi * c - xr * s
        result[k] = (er + tr, ei + ti)
        result[k + half] = (er - tr, ei - ti)
    return result


def spectra_kernel(messages, *refs):
    groups = [group for message in messages for group in message]
    count = len(groups)
    sources, outs = refs[:6], refs[6 : 6 + len(messages)]
    vre, vim, taps, cos_t, sin_t, mat, frames, turned, packed, ready, sems = refs[6 + len(messages) :]
    chosen = [u for group in groups for u in GROUPS[group]]
    first, last = min(chosen), max(chosen) + TAPS
    rows_per_slot = 32 * len(chosen)
    slot_stride = rows_per_slot + 8

    loads = []
    for i in (2, 0, 1, 3, 4, 5):
        source = sources[i]
        if i < 2:
            source = source.at[:, first * CHANNELS : last * CHANNELS]
        loads.append(pltpu.make_async_copy(source, (vre, vim, taps, cos_t, sin_t, mat)[i], sems.at[i]))
        loads[-1].start()
    loads[0].wait()

    for c, volts in ((0, vre), (1, vim)):
        loads[1 + c].wait()

        def fir(n1, _, c=c, volts=volts):
            rows = [taps[k : k + 1, pl.ds(pl.multiple_of(n1 * INNER, INNER), INNER)] for k in range(TAPS)]
            needed = sorted({u + k for u in chosen for k in range(TAPS)})
            window = {
                b: volts[
                    :, pl.ds(pl.multiple_of((b - first) * CHANNELS + n1 * INNER, INNER), INNER)
                ].astype(jnp.float32)
                for b in needed
            }
            for i, u in enumerate(chosen):
                total = window[u] * rows[0]
                for k in range(1, TAPS):
                    total = total + window[u + k] * rows[k]
                frames[c, i, n1] = total
            return 0

        lax.fori_loop(0, OUTER, fir, 0, unroll=2)

    for load in loads[3:]:
        load.wait()

    def outer(i, _):
        u = i // 2
        low = pl.multiple_of((i % 2) * 8, 8)
        points = [
            (frames[0, u, n1, pl.ds(low, 8), :], frames[1, u, n1, pl.ds(low, 8), :]) for n1 in range(OUTER)
        ]
        points = small_fft(points)
        for f1 in range(OUTER):
            re, im = points[f1]
            if f1:
                c, d = cos_t[f1 : f1 + 1, :], sin_t[f1 : f1 + 1, :]
                re, im = re * c + im * d, im * c - re * d
            at = low * slot_stride + u * 32 + f1
            turned[0, pl.ds(at, 8, stride=slot_stride), :] = re
            turned[1, pl.ds(at, 8, stride=slot_stride), :] = im
        return 0

    lax.fori_loop(0, 2 * len(chosen), outer, 0, unroll=2)

    matrix = mat[...]
    lane = lax.broadcasted_iota(jnp.int32, (32, INNER), 1)

    def inner(a, _):
        base = pl.multiple_of(a * slot_stride, 8)
        rows = jnp.concatenate(
            [turned[0, pl.ds(base, rows_per_slot), :], turned[1, pl.ds(base, rows_per_slot), :]], axis=1
        ).astype(jnp.bfloat16)
        spec = lax.dot_general(
            matrix, rows, (((1,), (1,)), ((), ())), preferred_element_type=jnp.float32
        )
        for g in range(count):
            for y in range(2):
                for c in range(2):
                    to = [pl.ds((y * 2 + s) * 32 * ROW_STRIDE + a, 32, stride=ROW_STRIDE) for s in range(2)]
                    at = [c * 128 + (y * 2 + pair) * 32 for pair in range(2)]
                    mixed = [spec[f2 : f2 + 32, g * INNER : (g + 1) * INNER] for f2 in at]
                    packed[g * 2 + c, to[0], :] = jnp.where(lane < 64, mixed[0], pltpu.roll(mixed[1], 64, 1))
                    packed[g * 2 + c, to[1], :] = jnp.where(lane < 64, pltpu.roll(mixed[0], 64, 1), mixed[1])
        return 0

    lax.fori_loop(0, SLOTS, inner, 0, unroll=8)

    stores = []
    tile = 0
    for message, to in zip(messages, outs):
        for quarter in range(4):

            def emit(p, _, tile=tile, wide=2 * len(message)):
                for i in range(tile, tile + wide):
                    ready[p, :, i * INNER : (i + 1) * INNER] = packed[
                        i, pl.ds(pl.multiple_of(p * ROW_STRIDE, 8), SLOTS), :
                    ].astype(jnp.bfloat16)
                return 0

            lax.fori_loop(quarter * 32, quarter * 32 + 32, emit, 0, unroll=4)
            part = pl.ds(quarter * 32, 32)
            lanes = slice(tile * INNER, (tile + 2 * len(message)) * INNER)
            stores.append(
                pltpu.make_async_copy(ready.at[part, :, lanes], to.at[part], sems.at[6 + len(stores)])
            )
            stores[-1].start()
        tile += 2 * len(message)
    for store in stores:
        store.wait()


def spectra_of(messages, vre, vim, taps, interpret=False):
    cos_t, sin_t = twist_tables()
    mat = inner_matrix().astype(jnp.bfloat16)
    groups = [group for message in messages for group in message]
    count = len(groups)
    many = 4 * count
    chosen = [u for group in groups for u in GROUPS[group]]
    samples = (max(chosen) + TAPS - min(chosen)) * CHANNELS
    return pl.pallas_call(
        functools.partial(spectra_kernel, messages),
        out_shape=[jax.ShapeDtypeStruct((DEVICES, SLOTS, 2 * INNER * len(m)), jnp.bfloat16) for m in messages],
        in_specs=[pl.BlockSpec(memory_space=pltpu.HBM)] * 6,
        out_specs=[pl.BlockSpec(memory_space=pltpu.HBM)] * len(messages),
        scratch_shapes=[
            pltpu.VMEM((SLOTS, samples), jnp.bfloat16),
            pltpu.VMEM((SLOTS, samples), jnp.bfloat16),
            pltpu.VMEM((TAPS, CHANNELS), jnp.float32),
            pltpu.VMEM((OUTER, INNER), jnp.float32),
            pltpu.VMEM((OUTER, INNER), jnp.float32),
            pltpu.VMEM((256, 256), jnp.bfloat16),
            pltpu.VMEM((2, many, OUTER, SLOTS, INNER), jnp.float32),
            pltpu.VMEM((2, SLOTS * (32 * many + 8), INNER), jnp.float32),
            pltpu.VMEM((2 * count, DEVICES * ROW_STRIDE, INNER), jnp.float32),
            pltpu.VMEM((DEVICES, SLOTS, 2 * count * INNER), jnp.bfloat16),
            pltpu.SemaphoreType.DMA((6 + 4 * len(messages),)),
        ],
        compiler_params=pltpu.CompilerParams(vmem_limit_bytes=58 * MIB),
        cost_estimate=pl.CostEstimate(
            flops=8 * 10**8 * count, bytes_accessed=16 * 10**6 * count, transcendentals=0
        ),
        interpret=interpret,
        name="spectra",
    )(vre, vim, taps, jnp.asarray(cos_t), jnp.asarray(sin_t), jnp.asarray(mat))


def quarter_kernel(wre, wim, slots, out, buf, names, chosen, sems):
    grp = lax.axis_index("grp")
    y_lo, core = grp // 2, grp % 2
    antennas, beams = wre.shape
    half = antennas // 2
    name_copy = pltpu.make_async_copy(slots.at[core], names, sems.at[4])
    name_copy.start()
    for y, source in ((0, wre), (1, wim)):

        @pl.when(y_lo == y)
        def _():
            for i in range(4):
                part = pl.ds(i * half // 2, half // 2)
                pltpu.make_async_copy(source.at[part], buf.at[part], sems.at[i]).start()
    name_copy.wait()
    row = names[...]

    def build(i, _):
        antenna = lax.broadcasted_iota(jnp.int32, (16, half), 0) + i * 16
        chosen[pl.ds(pl.multiple_of(i * 16, 16), 16), :] = jnp.where(antenna == row, 1.0, 0.0).astype(jnp.bfloat16)
        return 0
    lax.fori_loop(0, antennas // 16, build, 0, unroll=4)
    for y, source in ((0, wre), (1, wim)):

        @pl.when(y_lo == y)
        def _():
            for i in range(4):
                part = pl.ds(i * half // 2, half // 2)
                pltpu.make_async_copy(source.at[part], buf.at[part], sems.at[i]).wait()
    for j in range(0, beams, 256):
        w = buf[:, j : j + 256].astype(jnp.bfloat16)
        for k in range(0, half, 512):
            out[j : j + 256, k : k + 512] = lax.dot_general(
                w, chosen[:, k : k + 512], (((0,), (0,)), ((), ())), preferred_element_type=jnp.float32
            ).astype(jnp.bfloat16)


def quarter_of(wre, wim, antenna_map, interpret=False):
    antennas, beams = wre.shape
    half = antennas // 2
    return pl.pallas_call(
        quarter_kernel,
        in_specs=[pl.BlockSpec(memory_space=pltpu.HBM)] * 3,
        out_specs=pl.BlockSpec(memory_space=pltpu.VMEM),
        out_shape=jax.ShapeDtypeStruct((beams, half), jnp.bfloat16),
        scratch_shapes=[
            pltpu.VMEM((antennas, beams), jnp.float32),
            pltpu.VMEM((1, half), jnp.int32),
            pltpu.VMEM((antennas, half), jnp.bfloat16),
            pltpu.SemaphoreType.DMA((5,)),
        ],
        compiler_params=pltpu.CompilerParams(vmem_limit_bytes=58 * MIB),
        cost_estimate=pl.CostEstimate(flops=2 * 10**9, bytes_accessed=6 * 10**6, transcendentals=0),
        interpret=interpret,
        name="quarter",
    )(wre, wim, antenna_map.reshape(2, 1, half))


def pick_kernel(owners, offers, mine, other):
    core = lax.axis_index("grp") % 2
    mine[...] = offers[owners[core]]
    other[...] = offers[owners[1 - core]]


def pick_of(owners, offers, interpret=False):
    _, rows, columns = offers.shape
    return pl.pallas_call(
        pick_kernel,
        in_specs=[pl.BlockSpec(memory_space=pltpu.SMEM), pl.BlockSpec(memory_space=pltpu.VMEM)],
        out_specs=[pl.BlockSpec(memory_space=pltpu.VMEM)] * 2,
        out_shape=[jax.ShapeDtypeStruct((rows, columns), offers.dtype)] * 2,
        compiler_params=pltpu.CompilerParams(vmem_limit_bytes=8 * MIB),
        interpret=interpret,
        name="pick",
    )(owners, offers)


def join_kernel(axis, *refs):
    parts, out = refs[:-1], refs[-1]
    at = 0
    for part in parts:
        size = part.shape[axis]
        if axis == 0:
            out[at : at + size, :] = part[...]
        else:
            out[:, at : at + size] = part[...]
        at += size


def join_of(parts, axis, interpret=False):
    shape = list(parts[0].shape)
    shape[axis] = sum(p.shape[axis] for p in parts)
    return pl.pallas_call(
        functools.partial(join_kernel, axis),
        out_shape=jax.ShapeDtypeStruct(tuple(shape), parts[0].dtype),
        in_specs=[pl.BlockSpec(memory_space=pltpu.VMEM)] * len(parts),
        out_specs=pl.BlockSpec(memory_space=pltpu.VMEM),
        compiler_params=pltpu.CompilerParams(vmem_limit_bytes=8 * MIB),
        interpret=interpret,
        name="join",
    )(*parts)


def choose_matrix():
    chosen = np.zeros((2, 32, 3, 2, 2, 32), np.float32)
    for pair in range(2):
        for f1 in range(32):
            chosen[pair, f1, :, pair, :, f1] = 1.0
    return chosen.reshape(64, 384)


def products(core, part, spectra):
    half = part.shape[1] // 2
    near = pl.ds(pl.multiple_of(core * half, half), half)
    far = pl.ds(pl.multiple_of((1 - core) * half, half), half)
    left, right = part[:, :half], part[:, half:]
    return jnp.dot(left, spectra[near, :], preferred_element_type=jnp.float32) + jnp.dot(
        right, spectra[far, :], preferred_element_type=jnp.float32
    )


def early_kernel(w0, w1, w2, za, out):
    core = lax.axis_index("grp") % 2
    n = w0.shape[0]
    for i, part in enumerate((w0, w1, w2)):
        out[i * n : (i + 1) * n, :] = products(core, part, za)


def early_of(w0, w1, w2, spectra, interpret=False):
    return pl.pallas_call(
        early_kernel,
        out_shape=jax.ShapeDtypeStruct((3 * w0.shape[0], 768), jnp.float32),
        in_specs=[pl.BlockSpec(memory_space=pltpu.VMEM)] * 4,
        out_specs=pl.BlockSpec(memory_space=pltpu.VMEM),
        compiler_params=pltpu.CompilerParams(vmem_limit_bytes=24 * MIB),
        cost_estimate=pl.CostEstimate(flops=17 * 10**8, bytes_accessed=8 * 10**6, transcendentals=0),
        interpret=interpret,
        name="early",
    )(w0, w1, w2, spectra)


def beams_kernel(places, early, w3, za, choose, own, given, sums):
    for k in range(48):
        at = pl.multiple_of(places[k], 16)
        sums[pl.ds(at, 16), :] = early[k * 16 : (k + 1) * 16, :]
    core = lax.axis_index("grp") % 2
    result = products(core, w3, za)
    for k in range(16):
        at = pl.multiple_of(places[48 + k], 16)
        sums[pl.ds(at, 16), :] = result[k * 16 : (k + 1) * 16, :]
    beams = sums.shape[0] // 2
    powers = []
    for g in range(3):
        re_lanes, im_lanes = slice(g * 256, g * 256 + 128), slice(g * 256 + 128, g * 256 + 256)
        re = sums[:beams, re_lanes] - sums[beams:, im_lanes]
        im = sums[beams:, re_lanes] + sums[:beams, im_lanes]
        powers.append(re * re + im * im)
    total = lax.dot_general(
        choose[...],
        jnp.concatenate(powers, axis=1),
        (((1,), (1,)), ((), ())),
        preferred_element_type=jnp.float32,
        precision=lax.Precision.HIGHEST,
    )
    total = total * (1.0 / SPECTRA)
    own[...] = jnp.where(core == 0, total[:32], total[32:])
    given[...] = jnp.where(core == 0, total[32:], total[:32])


def beams_of(places, early, w3, spectra, interpret=False):
    rows = early.shape[0] + w3.shape[0]
    return pl.pallas_call(
        beams_kernel,
        out_shape=[jax.ShapeDtypeStruct((32, rows // 2), jnp.float32)] * 2,
        in_specs=[pl.BlockSpec(memory_space=pltpu.SMEM)] + [pl.BlockSpec(memory_space=pltpu.VMEM)] * 4,
        out_specs=[pl.BlockSpec(memory_space=pltpu.VMEM)] * 2,
        scratch_shapes=[pltpu.VMEM((rows, 768), jnp.float32)],
        compiler_params=pltpu.CompilerParams(vmem_limit_bytes=32 * MIB),
        cost_estimate=pl.CostEstimate(flops=17 * 10**8, bytes_accessed=8 * 10**6, transcendentals=0),
        interpret=interpret,
        name="beams",
    )(places, early, w3, spectra, jnp.asarray(choose_matrix()))


def index_of(z, x, y, core):
    return ((y % 2) * 2 + core) * 32 + (z % 4) * 8 + (x % 4) * 2 + (y % 4) // 2


EVERY = [(z, x, y, c) for z in range(4) for x in range(4) for y in range(4) for c in range(2)]
ORDER = (("y", "x", "z"), ("z", "y", "x"))
SHIFTS = (0, -1, 1, 2)


def permutation(stage, shift):
    pairs = []
    for z, x, y, core in EVERY:
        axis = ORDER[core][stage]
        source = {"z": z, "x": x, "y": y}
        source[axis] += shift
        pairs.append((index_of(source["z"], source["x"], source["y"], core), index_of(z, x, y, core)))
    return pairs


def gather_stage(block, stage):
    return [block] + [lax.ppermute(block, ALL, permutation(stage, shift)) for shift in SHIFTS[1:]]


def block_places(grp, dev):
    core = grp % 2
    z, x, y = dev // 8, dev // 2 % 4, dev % 2 * 2 + grp // 2
    k = np.arange(64)
    shift = np.array(SHIFTS)
    first, second, third = shift[k % 4], shift[k // 4 % 4], shift[k // 16]
    by_core = []
    for order in ORDER:
        moved = dict(zip(order, (first, second, third)))
        by_core.append([moved[axis] for axis in "zxy"])
    is_first = core == 0
    mz, mx, my = [jnp.where(is_first, jnp.asarray(a), jnp.asarray(b)) for a, b in zip(*by_core)]
    fz, fx, fy = (z + mz + 4) % 4, (x + mx + 4) % 4, (y + my + 4) % 4
    return (((fy % 2) * 32 + fz * 8 + fx * 2 + fy // 2) * 16).astype(jnp.int32)


SWAP = [(0, 1), (1, 0), (2, 3), (3, 2)]


def on_device(voltage_real, voltage_imaginary, filter_taps, weights_re, weights_im, owners, antenna_map):
    grp, dev = lax.axis_index("grp"), lax.axis_index("dev")
    core = grp % 2

    quarter = quarter_of(weights_re[0], weights_im[0], antenna_map)
    offers = lax.all_to_all(quarter.reshape(32, 16, -1), "dev", split_axis=0, concat_axis=0, tiled=True)

    volts = (voltage_real, voltage_imaginary, filter_taps)
    quarter, *volts = lax.optimization_barrier((quarter, *volts))
    (message,) = spectra_of(MESSAGES, *volts)
    message, offers = lax.optimization_barrier((message, offers))
    mine, other = pick_of(owners, offers)
    message, mine, other = lax.optimization_barrier((message, mine, other))
    spectra = lax.all_to_all(message, ALL, split_axis=0, concat_axis=0, tiled=True)
    spectra = spectra.reshape(DEVICES * SLOTS, -1)

    other = lax.ppermute(other, "grp", SWAP)
    block = join_of([mine, other], 1)
    block = join_of(gather_stage(block, 0), 0)
    block = join_of(gather_stage(block, 1), 0)
    parts = gather_stage(block, 2)

    early = early_of(*parts[:3], spectra)
    places = block_places(grp, dev)
    own, given = beams_of(places, early, parts[3], spectra)
    taken = lax.ppermute(given, "grp", SWAP)
    return jnp.where(core == 0, jnp.stack([own, taken]), jnp.stack([taken, own]))


def solution(mesh):
    return jax.shard_map(
        on_device,
        mesh=mesh,
        in_specs=(
            P(("grp", "dev"), None),
            P(("grp", "dev"), None),
            P(),
            P("dev", None, None),
            P("dev", None, None),
            P(),
            P(),
        ),
        out_specs=P(None, ("grp", "dev"), None),
        check_vma=False,
    )
```

```python
import functools
import math

import jax
import jax.numpy as jnp
import numpy as np
from jax import lax
from jax.experimental import pallas as pl
from jax.experimental.pallas import tpu as pltpu
from jax.sharding import PartitionSpec as P

CHANNELS = 4096
TAPS = 16
SPECTRA = 6
STEPS = 2
FRAMES = STEPS * SPECTRA
BLOCKS = FRAMES + TAPS - 1
OUTER = 32
INNER = 128
SLOTS = 16
DEVICES = 128
ROW_STRIDE = 24
GROUPS = ((0, 1, 6, 7), (2, 3, 8, 9), (4, 5, 10, 11))
MESSAGES = ((0, 1, 2),)
ALL = ("grp", "dev")
MIB = 1 << 20


def twist_tables():
    products = np.outer(np.arange(OUTER), np.arange(INNER)) % CHANNELS
    angles = products * (2.0 * math.pi / CHANNELS)
    return np.cos(angles).astype(np.float32), np.sin(angles).astype(np.float32)


def inner_matrix():
    products = np.outer(np.arange(INNER), np.arange(INNER)) % INNER
    angles = products * (2.0 * math.pi / INNER)
    norm = CHANNELS ** (-0.5)
    c, s = np.cos(angles) * norm, np.sin(angles) * norm
    return np.block([[c, s], [-s, c]]).astype(np.float32)


def small_fft(points):
    count = len(points)
    if count == 1:
        return points
    even = small_fft(points[0::2])
    odd = small_fft(points[1::2])
    half = count // 2
    result = [None] * count
    for k in range(half):
        er, ei = even[k]
        xr, xi = odd[k]
        if k == 0:
            tr, ti = xr, xi
        elif 4 * k == count:
            tr, ti = xi, -xr
        elif 8 * k == count:
            r = math.sqrt(0.5)
            tr, ti = (xr + xi) * r, (xi - xr) * r
        elif 8 * k == 3 * count:
            r = math.sqrt(0.5)
            tr, ti = (xi - xr) * r, (xr + xi) * (-r)
        else:
            c = math.cos(2.0 * math.pi * k / count)
            s = math.sin(2.0 * math.pi * k / count)
            tr, ti = xr * c + xi * s, xi * c - xr * s
        result[k] = (er + tr, ei + ti)
        result[k + half] = (er - tr, ei - ti)
    return result


def spectra_kernel(messages, *refs):
    groups = [group for message in messages for group in message]
    count = len(groups)
    sources, outs = refs[:6], refs[6 : 6 + len(messages)]
    vre, vim, taps, cos_t, sin_t, mat, frames, turned, packed, ready, sems = refs[6 + len(messages) :]
    chosen = [u for group in groups for u in GROUPS[group]]
    first, last = min(chosen), max(chosen) + TAPS
    rows_per_slot = 32 * len(chosen)
    slot_stride = rows_per_slot + 8

    loads = []
    for i in (2, 0, 1, 3, 4, 5):
        source = sources[i]
        if i < 2:
            source = source.at[:, first * CHANNELS : last * CHANNELS]
        loads.append(pltpu.make_async_copy(source, (vre, vim, taps, cos_t, sin_t, mat)[i], sems.at[i]))
        loads[-1].start()
    loads[0].wait()

    for c, volts in ((0, vre), (1, vim)):
        loads[1 + c].wait()

        def fir(n1, _, c=c, volts=volts):
            rows = [taps[k : k + 1, pl.ds(pl.multiple_of(n1 * INNER, INNER), INNER)] for k in range(TAPS)]
            needed = sorted({u + k for u in chosen for k in range(TAPS)})
            window = {
                b: volts[
                    :, pl.ds(pl.multiple_of((b - first) * CHANNELS + n1 * INNER, INNER), INNER)
                ].astype(jnp.float32)
                for b in needed
            }
            for i, u in enumerate(chosen):
                total = window[u] * rows[0]
                for k in range(1, TAPS):
                    total = total + window[u + k] * rows[k]
                frames[c, i, n1] = total
            return 0

        lax.fori_loop(0, OUTER, fir, 0, unroll=2)

    for load in loads[3:]:
        load.wait()

    def outer(i, _):
        u = i // 2
        low = pl.multiple_of((i % 2) * 8, 8)
        points = [
            (frames[0, u, n1, pl.ds(low, 8), :], frames[1, u, n1, pl.ds(low, 8), :]) for n1 in range(OUTER)
        ]
        points = small_fft(points)
        for f1 in range(OUTER):
            re, im = points[f1]
            if f1:
                c, d = cos_t[f1 : f1 + 1, :], sin_t[f1 : f1 + 1, :]
                re, im = re * c + im * d, im * c - re * d
            at = low * slot_stride + u * 32 + f1
            turned[0, pl.ds(at, 8, stride=slot_stride), :] = re
            turned[1, pl.ds(at, 8, stride=slot_stride), :] = im
        return 0

    lax.fori_loop(0, 2 * len(chosen), outer, 0, unroll=2)

    matrix = mat[...]
    lane = lax.broadcasted_iota(jnp.int32, (32, INNER), 1)

    def inner(a, _):
        base = pl.multiple_of(a * slot_stride, 8)
        rows = jnp.concatenate(
            [turned[0, pl.ds(base, rows_per_slot), :], turned[1, pl.ds(base, rows_per_slot), :]], axis=1
        ).astype(jnp.bfloat16)
        spec = lax.dot_general(
            matrix, rows, (((1,), (1,)), ((), ())), preferred_element_type=jnp.float32
        )
        for g in range(count):
            for y in range(2):
                for c in range(2):
                    to = [pl.ds((y * 2 + s) * 32 * ROW_STRIDE + a, 32, stride=ROW_STRIDE) for s in range(2)]
                    at = [c * 128 + (y * 2 + pair) * 32 for pair in range(2)]
                    mixed = [spec[f2 : f2 + 32, g * INNER : (g + 1) * INNER] for f2 in at]
                    packed[g * 2 + c, to[0], :] = jnp.where(lane < 64, mixed[0], pltpu.roll(mixed[1], 64, 1))
                    packed[g * 2 + c, to[1], :] = jnp.where(lane < 64, pltpu.roll(mixed[0], 64, 1), mixed[1])
        return 0

    lax.fori_loop(0, SLOTS, inner, 0, unroll=8)

    stores = []
    tile = 0
    for message, to in zip(messages, outs):
        for quarter in range(4):

            def emit(p, _, tile=tile, wide=2 * len(message)):
                for i in range(tile, tile + wide):
                    ready[p, :, i * INNER : (i + 1) * INNER] = packed[
                        i, pl.ds(pl.multiple_of(p * ROW_STRIDE, 8), SLOTS), :
                    ].astype(jnp.bfloat16)
                return 0

            lax.fori_loop(quarter * 32, quarter * 32 + 32, emit, 0, unroll=4)
            part = pl.ds(quarter * 32, 32)
            lanes = slice(tile * INNER, (tile + 2 * len(message)) * INNER)
            stores.append(
                pltpu.make_async_copy(ready.at[part, :, lanes], to.at[part], sems.at[6 + len(stores)])
            )
            stores[-1].start()
        tile += 2 * len(message)
    for store in stores:
        store.wait()


def spectra_of(messages, vre, vim, taps, interpret=False):
    cos_t, sin_t = twist_tables()
    mat = inner_matrix().astype(jnp.bfloat16)
    groups = [group for message in messages for group in message]
    count = len(groups)
    many = 4 * count
    chosen = [u for group in groups for u in GROUPS[group]]
    samples = (max(chosen) + TAPS - min(chosen)) * CHANNELS
    return pl.pallas_call(
        functools.partial(spectra_kernel, messages),
        out_shape=[jax.ShapeDtypeStruct((DEVICES, SLOTS, 2 * INNER * len(m)), jnp.bfloat16) for m in messages],
        in_specs=[pl.BlockSpec(memory_space=pltpu.HBM)] * 6,
        out_specs=[pl.BlockSpec(memory_space=pltpu.HBM)] * len(messages),
        scratch_shapes=[
            pltpu.VMEM((SLOTS, samples), jnp.bfloat16),
            pltpu.VMEM((SLOTS, samples), jnp.bfloat16),
            pltpu.VMEM((TAPS, CHANNELS), jnp.float32),
            pltpu.VMEM((OUTER, INNER), jnp.float32),
            pltpu.VMEM((OUTER, INNER), jnp.float32),
            pltpu.VMEM((256, 256), jnp.bfloat16),
            pltpu.VMEM((2, many, OUTER, SLOTS, INNER), jnp.float32),
            pltpu.VMEM((2, SLOTS * (32 * many + 8), INNER), jnp.float32),
            pltpu.VMEM((2 * count, DEVICES * ROW_STRIDE, INNER), jnp.float32),
            pltpu.VMEM((DEVICES, SLOTS, 2 * count * INNER), jnp.bfloat16),
            pltpu.SemaphoreType.DMA((6 + 4 * len(messages),)),
        ],
        compiler_params=pltpu.CompilerParams(vmem_limit_bytes=58 * MIB),
        cost_estimate=pl.CostEstimate(
            flops=8 * 10**8 * count, bytes_accessed=16 * 10**6 * count, transcendentals=0
        ),
        interpret=interpret,
        name="spectra",
    )(vre, vim, taps, jnp.asarray(cos_t), jnp.asarray(sin_t), jnp.asarray(mat))


def quarter_kernel(wre, wim, slots, out, buf, names, chosen, ready, sems):
    grp = lax.axis_index("grp")
    y_lo, core = grp // 2, grp % 2
    antennas, beams = wre.shape
    half = antennas // 2
    name_copy = pltpu.make_async_copy(slots.at[core], names, sems.at[4])
    name_copy.start()
    for y, source in ((0, wre), (1, wim)):

        @pl.when(y_lo == y)
        def _():
            for i in range(4):
                part = pl.ds(i * half // 2, half // 2)
                pltpu.make_async_copy(source.at[part], buf.at[part], sems.at[i]).start()
    name_copy.wait()
    row = names[...]

    def build(i, _):
        antenna = lax.broadcasted_iota(jnp.int32, (16, half), 0) + i * 16
        chosen[pl.ds(pl.multiple_of(i * 16, 16), 16), :] = jnp.where(antenna == row, 1.0, 0.0).astype(jnp.bfloat16)
        return 0
    lax.fori_loop(0, antennas // 16, build, 0, unroll=8)
    for y, source in ((0, wre), (1, wim)):

        @pl.when(y_lo == y)
        def _():
            for i in range(4):
                part = pl.ds(i * half // 2, half // 2)
                pltpu.make_async_copy(source.at[part], buf.at[part], sems.at[i]).wait()
    stores = []
    for j in range(0, beams, 256):
        w = buf[:, j : j + 256].astype(jnp.bfloat16)
        for k in range(0, half, 512):
            ready[j : j + 256, k : k + 512] = lax.dot_general(
                w, chosen[:, k : k + 512], (((0,), (0,)), ((), ())), preferred_element_type=jnp.float32
            ).astype(jnp.bfloat16)
        part = pl.ds(j, 256)
        stores.append(pltpu.make_async_copy(ready.at[part], out.at[part], sems.at[5 + len(stores)]))
        stores[-1].start()
    for store in stores:
        store.wait()


def quarter_of(wre, wim, antenna_map, interpret=False):
    antennas, beams = wre.shape
    half = antennas // 2
    return pl.pallas_call(
        quarter_kernel,
        in_specs=[pl.BlockSpec(memory_space=pltpu.HBM)] * 3,
        out_specs=pl.BlockSpec(memory_space=pltpu.HBM),
        out_shape=jax.ShapeDtypeStruct((beams, half), jnp.bfloat16),
        scratch_shapes=[
            pltpu.VMEM((antennas, beams), jnp.float32),
            pltpu.VMEM((1, half), jnp.int32),
            pltpu.VMEM((antennas, half), jnp.bfloat16),
            pltpu.VMEM((beams, half), jnp.bfloat16),
            pltpu.SemaphoreType.DMA((7,)),
        ],
        compiler_params=pltpu.CompilerParams(vmem_limit_bytes=58 * MIB),
        cost_estimate=pl.CostEstimate(flops=2 * 10**9, bytes_accessed=6 * 10**6, transcendentals=0),
        interpret=interpret,
        name="quarter",
    )(wre, wim, antenna_map.reshape(2, 1, half))


def pick_kernel(owners, offers, mine, other):
    core = lax.axis_index("grp") % 2
    mine[...] = offers[owners[core]]
    other[...] = offers[owners[1 - core]]


def pick_of(owners, offers, interpret=False):
    _, rows, columns = offers.shape
    return pl.pallas_call(
        pick_kernel,
        in_specs=[pl.BlockSpec(memory_space=pltpu.SMEM), pl.BlockSpec(memory_space=pltpu.VMEM)],
        out_specs=[pl.BlockSpec(memory_space=pltpu.VMEM)] * 2,
        out_shape=[jax.ShapeDtypeStruct((rows, columns), offers.dtype)] * 2,
        compiler_params=pltpu.CompilerParams(vmem_limit_bytes=8 * MIB),
        interpret=interpret,
        name="pick",
    )(owners, offers)


def join_kernel(axis, *refs):
    parts, out = refs[:-1], refs[-1]
    at = 0
    for part in parts:
        size = part.shape[axis]
        if axis == 0:
            out[at : at + size, :] = part[...]
        else:
            out[:, at : at + size] = part[...]
        at += size


def join_of(parts, axis, interpret=False):
    shape = list(parts[0].shape)
    shape[axis] = sum(p.shape[axis] for p in parts)
    return pl.pallas_call(
        functools.partial(join_kernel, axis),
        out_shape=jax.ShapeDtypeStruct(tuple(shape), parts[0].dtype),
        in_specs=[pl.BlockSpec(memory_space=pltpu.VMEM)] * len(parts),
        out_specs=pl.BlockSpec(memory_space=pltpu.VMEM),
        compiler_params=pltpu.CompilerParams(vmem_limit_bytes=8 * MIB),
        interpret=interpret,
        name="join",
    )(*parts)


def choose_matrix():
    chosen = np.zeros((2, 32, 3, 2, 2, 32), np.float32)
    for pair in range(2):
        for f1 in range(32):
            chosen[pair, f1, :, pair, :, f1] = 1.0
    return chosen.reshape(64, 384)


def products(core, part, spectra):
    half = part.shape[1] // 2
    near = pl.ds(pl.multiple_of(core * half, half), half)
    far = pl.ds(pl.multiple_of((1 - core) * half, half), half)
    left, right = part[:, :half], part[:, half:]
    return jnp.dot(left, spectra[near, :], preferred_element_type=jnp.float32) + jnp.dot(
        right, spectra[far, :], preferred_element_type=jnp.float32
    )


def early_kernel(w0, w1, w2, za, out):
    core = lax.axis_index("grp") % 2
    n = w0.shape[0]
    for i, part in enumerate((w0, w1, w2)):
        out[i * n : (i + 1) * n, :] = products(core, part, za)


def early_of(w0, w1, w2, spectra, interpret=False):
    return pl.pallas_call(
        early_kernel,
        out_shape=jax.ShapeDtypeStruct((3 * w0.shape[0], 768), jnp.float32),
        in_specs=[pl.BlockSpec(memory_space=pltpu.VMEM)] * 4,
        out_specs=pl.BlockSpec(memory_space=pltpu.VMEM),
        compiler_params=pltpu.CompilerParams(vmem_limit_bytes=24 * MIB),
        cost_estimate=pl.CostEstimate(flops=17 * 10**8, bytes_accessed=8 * 10**6, transcendentals=0),
        interpret=interpret,
        name="early",
    )(w0, w1, w2, spectra)


def beams_kernel(places, early, w3, za, choose, own, given, sums):
    for k in range(48):
        at = pl.multiple_of(places[k], 16)
        sums[pl.ds(at, 16), :] = early[k * 16 : (k + 1) * 16, :]
    core = lax.axis_index("grp") % 2
    result = products(core, w3, za)
    for k in range(16):
        at = pl.multiple_of(places[48 + k], 16)
        sums[pl.ds(at, 16), :] = result[k * 16 : (k + 1) * 16, :]
    beams = sums.shape[0] // 2
    powers = []
    for g in range(3):
        re_lanes, im_lanes = slice(g * 256, g * 256 + 128), slice(g * 256 + 128, g * 256 + 256)
        re = sums[:beams, re_lanes] - sums[beams:, im_lanes]
        im = sums[beams:, re_lanes] + sums[:beams, im_lanes]
        powers.append(re * re + im * im)
    total = lax.dot_general(
        choose[...],
        jnp.concatenate(powers, axis=1),
        (((1,), (1,)), ((), ())),
        preferred_element_type=jnp.float32,
        precision=lax.Precision.HIGHEST,
    )
    total = total * (1.0 / SPECTRA)
    own[...] = jnp.where(core == 0, total[:32], total[32:])
    given[...] = jnp.where(core == 0, total[32:], total[:32])


def beams_of(places, early, w3, spectra, interpret=False):
    rows = early.shape[0] + w3.shape[0]
    return pl.pallas_call(
        beams_kernel,
        out_shape=[jax.ShapeDtypeStruct((32, rows // 2), jnp.float32)] * 2,
        in_specs=[pl.BlockSpec(memory_space=pltpu.SMEM)] + [pl.BlockSpec(memory_space=pltpu.VMEM)] * 4,
        out_specs=[pl.BlockSpec(memory_space=pltpu.VMEM)] * 2,
        scratch_shapes=[pltpu.VMEM((rows, 768), jnp.float32)],
        compiler_params=pltpu.CompilerParams(vmem_limit_bytes=32 * MIB),
        cost_estimate=pl.CostEstimate(flops=17 * 10**8, bytes_accessed=8 * 10**6, transcendentals=0),
        interpret=interpret,
        name="beams",
    )(places, early, w3, spectra, jnp.asarray(choose_matrix()))


def index_of(z, x, y, core):
    return ((y % 2) * 2 + core) * 32 + (z % 4) * 8 + (x % 4) * 2 + (y % 4) // 2


EVERY = [(z, x, y, c) for z in range(4) for x in range(4) for y in range(4) for c in range(2)]
ORDER = (("y", "x", "z"), ("z", "y", "x"))
SHIFTS = (0, -1, 1, 2)


def permutation(stage, shift):
    pairs = []
    for z, x, y, core in EVERY:
        axis = ORDER[core][stage]
        source = {"z": z, "x": x, "y": y}
        source[axis] += shift
        pairs.append((index_of(source["z"], source["x"], source["y"], core), index_of(z, x, y, core)))
    return pairs


def gather_stage(block, stage):
    return [block] + [lax.ppermute(block, ALL, permutation(stage, shift)) for shift in SHIFTS[1:]]


def block_places(grp, dev):
    core = grp % 2
    z, x, y = dev // 8, dev // 2 % 4, dev % 2 * 2 + grp // 2
    k = np.arange(64)
    shift = np.array(SHIFTS)
    first, second, third = shift[k % 4], shift[k // 4 % 4], shift[k // 16]
    by_core = []
    for order in ORDER:
        moved = dict(zip(order, (first, second, third)))
        by_core.append([moved[axis] for axis in "zxy"])
    is_first = core == 0
    mz, mx, my = [jnp.where(is_first, jnp.asarray(a), jnp.asarray(b)) for a, b in zip(*by_core)]
    fz, fx, fy = (z + mz + 4) % 4, (x + mx + 4) % 4, (y + my + 4) % 4
    return (((fy % 2) * 32 + fz * 8 + fx * 2 + fy // 2) * 16).astype(jnp.int32)


SWAP = [(0, 1), (1, 0), (2, 3), (3, 2)]


def on_device(voltage_real, voltage_imaginary, filter_taps, weights_re, weights_im, owners, antenna_map):
    grp, dev = lax.axis_index("grp"), lax.axis_index("dev")
    core = grp % 2

    quarter = quarter_of(weights_re[0], weights_im[0], antenna_map)
    offers = lax.all_to_all(quarter.reshape(32, 16, -1), "dev", split_axis=0, concat_axis=0, tiled=True)

    volts = (voltage_real, voltage_imaginary, filter_taps)
    quarter, *volts = lax.optimization_barrier((quarter, *volts))
    (message,) = spectra_of(MESSAGES, *volts)
    message, offers = lax.optimization_barrier((message, offers))
    mine, other = pick_of(owners, offers)
    message, mine, other = lax.optimization_barrier((message, mine, other))
    spectra = lax.all_to_all(message, ALL, split_axis=0, concat_axis=0, tiled=True)
    spectra = spectra.reshape(DEVICES * SLOTS, -1)

    other = lax.ppermute(other, "grp", SWAP)
    block = join_of([mine, other], 1)
    block = join_of(gather_stage(block, 0), 0)
    block = join_of(gather_stage(block, 1), 0)
    parts = gather_stage(block, 2)

    early = early_of(*parts[:3], spectra)
    places = block_places(grp, dev)
    own, given = beams_of(places, early, parts[3], spectra)
    taken = lax.ppermute(given, "grp", SWAP)
    return jnp.where(core == 0, jnp.stack([own, taken]), jnp.stack([taken, own]))


def solution(mesh):
    return jax.shard_map(
        on_device,
        mesh=mesh,
        in_specs=(
            P(("grp", "dev"), None),
            P(("grp", "dev"), None),
            P(),
            P("dev", None, None),
            P("dev", None, None),
            P(),
            P(),
        ),
        out_specs=P(None, ("grp", "dev"), None),
        check_vma=False,
    )
```

```python
import functools
import math

import jax
import jax.numpy as jnp
import numpy as np
from jax import lax
from jax.experimental import pallas as pl
from jax.experimental.pallas import tpu as pltpu
from jax.sharding import PartitionSpec as P

CHANNELS = 4096
TAPS = 16
SPECTRA = 6
STEPS = 2
FRAMES = STEPS * SPECTRA
BLOCKS = FRAMES + TAPS - 1
OUTER = 32
INNER = 128
SLOTS = 16
DEVICES = 128
ROW_STRIDE = 24
GROUPS = ((0, 1, 6, 7), (2, 3, 8, 9), (4, 5, 10, 11))
MESSAGES = ((0, 1, 2),)
ALL = ("grp", "dev")
MIB = 1 << 20


def twist_tables():
    products = np.outer(np.arange(OUTER), np.arange(INNER)) % CHANNELS
    angles = products * (2.0 * math.pi / CHANNELS)
    return np.cos(angles).astype(np.float32), np.sin(angles).astype(np.float32)


def inner_matrix():
    products = np.outer(np.arange(INNER), np.arange(INNER)) % INNER
    angles = products * (2.0 * math.pi / INNER)
    norm = CHANNELS ** (-0.5)
    c, s = np.cos(angles) * norm, np.sin(angles) * norm
    return np.block([[c, s], [-s, c]]).astype(np.float32)


def small_fft(points):
    count = len(points)
    if count == 1:
        return points
    even = small_fft(points[0::2])
    odd = small_fft(points[1::2])
    half = count // 2
    result = [None] * count
    for k in range(half):
        er, ei = even[k]
        xr, xi = odd[k]
        if k == 0:
            tr, ti = xr, xi
        elif 4 * k == count:
            tr, ti = xi, -xr
        elif 8 * k == count:
            r = math.sqrt(0.5)
            tr, ti = (xr + xi) * r, (xi - xr) * r
        elif 8 * k == 3 * count:
            r = math.sqrt(0.5)
            tr, ti = (xi - xr) * r, (xr + xi) * (-r)
        else:
            c = math.cos(2.0 * math.pi * k / count)
            s = math.sin(2.0 * math.pi * k / count)
            tr, ti = xr * c + xi * s, xi * c - xr * s
        result[k] = (er + tr, ei + ti)
        result[k + half] = (er - tr, ei - ti)
    return result


def spectra_kernel(messages, *refs):
    groups = [group for message in messages for group in message]
    count = len(groups)
    sources, outs = refs[:6], refs[6 : 6 + len(messages)]
    vre, vim, taps, cos_t, sin_t, mat, frames, turned, packed, ready, sems = refs[6 + len(messages) :]
    chosen = [u for group in groups for u in GROUPS[group]]
    first, last = min(chosen), max(chosen) + TAPS
    rows_per_slot = 32 * len(chosen)
    slot_stride = rows_per_slot + 8

    loads = []
    for i in (2, 0, 1, 3, 4, 5):
        source = sources[i]
        if i < 2:
            source = source.at[:, first * CHANNELS : last * CHANNELS]
        loads.append(pltpu.make_async_copy(source, (vre, vim, taps, cos_t, sin_t, mat)[i], sems.at[i]))
        loads[-1].start()
    loads[0].wait()

    for c, volts in ((0, vre), (1, vim)):
        loads[1 + c].wait()

        def fir(n1, _, c=c, volts=volts):
            rows = [taps[k : k + 1, pl.ds(pl.multiple_of(n1 * INNER, INNER), INNER)] for k in range(TAPS)]
            needed = sorted({u + k for u in chosen for k in range(TAPS)})
            window = {
                b: volts[
                    :, pl.ds(pl.multiple_of((b - first) * CHANNELS + n1 * INNER, INNER), INNER)
                ].astype(jnp.float32)
                for b in needed
            }
            for i, u in enumerate(chosen):
                total = window[u] * rows[0]
                for k in range(1, TAPS):
                    total = total + window[u + k] * rows[k]
                frames[c, i, n1] = total
            return 0

        lax.fori_loop(0, OUTER, fir, 0, unroll=2)

    for load in loads[3:]:
        load.wait()

    def outer(i, _):
        u = i // 2
        low = pl.multiple_of((i % 2) * 8, 8)
        points = [
            (frames[0, u, n1, pl.ds(low, 8), :], frames[1, u, n1, pl.ds(low, 8), :]) for n1 in range(OUTER)
        ]
        points = small_fft(points)
        for f1 in range(OUTER):
            re, im = points[f1]
            if f1:
                c, d = cos_t[f1 : f1 + 1, :], sin_t[f1 : f1 + 1, :]
                re, im = re * c + im * d, im * c - re * d
            at = low * slot_stride + u * 32 + f1
            turned[0, pl.ds(at, 8, stride=slot_stride), :] = re
            turned[1, pl.ds(at, 8, stride=slot_stride), :] = im
        return 0

    lax.fori_loop(0, 2 * len(chosen), outer, 0, unroll=2)

    matrix = mat[...]
    lane = lax.broadcasted_iota(jnp.int32, (32, INNER), 1)

    def inner(a, _):
        base = pl.multiple_of(a * slot_stride, 8)
        rows = jnp.concatenate(
            [turned[0, pl.ds(base, rows_per_slot), :], turned[1, pl.ds(base, rows_per_slot), :]], axis=1
        ).astype(jnp.bfloat16)
        spec = lax.dot_general(
            matrix, rows, (((1,), (1,)), ((), ())), preferred_element_type=jnp.float32
        )
        for g in range(count):
            for y in range(2):
                for c in range(2):
                    to = [pl.ds((y * 2 + s) * 32 * ROW_STRIDE + a, 32, stride=ROW_STRIDE) for s in range(2)]
                    at = [c * 128 + (y * 2 + pair) * 32 for pair in range(2)]
                    mixed = [spec[f2 : f2 + 32, g * INNER : (g + 1) * INNER] for f2 in at]
                    packed[g * 2 + c, to[0], :] = jnp.where(lane < 64, mixed[0], pltpu.roll(mixed[1], 64, 1))
                    packed[g * 2 + c, to[1], :] = jnp.where(lane < 64, pltpu.roll(mixed[0], 64, 1), mixed[1])
        return 0

    lax.fori_loop(0, SLOTS, inner, 0, unroll=8)

    stores = []
    tile = 0
    for message, to in zip(messages, outs):
        for quarter in range(4):

            def emit(p, _, tile=tile, wide=2 * len(message)):
                for i in range(tile, tile + wide):
                    ready[p, :, i * INNER : (i + 1) * INNER] = packed[
                        i, pl.ds(pl.multiple_of(p * ROW_STRIDE, 8), SLOTS), :
                    ].astype(jnp.bfloat16)
                return 0

            lax.fori_loop(quarter * 32, quarter * 32 + 32, emit, 0, unroll=4)
            part = pl.ds(quarter * 32, 32)
            lanes = slice(tile * INNER, (tile + 2 * len(message)) * INNER)
            stores.append(
                pltpu.make_async_copy(ready.at[part, :, lanes], to.at[part], sems.at[6 + len(stores)])
            )
            stores[-1].start()
        tile += 2 * len(message)
    for store in stores:
        store.wait()


def spectra_of(messages, vre, vim, taps, interpret=False):
    cos_t, sin_t = twist_tables()
    mat = inner_matrix().astype(jnp.bfloat16)
    groups = [group for message in messages for group in message]
    count = len(groups)
    many = 4 * count
    chosen = [u for group in groups for u in GROUPS[group]]
    samples = (max(chosen) + TAPS - min(chosen)) * CHANNELS
    return pl.pallas_call(
        functools.partial(spectra_kernel, messages),
        out_shape=[jax.ShapeDtypeStruct((DEVICES, SLOTS, 2 * INNER * len(m)), jnp.bfloat16) for m in messages],
        in_specs=[pl.BlockSpec(memory_space=pltpu.HBM)] * 6,
        out_specs=[pl.BlockSpec(memory_space=pltpu.HBM)] * len(messages),
        scratch_shapes=[
            pltpu.VMEM((SLOTS, samples), jnp.bfloat16),
            pltpu.VMEM((SLOTS, samples), jnp.bfloat16),
            pltpu.VMEM((TAPS, CHANNELS), jnp.float32),
            pltpu.VMEM((OUTER, INNER), jnp.float32),
            pltpu.VMEM((OUTER, INNER), jnp.float32),
            pltpu.VMEM((256, 256), jnp.bfloat16),
            pltpu.VMEM((2, many, OUTER, SLOTS, INNER), jnp.float32),
            pltpu.VMEM((2, SLOTS * (32 * many + 8), INNER), jnp.float32),
            pltpu.VMEM((2 * count, DEVICES * ROW_STRIDE, INNER), jnp.float32),
            pltpu.VMEM((DEVICES, SLOTS, 2 * count * INNER), jnp.bfloat16),
            pltpu.SemaphoreType.DMA((6 + 4 * len(messages),)),
        ],
        compiler_params=pltpu.CompilerParams(vmem_limit_bytes=58 * MIB),
        cost_estimate=pl.CostEstimate(
            flops=8 * 10**8 * count, bytes_accessed=16 * 10**6 * count, transcendentals=0
        ),
        interpret=interpret,
        name="spectra",
    )(vre, vim, taps, jnp.asarray(cos_t), jnp.asarray(sin_t), jnp.asarray(mat))


def quarter_kernel(wre, wim, slots, out, buf, names, chosen, ready, sems):
    grp = lax.axis_index("grp")
    y_lo, core = grp // 2, grp % 2
    antennas, beams = wre.shape
    half = antennas // 2
    name_copy = pltpu.make_async_copy(slots.at[core], names, sems.at[4])
    name_copy.start()
    for y, source in ((0, wre), (1, wim)):

        @pl.when(y_lo == y)
        def _():
            for i in range(4):
                part = pl.ds(i * half // 2, half // 2)
                pltpu.make_async_copy(source.at[part], buf.at[part], sems.at[i]).start()
    name_copy.wait()
    row = names[...]

    def build(i, _):
        antenna = lax.broadcasted_iota(jnp.int32, (16, half), 0) + i * 16
        chosen[pl.ds(pl.multiple_of(i * 16, 16), 16), :] = jnp.where(antenna == row, 1.0, 0.0).astype(jnp.bfloat16)
        return 0
    lax.fori_loop(0, antennas // 16, build, 0, unroll=8)
    for y, source in ((0, wre), (1, wim)):

        @pl.when(y_lo == y)
        def _():
            for i in range(4):
                part = pl.ds(i * half // 2, half // 2)
                pltpu.make_async_copy(source.at[part], buf.at[part], sems.at[i]).wait()
    stores = []
    for j in range(0, beams, 256):
        w = buf[:, j : j + 256].astype(jnp.bfloat16)
        for k in range(0, half, 512):
            ready[j : j + 256, k : k + 512] = lax.dot_general(
                w, chosen[:, k : k + 512], (((0,), (0,)), ((), ())), preferred_element_type=jnp.float32
            ).astype(jnp.bfloat16)
        part = pl.ds(j, 256)
        stores.append(pltpu.make_async_copy(ready.at[part], out.at[part], sems.at[5 + len(stores)]))
        stores[-1].start()
    for store in stores:
        store.wait()


def quarter_of(wre, wim, antenna_map, interpret=False):
    antennas, beams = wre.shape
    half = antennas // 2
    return pl.pallas_call(
        quarter_kernel,
        in_specs=[pl.BlockSpec(memory_space=pltpu.HBM)] * 3,
        out_specs=pl.BlockSpec(memory_space=pltpu.HBM),
        out_shape=jax.ShapeDtypeStruct((beams, half), jnp.bfloat16),
        scratch_shapes=[
            pltpu.VMEM((antennas, beams), jnp.float32),
            pltpu.VMEM((1, half), jnp.int32),
            pltpu.VMEM((antennas, half), jnp.bfloat16),
            pltpu.VMEM((beams, half), jnp.bfloat16),
            pltpu.SemaphoreType.DMA((7,)),
        ],
        compiler_params=pltpu.CompilerParams(vmem_limit_bytes=58 * MIB),
        cost_estimate=pl.CostEstimate(flops=2 * 10**9, bytes_accessed=6 * 10**6, transcendentals=0),
        interpret=interpret,
        name="quarter",
    )(wre, wim, antenna_map.reshape(2, 1, half))


def pick_kernel(owners, offers, mine, other):
    core = lax.axis_index("grp") % 2
    mine[...] = offers[owners[core]]
    other[...] = offers[owners[1 - core]]


def pick_of(owners, offers, interpret=False):
    _, rows, columns = offers.shape
    return pl.pallas_call(
        pick_kernel,
        in_specs=[pl.BlockSpec(memory_space=pltpu.SMEM), pl.BlockSpec(memory_space=pltpu.VMEM)],
        out_specs=[pl.BlockSpec(memory_space=pltpu.VMEM)] * 2,
        out_shape=[jax.ShapeDtypeStruct((rows, columns), offers.dtype)] * 2,
        compiler_params=pltpu.CompilerParams(vmem_limit_bytes=8 * MIB),
        interpret=interpret,
        name="pick",
    )(owners, offers)


def join_kernel(axis, *refs):
    parts, out = refs[:-1], refs[-1]
    at = 0
    for part in parts:
        size = part.shape[axis]
        if axis == 0:
            out[at : at + size, :] = part[...]
        else:
            out[:, at : at + size] = part[...]
        at += size


def join_of(parts, axis, interpret=False):
    shape = list(parts[0].shape)
    shape[axis] = sum(p.shape[axis] for p in parts)
    return pl.pallas_call(
        functools.partial(join_kernel, axis),
        out_shape=jax.ShapeDtypeStruct(tuple(shape), parts[0].dtype),
        in_specs=[pl.BlockSpec(memory_space=pltpu.VMEM)] * len(parts),
        out_specs=pl.BlockSpec(memory_space=pltpu.VMEM),
        compiler_params=pltpu.CompilerParams(vmem_limit_bytes=8 * MIB),
        interpret=interpret,
        name="join",
    )(*parts)


def choose_matrix():
    chosen = np.zeros((2, 32, 3, 2, 2, 32), np.float32)
    for pair in range(2):
        for f1 in range(32):
            chosen[pair, f1, :, pair, :, f1] = 1.0
    return chosen.reshape(64, 384)


def products(core, part, spectra):
    half = part.shape[1] // 2
    near = pl.ds(pl.multiple_of(core * half, half), half)
    far = pl.ds(pl.multiple_of((1 - core) * half, half), half)
    left, right = part[:, :half], part[:, half:]
    return jnp.dot(left, spectra[near, :], preferred_element_type=jnp.float32) + jnp.dot(
        right, spectra[far, :], preferred_element_type=jnp.float32
    )


def early_kernel(w0, w1, za, out):
    core = lax.axis_index("grp") % 2
    n = w0.shape[0]
    for i, part in enumerate((w0, w1)):
        out[i * n : (i + 1) * n, :] = products(core, part, za)


def early_of(w0, w1, spectra, interpret=False):
    return pl.pallas_call(
        early_kernel,
        out_shape=jax.ShapeDtypeStruct((2 * w0.shape[0], 768), jnp.float32),
        in_specs=[pl.BlockSpec(memory_space=pltpu.VMEM)] * 3,
        out_specs=pl.BlockSpec(memory_space=pltpu.VMEM),
        compiler_params=pltpu.CompilerParams(vmem_limit_bytes=24 * MIB),
        cost_estimate=pl.CostEstimate(flops=17 * 10**8, bytes_accessed=8 * 10**6, transcendentals=0),
        interpret=interpret,
        name="early",
    )(w0, w1, spectra)


def beams_kernel(places, early, w2, w3, za, choose, own, given, sums):
    for k in range(32):
        at = pl.multiple_of(places[k], 16)
        sums[pl.ds(at, 16), :] = early[k * 16 : (k + 1) * 16, :]
    core = lax.axis_index("grp") % 2
    for i, part in enumerate((w2, w3)):
        result = products(core, part, za)
        for k in range(16):
            at = pl.multiple_of(places[(i + 2) * 16 + k], 16)
            sums[pl.ds(at, 16), :] = result[k * 16 : (k + 1) * 16, :]
    beams = sums.shape[0] // 2
    powers = []
    for g in range(3):
        re_lanes, im_lanes = slice(g * 256, g * 256 + 128), slice(g * 256 + 128, g * 256 + 256)
        re = sums[:beams, re_lanes] - sums[beams:, im_lanes]
        im = sums[beams:, re_lanes] + sums[:beams, im_lanes]
        powers.append(re * re + im * im)
    total = lax.dot_general(
        choose[...],
        jnp.concatenate(powers, axis=1),
        (((1,), (1,)), ((), ())),
        preferred_element_type=jnp.float32,
        precision=lax.Precision.HIGHEST,
    )
    total = total * (1.0 / SPECTRA)
    own[...] = jnp.where(core == 0, total[:32], total[32:])
    given[...] = jnp.where(core == 0, total[32:], total[:32])


def beams_of(places, early, w2, w3, spectra, interpret=False):
    rows = early.shape[0] + 2 * w2.shape[0]
    return pl.pallas_call(
        beams_kernel,
        out_shape=[jax.ShapeDtypeStruct((32, rows // 2), jnp.float32)] * 2,
        in_specs=[pl.BlockSpec(memory_space=pltpu.SMEM)] + [pl.BlockSpec(memory_space=pltpu.VMEM)] * 5,
        out_specs=[pl.BlockSpec(memory_space=pltpu.VMEM)] * 2,
        scratch_shapes=[pltpu.VMEM((rows, 768), jnp.float32)],
        compiler_params=pltpu.CompilerParams(vmem_limit_bytes=32 * MIB),
        cost_estimate=pl.CostEstimate(flops=17 * 10**8, bytes_accessed=8 * 10**6, transcendentals=0),
        interpret=interpret,
        name="beams",
    )(places, early, w2, w3, spectra, jnp.asarray(choose_matrix()))


def index_of(z, x, y, core):
    return ((y % 2) * 2 + core) * 32 + (z % 4) * 8 + (x % 4) * 2 + (y % 4) // 2


EVERY = [(z, x, y, c) for z in range(4) for x in range(4) for y in range(4) for c in range(2)]
ORDER = (("y", "x", "z"), ("z", "y", "x"))
SHIFTS = (0, -1, 1, 2)


def permutation(stage, shift):
    pairs = []
    for z, x, y, core in EVERY:
        axis = ORDER[core][stage]
        source = {"z": z, "x": x, "y": y}
        source[axis] += shift
        pairs.append((index_of(source["z"], source["x"], source["y"], core), index_of(z, x, y, core)))
    return pairs


def gather_stage(block, stage):
    return [block] + [lax.ppermute(block, ALL, permutation(stage, shift)) for shift in SHIFTS[1:]]


def block_places(grp, dev):
    core = grp % 2
    z, x, y = dev // 8, dev // 2 % 4, dev % 2 * 2 + grp // 2
    k = np.arange(64)
    shift = np.array(SHIFTS)
    first, second, third = shift[k % 4], shift[k // 4 % 4], shift[k // 16]
    by_core = []
    for order in ORDER:
        moved = dict(zip(order, (first, second, third)))
        by_core.append([moved[axis] for axis in "zxy"])
    is_first = core == 0
    mz, mx, my = [jnp.where(is_first, jnp.asarray(a), jnp.asarray(b)) for a, b in zip(*by_core)]
    fz, fx, fy = (z + mz + 4) % 4, (x + mx + 4) % 4, (y + my + 4) % 4
    return (((fy % 2) * 32 + fz * 8 + fx * 2 + fy // 2) * 16).astype(jnp.int32)


SWAP = [(0, 1), (1, 0), (2, 3), (3, 2)]


def on_device(voltage_real, voltage_imaginary, filter_taps, weights_re, weights_im, owners, antenna_map):
    grp, dev = lax.axis_index("grp"), lax.axis_index("dev")
    core = grp % 2

    quarter = quarter_of(weights_re[0], weights_im[0], antenna_map)
    offers = lax.all_to_all(quarter.reshape(32, 16, -1), "dev", split_axis=0, concat_axis=0, tiled=True)

    volts = (voltage_real, voltage_imaginary, filter_taps)
    quarter, *volts = lax.optimization_barrier((quarter, *volts))
    (message,) = spectra_of(MESSAGES, *volts)
    message, offers = lax.optimization_barrier((message, offers))
    mine, other = pick_of(owners, offers)
    message, mine, other = lax.optimization_barrier((message, mine, other))
    spectra = lax.all_to_all(message, ALL, split_axis=0, concat_axis=0, tiled=True)
    spectra = spectra.reshape(DEVICES * SLOTS, -1)

    other = lax.ppermute(other, "grp", SWAP)
    block = join_of([mine, other], 1)
    block = join_of(gather_stage(block, 0), 0)
    block = join_of(gather_stage(block, 1), 0)
    parts = gather_stage(block, 2)

    early = early_of(parts[0], parts[3], spectra)
    places = block_places(grp, dev)
    places = jnp.concatenate([places[:16], places[48:], places[16:48]])
    own, given = beams_of(places, early, parts[1], parts[2], spectra)
    taken = lax.ppermute(given, "grp", SWAP)
    return jnp.where(core == 0, jnp.stack([own, taken]), jnp.stack([taken, own]))


def solution(mesh):
    return jax.shard_map(
        on_device,
        mesh=mesh,
        in_specs=(
            P(("grp", "dev"), None),
            P(("grp", "dev"), None),
            P(),
            P("dev", None, None),
            P("dev", None, None),
            P(),
            P(),
        ),
        out_specs=P(None, ("grp", "dev"), None),
        check_vma=False,
    )
```
